32 devices in a mesh: feat: 4 (over y, core), wide: 8 (over z, x).
Axes of the slice: x: 2, y: 2, z: 4, core: 2. Of those that a mesh axis runs over, the one named last changes fastest.
Arguments:
- inputs: float32 [2048, 768], P('wide'), may hold values from -4 to 4, as said below
- cotangent: float32 [2048, 768], P('wide'), may hold values from -6 to 6
- random_proj: float32 [64, 64], P(None, 'feat'), may hold values from -2.5 to 2.5, as said below
- position_bias: float32 [12, 4096], P(None, 'wide'), may hold values from -3 to 3
- w_qkv: float32 [768, 2304], P('wide'), may hold values from -1 to 1, as said below
- b_qkv: float32 [2304], P('wide'), may hold values from -1 to 1, as said below
- w_out: float32 [768, 768], P('wide'), may hold values from -0.875 to 0.875
- b_out: float32 [768], P('wide'), may hold values from -1 to 1
- ln1_gain: float32 [768], P('wide'), may hold values from 0.5 to 1.5
- ln1_bias: float32 [768], P('wide'), may hold values from -1 to 1
- w_up: float32 [768, 3072], P('wide'), may hold values from -0.21875 to 0.21875
- b_up: float32 [3072], P('wide'), may hold values from -1 to 1
- w_down: float32 [3072, 768], P('wide'), may hold values from -0.109375 to 0.109375
- b_down: float32 [768], P('wide'), may hold values from -1 to 1
- ln2_gain: float32 [768], P('wide'), may hold values from 0.5 to 1.5
- ln2_bias: float32 [768], P('wide'), may hold values from -1 to 1
Outputs:
- output: float32 [2048, 768], P('wide')
- d_inputs: float32 [2048, 768], P('wide')
- d_position_bias: float32 [12, 4096], P(None, 'wide')
- d_w_qkv: float32 [768, 2304], P('wide')
- d_b_qkv: float32 [2304], P('wide')
- d_w_out: float32 [768, 768], P('wide')
- d_b_out: float32 [768], P('wide')
- d_ln1_gain: float32 [768], P('wide')
- d_ln1_bias: float32 [768], P('wide')
- d_w_up: float32 [768, 3072], P('wide')
- d_b_up: float32 [3072], P('wide')
- d_w_down: float32 [3072, 768], P('wide')
- d_b_down: float32 [768], P('wide')
- d_ln2_gain: float32 [768], P('wide')
- d_ln2_bias: float32 [768], P('wide')
The draws below stay inside these ranges and needn't reach their ends.
Inputs may be any that keep to these rules, and one draw needn't show every extreme that they name: `inputs`: independent entries of deviation about one. `random_proj`: independent entries of deviation about one. `w_qkv`: independent entries of deviation about (1536)^(-1/2). `b_qkv`: independent entries of deviation about 0.3.
All inputs are finite; a program needn't handle non-finite values.
Results may differ from the reference program's by a relative error of at most 0.0003.
Values sent between devices are 32-bit elements; how exact they have to be, the bound alone decides.
No kernel may reach another device: no remote copies, remote signals or barrier semaphores. Data moves between devices by JAX's collectives and lax.ppermute only.
A program may use at most 384 MiB of HBM per device.

```python
import jax
import jax.numpy as jnp
from jax import lax

D = 768
HEADS = 12
HEAD_DIM = 64
FF = 3072
FEATURES = 64
LENGTH = 2048


def draw_inputs(key, part):
    key = jax.random.fold_in(key, 11)
    values = jax.random.normal(key, (LENGTH, D), jnp.float32)
    return jnp.clip(values, -4.0, 4.0)


def draw_random_proj(key, part):
    key = jax.random.fold_in(key, 12)
    values = jax.random.normal(key, (HEAD_DIM, FEATURES), jnp.float32)
    return jnp.clip(values, -2.5, 2.5)


def draw_w_qkv(key, part):
    key = jax.random.fold_in(key, 13)
    values = jnp.clip(jax.random.normal(key, (D, 3 * D), jnp.float32), -3.0, 3.0)
    return values * (2.0 * D) ** (-0.5)


def draw_b_qkv(key, part):
    key = jax.random.fold_in(key, 14)
    values = 0.3 * jax.random.normal(key, (3 * D,), jnp.float32)
    return jnp.clip(values, -1.0, 1.0)


def block_scale(own_key, shape, shards, low, top_value):
    def one(axis_at, blocks):
        steps = jax.random.uniform(jax.random.fold_in(jax.random.fold_in(own_key, 6), axis_at), (blocks,), jnp.float32, low / len(shards), top_value / len(shards))
        return jnp.repeat(jnp.exp(steps), shape[axis_at] // blocks).reshape((-1,) + (1,) * (len(shape) - axis_at - 1))

    level = one(*shards[0])
    for cut in shards[1:]:
        level = level * one(*cut)
    return level


def centred(key, dims, deviation, most, pieces=(), held_as=jnp.bfloat16):
    array = jax.random.normal(key, dims, jnp.float32) * deviation
    if len(pieces) > 0:
        array = block_scale(key, dims, pieces, -0.22, 0.18) * array
    return jnp.clip(array, min=-most, max=most).astype(held_as)


def setup_inputs(seed: int = 0) -> dict:
    arg_keys = jax.random.split(jax.random.key(seed), 17)
    inputs = draw_inputs(jax.random.fold_in(arg_keys[16], 71), 0)
    cotangent = centred(arg_keys[1], (LENGTH, D), 1.0, 6.0, ((0, 8),), jnp.float32)
    random_proj = draw_random_proj(jax.random.fold_in(arg_keys[16], 71), 0)
    position_bias = centred(arg_keys[3], (HEADS, 2 * LENGTH), 1.0, 3.0, ((1, 8),), jnp.float32)
    w_qkv = draw_w_qkv(jax.random.fold_in(arg_keys[16], 71), 0)
    b_qkv = draw_b_qkv(jax.random.fold_in(arg_keys[16], 71), 0)
    w_out = centred(arg_keys[6], (D, D), (D // 16) ** -0.5, 0.875, ((0, 8),), jnp.float32)
    b_out = centred(arg_keys[7], (D,), 0.3, 1.0, ((0, 8),), jnp.float32)
    ln1_gain = jnp.clip(1.0 + 0.1 * jax.random.normal(arg_keys[8], (D,), jnp.float32), 0.5, 1.5)
    ln1_bias = centred(arg_keys[9], (D,), 0.3, 1.0, ((0, 8),), jnp.float32)
    w_up = centred(arg_keys[10], (D, FF), D ** -0.5, 0.21875, ((0, 8),), jnp.float32)
    b_up = centred(arg_keys[11], (FF,), 0.3, 1.0, ((0, 8),), jnp.float32)
    w_down = centred(arg_keys[12], (FF, D), FF ** -0.5, 0.109375, ((0, 8),), jnp.float32)
    b_down = centred(arg_keys[13], (D,), 0.3, 1.0, ((0, 8),), jnp.float32)
    ln2_gain = jnp.clip(1.0 + 0.1 * jax.random.normal(arg_keys[14], (D,), jnp.float32), 0.5, 1.5)
    ln2_bias = centred(arg_keys[15], (D,), 0.3, 1.0, ((0, 8),), jnp.float32)
    return dict(inputs=inputs, cotangent=cotangent, random_proj=random_proj, position_bias=position_bias, w_qkv=w_qkv, b_qkv=b_qkv, w_out=w_out, b_out=b_out, ln1_gain=ln1_gain, ln1_bias=ln1_bias, w_up=w_up, b_up=b_up, w_down=w_down, b_down=b_down, ln2_gain=ln2_gain, ln2_bias=ln2_bias)


@jax.custom_vjp
def low(v):
    return lax.optimization_barrier(v.astype(jnp.bfloat16)).astype(jnp.float32)

@jax.custom_vjp
def low_back(v):
    return v

def low_keep(v):
    return (low(v), None)

def low_pass(kept, grad):
    return (grad,)

def back_keep(v):
    return (v, None)

def back_low(kept, grad):
    return (low(grad),)
low.defvjp(low_keep, low_pass)
low_back.defvjp(back_keep, back_low)
eps_norm = 1e-06
highest = lax.Precision.HIGHEST

def toeplitz(window, row_count, col_count):
    span_count = row_count + col_count - 1
    turned = jnp.roll(window[:, ::-1], -(row_count - 1), axis=1)
    flattened = jnp.tile(turned, (1, row_count))[:, :row_count * (span_count - 1)]
    return flattened.reshape(window.shape[0], row_count, span_count - 1)[:, :, :col_count]

def block_terms(query_maps, key_maps, value_block, window):
    scores = jnp.einsum('ihm,jhm->hij', query_maps, key_maps, precision=highest)
    weight = scores * toeplitz(window, query_maps.shape[0], key_maps.shape[0])
    numerator = jnp.einsum('hij,jhe->ihe', weight, value_block, precision=highest)
    denominator = lax.optimization_barrier(jnp.sum(weight, axis=2)).T
    return (numerator, denominator)

def layer_norm(values_in, norm_gain, norm_bias):
    average = lax.optimization_barrier(jnp.mean(values_in, axis=1, keepdims=True))
    centered = values_in - average
    variance = lax.optimization_barrier(jnp.mean(centered * centered, axis=1, keepdims=True))
    return centered * lax.rsqrt(variance + eps_norm) * norm_gain + norm_bias

def feature_maps(qkv_rows, random_proj):
    row_count = qkv_rows.shape[0]
    model_width = HEADS * HEAD_DIM
    root_scale = HEAD_DIM ** (-0.25)
    queries = qkv_rows[:, :model_width].reshape(row_count, HEADS, HEAD_DIM) * root_scale
    key_vecs = qkv_rows[:, model_width:2 * model_width].reshape(row_count, HEADS, HEAD_DIM) * root_scale
    value_rows = qkv_rows[:, 2 * model_width:]
    phi_q = jnp.exp(jnp.einsum('lhe,em->lhm', queries, random_proj, precision=highest))
    key_proj = jnp.einsum('lhe,em->lhm', key_vecs, random_proj, precision=highest)
    phi_k = jnp.exp(key_proj - 0.5 * lax.optimization_barrier(jnp.sum(key_vecs * key_vecs, axis=2, keepdims=True)))
    return (phi_q, phi_k.reshape(row_count, -1), value_rows)

def feed_forward(attended, residual, w_out, b_out, gain_one, bias_one, w_up, b_up, w_down, b_down, gain_two, bias_two):
    projected = jnp.dot(attended, w_out, precision=highest, preferred_element_type=jnp.float32) + b_out
    first_norm = layer_norm(residual + projected, gain_one, bias_one)
    pre_act = jnp.dot(first_norm, w_up, precision=highest, preferred_element_type=jnp.float32) + b_up
    hidden = jax.nn.gelu(pre_act, approximate=False)
    branch = jnp.dot(hidden, w_down, precision=highest, preferred_element_type=jnp.float32) + b_down
    return layer_norm(first_norm + branch, gain_two, bias_two)

def attention(phi_q, phi_k, value_all, bias_factor):
    length = phi_q.shape[0]
    query_rows = min(512, length)
    key_rows = min(2048, length)
    key_starts = jnp.arange(0, length, key_rows, dtype=jnp.int32)
    query_starts = jnp.arange(0, length, query_rows, dtype=jnp.int32)

    def per_query(q_start):
        query_block = lax.dynamic_slice_in_dim(phi_q, q_start, query_rows, 0)

        def per_key(running, k_start):
            key_block = lax.dynamic_slice_in_dim(phi_k, k_start, key_rows, 0)
            value_block = lax.dynamic_slice_in_dim(value_all, k_start, key_rows, 0)
            table_first = q_start - k_start + length - key_rows + 1
            window = lax.dynamic_slice_in_dim(bias_factor, table_first, query_rows + key_rows - 1, 1)
            numerator, denominator = block_terms(query_block, key_block, value_block, window)
            return ((running[0] + numerator, running[1] + denominator), None)
        initial = (jnp.zeros((query_rows, HEADS, HEAD_DIM), jnp.float32), jnp.zeros((query_rows, HEADS), jnp.float32))
        (numerator, denominator), unused = lax.scan(jax.checkpoint(per_key), initial, key_starts)
        return numerator / denominator[:, :, None]
    attended = lax.map(jax.checkpoint(per_query), query_starts)
    return attended.reshape(length, HEADS * HEAD_DIM)

def reference(inputs, cotangent, random_proj, position_bias, w_qkv, b_qkv, w_out, b_out, ln1_gain, ln1_bias, w_up, b_up, w_down, b_down, ln2_gain, ln2_bias):

    def forward(inputs, position_bias, w_qkv, b_qkv, w_out, b_out, ln1_gain, ln1_bias, w_up, b_up, w_down, b_down, ln2_gain, ln2_bias):
        length = inputs.shape[0]
        qkv_rows = jnp.dot(inputs, w_qkv, precision=highest, preferred_element_type=jnp.float32) + b_qkv
        phi_q, key_feats, value_rows = feature_maps(qkv_rows, random_proj)
        attended = attention(phi_q, key_feats.reshape(length, HEADS, -1), value_rows.reshape(length, HEADS, HEAD_DIM), jnp.exp(position_bias))
        return feed_forward(attended, inputs, w_out, b_out, ln1_gain, ln1_bias, w_up, b_up, w_down, b_down, ln2_gain, ln2_bias)
    output, pullback = jax.vjp(forward, inputs, position_bias, w_qkv, b_qkv, w_out, b_out, ln1_gain, ln1_bias, w_up, b_up, w_down, b_down, ln2_gain, ln2_bias)
    d_inputs, d_position_bias, d_w_qkv, d_b_qkv, d_w_out, d_b_out, d_ln1_gain, d_ln1_bias, d_w_up, d_b_up, d_w_down, d_b_down, d_ln2_gain, d_ln2_bias = pullback(cotangent)
    return (output, d_inputs, d_position_bias, d_w_qkv, d_b_qkv, d_w_out, d_b_out, d_ln1_gain, d_ln1_bias, d_w_up, d_b_up, d_w_down, d_b_down, d_ln2_gain, d_ln2_bias)
```

```python
import functools

import jax
import jax.numpy as jnp
from jax import lax
from jax.experimental import pallas as pl
from jax.experimental.pallas import tpu as pltpu
from jax.sharding import Mesh
from jax.sharding import PartitionSpec as P

HEADS = 12
HEAD_DIM = 64
FEATURES = 64
EPS = 1e-06
f32 = jnp.float32
bf16 = jnp.bfloat16

GROUP = ("y", "x")
FEAT = ("y", "core")


def split(value):
    high = value.astype(bf16)
    return high, (value - high.astype(f32)).astype(bf16)


def dot(a, b, ca, cb):
    return lax.dot_general(a, b, (((ca,), (cb,)), ((), ())), preferred_element_type=f32)


def dot3s(a, b, ca, cb):
    return dot(a[0], b[0], ca, cb) + (dot(a[0], b[1], ca, cb) + dot(a[1], b[0], ca, cb))


def dot3(a, b, ca, cb):
    return dot3s(split(a), split(b), ca, cb)


def call(kernel, outs, args, name, scratch=(), flops=0, smem=0):
    nbytes = sum(a.size * a.dtype.itemsize for a in args) + sum(
        o.size * o.dtype.itemsize for o in outs
    )
    return pl.pallas_call(
        kernel,
        out_shape=outs,
        in_specs=[
            pl.BlockSpec(memory_space=pltpu.SMEM if i < smem else pltpu.VMEM)
            for i in range(len(args))
        ],
        out_specs=[pl.BlockSpec(memory_space=pltpu.VMEM)] * len(outs),
        scratch_shapes=list(scratch),
        compiler_params=pltpu.CompilerParams(vmem_limit_bytes=48 * 1024 * 1024),
        cost_estimate=pl.CostEstimate(flops=flops, bytes_accessed=nbytes, transcendentals=0),
        name=name,
    )(*args)


def shape(*dims, dtype=f32):
    return jax.ShapeDtypeStruct(dims, dtype)


def assemble(target, own, other, first, rows, core):
    for held in (0, 1):

        @pl.when(core == held)
        def _():
            for z in range(own.shape[0]):
                at = rows * (2 * z + held)
                target[at : at + rows, :] = own[z, first : first + rows, :]
                at = rows * (2 * z + 1 - held)
                target[at : at + rows, :] = other[z, first : first + rows, :]


def qkv_kernel(rows, ids, x_ref, own, other, b_ref, proj_ref, w_out, pq_out, kv_out, key_out):
    assemble(w_out, own, other, 0, rows, ids[0])
    qkv = dot3(x_ref[...], w_out[...], 1, 0) + b_ref[...]
    turned = qkv.T
    scale = HEAD_DIM**-0.25
    proj = split(proj_ref[...])
    heads = pq_out.shape[0] // HEAD_DIM
    for h in range(heads):
        lo, hi = HEAD_DIM * h, HEAD_DIM * (h + 1)
        width = heads * HEAD_DIM
        q = turned[lo:hi] * scale
        k = turned[width + lo : width + hi] * scale
        pq_out[lo:hi] = jnp.exp(dot3s(proj, split(q), 0, 0))
        pk = dot3s(proj, split(k), 0, 0) - 0.5 * jnp.sum(k * k, axis=0, keepdims=True)
        kv_out[128 * h : 128 * h + 64] = jnp.exp(pk)
        kv_out[128 * h + 64 : 128 * h + 128] = turned[2 * width + lo : 2 * width + hi]
        key_out[lo:hi] = k


def rolled_rows(table, row):
    wide = jnp.broadcast_to(row, (8, row.shape[1]))
    return pltpu.roll(wide, 0, 1, stride=1, stride_axis=0)


def factor_tile(window, queries):
    rows = []
    for g in range(queries // 8):
        moved = window if g == 0 else pltpu.roll(window, 8 * g, 1)
        rows.append(moved[:, queries:])
    return jnp.concatenate(rows, axis=0)


def attention_kernel(groups, blocks, ids, starts, *refs):
    nkv = blocks if groups == 1 else 1
    kv_refs = refs[:nkv]
    pq_ref, bias_ref, w_ref = refs[nkv : nkv + 3]
    kcat, vcat, att_out, den_out = refs[nkv + 3 : nkv + 7]
    parts = refs[nkv + 7 : nkv + 11]
    table, qcat, out_rows = refs[nkv + 11 :]
    heads = pq_ref.shape[0] // 64
    queries = pq_ref.shape[1]
    step = pl.program_id(0)

    @pl.when(step == 0)
    def _():
        for h in range(heads):
            table[8 * h : 8 * h + 8] = rolled_rows(table, jnp.exp(bias_ref[h : h + 1]))
            high, low = split(pq_ref[64 * h : 64 * h + 64])
            qcat[h, 0:64] = high
            qcat[h, 64:128] = high
            qcat[h, 128:192] = low
        att_out[...] = jnp.zeros_like(att_out)
        den_out[...] = jnp.zeros_like(den_out)

    for n in range(blocks):
        block = kv_refs[n] if groups == 1 else kv_refs[0].at[n]
        for h in range(heads):
            for part, cat in ((0, kcat), (64, vcat)):
                high, low = split(block[128 * h + part : 128 * h + part + 64])
                cat[n, h, 0:64] = high
                cat[n, h, 64:128] = low
                cat[n, h, 128:192] = high

    def advance(n, carry):
        start = pl.multiple_of(starts[step * blocks + n], 128)
        for h in range(heads):
            scores = dot(kcat[n, h], qcat[h], 0, 0)
            window = table[8 * h : 8 * h + 8, pl.ds(start, 2 * queries)]
            weight = scores * factor_tile(window, queries)
            high, low = split(weight)
            both = dot(vcat[n, h, 0:128], high, 1, 0)
            more = dot(vcat[n, h, 0:64], low, 1, 0)
            att_out[64 * h : 64 * h + 64] += both[0:64] + both[64:128] + more
            den_out[h : h + 1] += jnp.sum(weight, axis=0, keepdims=True)
        return carry

    lax.fori_loop(0, blocks, advance, 0)

    @pl.when(step == groups - 1)
    def _():
        for h in range(heads):
            att_out[64 * h : 64 * h + 64] = att_out[64 * h : 64 * h + 64] / den_out[h : h + 1]
        out_rows[...] = dot3(att_out[...], w_ref[...], 0, 0)
        rows = queries // 4
        for k in range(4):
            first = pl.multiple_of(lax.bitwise_xor(ids[1], k) * rows, 8)
            parts[k][...] = out_rows[pl.ds(first, rows), :]


def attention(ids, starts, kv, pq, window, w_rows):
    stacked = not isinstance(kv, list)
    count = kv.shape[0] if stacked else len(kv)
    blocks = 8 if stacked else count
    groups = count // blocks
    kv = [kv] if stacked else kv
    queries = pq.shape[1]
    heads = pq.shape[0] // 64
    width = w_rows.shape[1]
    whole = lambda a: pl.BlockSpec(a.shape, lambda g, nd=len(a.shape): (0,) * nd)
    smem = pl.BlockSpec(memory_space=pltpu.SMEM)
    kv_spec = (
        [pl.BlockSpec((blocks,) + kv[0].shape[1:], lambda g: (g, 0, 0))]
        if stacked
        else [whole(a) for a in kv]
    )
    cat = shape(count, heads, 192, queries, dtype=bf16)
    cat_spec = pl.BlockSpec((blocks, heads, 192, queries), lambda g: (g, 0, 0, 0))
    rows = shape(queries // 4, width)
    outs = [cat, cat, shape(heads * 64, queries), shape(8, queries)] + [rows] * 4
    specs = [cat_spec, cat_spec] + [whole(a) for a in outs[2:]]
    tile = queries * queries * 64
    return pl.pallas_call(
        functools.partial(attention_kernel, groups, blocks),
        grid=(groups,),
        out_shape=outs,
        in_specs=[smem, smem] + kv_spec + [whole(pq), whole(window), whole(w_rows)],
        out_specs=specs,
        scratch_shapes=[
            pltpu.VMEM((8 * heads, window.shape[1]), f32),
            pltpu.VMEM((heads, 192, queries), bf16),
            pltpu.VMEM((queries, width), f32),
        ],
        compiler_params=pltpu.CompilerParams(vmem_limit_bytes=52 * 1024 * 1024),
        cost_estimate=pl.CostEstimate(
            flops=12 * tile * count * heads, bytes_accessed=8 << 20, transcendentals=0
        ),
        name="attention",
    )(ids, starts, *kv, pq, window, w_rows)


def attention_back_kernel(groups, blocks, ids, starts, *refs):
    kcat, vcat, pq_ref, bias_ref, w_ref, att_ref, den_ref = refs[:7]
    dz = refs[7:11]
    nkv = blocks if groups == 1 else 1
    dkv = refs[11 : 11 + nkv]
    dpq_out, dbias_out, dz_out = refs[11 + nkv : 14 + nkv]
    table, qcat, gcat, gden, diag = refs[14 + nkv :]
    heads = pq_ref.shape[0] // 64
    queries = pq_ref.shape[1]
    step = pl.program_id(0)

    @pl.when(step == 0)
    def _():
        rows = queries // 4
        for k in range(4):
            first = pl.multiple_of(lax.bitwise_xor(ids[1], k) * rows, 8)
            dz_out[pl.ds(first, rows), :] = dz[k][...]
        d_att = dot3(w_ref[...], dz_out[...], 1, 1)
        gden[...] = jnp.zeros_like(gden)
        for h in range(heads):
            lo, hi = 64 * h, 64 * h + 64
            table[8 * h : 8 * h + 8] = rolled_rows(table, jnp.exp(bias_ref[h : h + 1]))
            for value, cat in ((pq_ref[lo:hi], qcat), (d_att[lo:hi] / den_ref[h : h + 1], gcat)):
                high, low = split(value)
                cat[h, 0:64] = high
                cat[h, 64:128] = high
                cat[h, 128:192] = low
            gden[h : h + 1] = -(
                jnp.sum(d_att[lo:hi] * att_ref[lo:hi], axis=0, keepdims=True) / den_ref[h : h + 1]
            )
        dpq_out[...] = jnp.zeros_like(dpq_out)
        diag[...] = jnp.zeros_like(diag)

    def advance(n, carry):
        start = pl.multiple_of(starts[step * blocks + n], 128)
        for h in range(heads):
            scores = dot(kcat[n, h], qcat[h], 0, 0)
            factor = factor_tile(table[8 * h : 8 * h + 8, pl.ds(start, 2 * queries)], queries)
            d_weight = dot(vcat[n, h], gcat[h], 0, 0) + gden[h : h + 1]
            w_high, w_low = split(scores * factor)
            e_high, e_low = split(d_weight * factor)
            pairs = d_weight * scores
            both = dot(gcat[h, 64:192], w_high, 1, 1)
            dv = both[0:64] + both[64:128] + dot(gcat[h, 0:64], w_low, 1, 1)
            both = dot(qcat[h, 64:192], e_high, 1, 1)
            dk = both[0:64] + both[64:128] + dot(qcat[h, 0:64], e_low, 1, 1)
            both = dot(kcat[n, h, 0:128], e_high, 1, 0)
            dq = both[0:64] + both[64:128] + dot(kcat[n, h, 0:64], e_low, 1, 0)
            dpq_out[64 * h : 64 * h + 64] += dq
            if groups == 1:
                for i in range(blocks):

                    @pl.when(n == i)
                    def _():
                        dkv[i][128 * h : 128 * h + 64] = dk
                        dkv[i][128 * h + 64 : 128 * h + 128] = dv
            else:
                dkv[0][n, 128 * h : 128 * h + 64] = dk
                dkv[0][n, 128 * h + 64 : 128 * h + 128] = dv
            total = jnp.zeros((8, 2 * queries), f32)
            empty = jnp.zeros((8, queries), f32)
            for g in range(queries // 8):
                padded = jnp.concatenate([empty, pairs[8 * g : 8 * g + 8]], axis=1)
                total = total + (padded if g == 0 else pltpu.roll(padded, 2 * queries - 8 * g, 1))
            diag[8 * h : 8 * h + 8, pl.ds(start, 2 * queries)] += total
        return carry

    lax.fori_loop(0, blocks, advance, 0)

    @pl.when(step == groups - 1)
    def _():
        length = diag.shape[1]
        dbias_out[...] = jnp.zeros_like(dbias_out)
        for h in range(heads):
            total = diag[8 * h : 8 * h + 1]
            for s in range(1, 8):
                total = total + pltpu.roll(diag[8 * h + s : 8 * h + s + 1], length - s, 1)
            dbias_out[h : h + 1] = total * jnp.exp(bias_ref[h : h + 1])


def attention_back(ids, starts, kcat, vcat, pq, window, w_rows, att, den, dz, stacked):
    count, heads, _, queries = kcat.shape
    blocks = 8 if stacked else count
    groups = count // blocks
    whole = lambda a: pl.BlockSpec(a.shape, lambda g, nd=len(a.shape): (0,) * nd)
    smem = pl.BlockSpec(memory_space=pltpu.SMEM)
    cat_spec = pl.BlockSpec((blocks, heads, 192, queries), lambda g: (g, 0, 0, 0))
    if stacked:
        dkv = [shape(count, heads * 128, queries)]
        dkv_spec = [pl.BlockSpec((blocks, heads * 128, queries), lambda g: (g, 0, 0))]
    else:
        dkv = [shape(heads * 128, queries)] * count
        dkv_spec = [whole(a) for a in dkv]
    outs = dkv + [
        shape(heads * 64, queries),
        shape(8, window.shape[1]),
        shape(queries, w_rows.shape[1]),
    ]
    small = [pq, window, w_rows, att, den] + list(dz)
    tile = queries * queries * 64
    return pl.pallas_call(
        functools.partial(attention_back_kernel, groups, blocks),
        grid=(groups,),
        out_shape=outs,
        in_specs=[smem, smem, cat_spec, cat_spec] + [whole(a) for a in small],
        out_specs=dkv_spec + [whole(a) for a in outs[len(dkv) :]],
        scratch_shapes=[
            pltpu.VMEM((8 * heads, window.shape[1]), f32),
            pltpu.VMEM((heads, 192, queries), bf16),
            pltpu.VMEM((heads, 192, queries), bf16),
            pltpu.VMEM((8, queries), f32),
            pltpu.VMEM((8 * heads, window.shape[1]), f32),
        ],
        compiler_params=pltpu.CompilerParams(vmem_limit_bytes=52 * 1024 * 1024),
        cost_estimate=pl.CostEstimate(
            flops=30 * tile * count * heads, bytes_accessed=12 << 20, transcendentals=0
        ),
        name="attention_back",
    )(ids, starts, kcat, vcat, *small)


def normed(value):
    mean = jnp.mean(value, axis=1, keepdims=True)
    centered = value - mean
    var = jnp.mean(centered * centered, axis=1, keepdims=True)
    inverse = lax.rsqrt(var + EPS)
    return centered * inverse, inverse


def norm_back(upstream, n, inverse, gain):
    scaled = gain * upstream
    mean = jnp.mean(scaled, axis=1, keepdims=True)
    slope = jnp.mean(scaled * n, axis=1, keepdims=True)
    return (scaled - mean - n * slope) * inverse


def colsum(value):
    return jnp.sum(value, axis=0, keepdims=True)


def norm_one_kernel(ids, p0, p1, p2, p3, x_ref, vec_ref, first_out, n_out, inverse_out):
    rows = p0.shape[0]
    at = pl.multiple_of(ids[1] * rows, 8)
    value = x_ref[pl.ds(at, rows), :] + ((p0[...] + p1[...]) + (p2[...] + p3[...]) + vec_ref[1:2])
    n, inverse = normed(value)
    first_out[...] = n * vec_ref[2:3] + vec_ref[3:4]
    n_out[...] = n
    inverse_out[...] = jnp.broadcast_to(inverse, inverse_out.shape)


def norm_two_kernel(p0, p1, p2, p3, first_ref, cot_ref, vec_ref, rows_out, dz_out, grads_out):
    value = first_ref[...] + ((p0[...] + p1[...]) + (p2[...] + p3[...]) + vec_ref[4:5])
    n, inverse = normed(value)
    rows_out[...] = n * vec_ref[5:6] + vec_ref[6:7]
    up = cot_ref[...]
    dz = norm_back(up, n, inverse, vec_ref[5:6])
    dz_out[...] = dz
    grads_out[...] = jnp.zeros_like(grads_out)
    grads_out[0:1] = colsum(up * n)
    grads_out[1:2] = colsum(up)
    grads_out[2:3] = colsum(dz)


def norm_one_back_kernel(p0, p1, p2, p3, dz_ref, n_ref, inverse_ref, vec_ref, dz_out, grads_out):
    up = dz_ref[...] + ((p0[...] + p1[...]) + (p2[...] + p3[...]))
    n = n_ref[...]
    dz = norm_back(up, n, inverse_ref[:, 0:1], vec_ref[2:3])
    dz_out[...] = dz
    grads_out[...] = jnp.zeros_like(grads_out)
    grads_out[0:1] = colsum(up * n)
    grads_out[1:2] = colsum(up)
    grads_out[2:3] = colsum(dz)


def stack_rows(target, refs):
    rows = refs[0].shape[0]
    for k, ref in enumerate(refs):
        target[rows * k : rows * (k + 1), :] = ref[...]


def forward_kernel(rows_up, rows_down, ids, f0, f1, f2, f3, own, other, vec_ref, *refs):
    pre_out, first_out, up_out, down_out = refs[:4]
    parts = refs[4:8]
    assemble(up_out, own, other, 0, rows_up, ids[0])
    assemble(down_out, own, other, rows_up, rows_down, ids[0])
    stack_rows(first_out, (f0, f1, f2, f3))
    pre = dot3(first_out[...], up_out[...], 1, 0) + vec_ref[0:1]
    pre_out[...] = pre
    hidden = 0.5 * pre * (1.0 + lax.erf(pre * (0.5**0.5)))
    branch = dot3(hidden, down_out[...], 1, 0)
    rows = f0.shape[0]
    for k in range(4):
        parts[k][...] = branch[rows * k : rows * (k + 1)]


def backward_kernel(z0, z1, z2, z3, pre_ref, up_ref, down_ref, *refs):
    dz_out, d_pre_out = refs[:2]
    parts = refs[2:6]
    stack_rows(dz_out, (z0, z1, z2, z3))
    d_hidden = dot3(dz_out[...], down_ref[...], 1, 1)
    pre = pre_ref[...]
    density = jnp.exp(-0.5 * pre * pre) * ((2.0 * jnp.pi) ** -0.5)
    d_pre = d_hidden * (0.5 * (1.0 + lax.erf(pre * (0.5**0.5))) + pre * density)
    d_pre_out[...] = d_pre
    d_first = dot3(d_pre, up_ref[...], 1, 1)
    rows = z0.shape[0]
    for k in range(4):
        parts[k][...] = d_first[rows * k : rows * (k + 1)]


def spread(ids, keep, send, rows_at, count, source):
    for held in (0, 1):

        @pl.when(ids[0] == held)
        def _():
            for z in range(keep.shape[0]):
                at = count * (2 * z + held)
                keep[z, rows_at : rows_at + count, :] = source[at : at + count, :]
                at = count * (2 * z + 1 - held)
                send[z, rows_at : rows_at + count, :] = source[at : at + count, :]


def spread_lanes(ids, keep, send, row, lane, count, source):
    for held in (0, 1):

        @pl.when(ids[0] == held)
        def _():
            for z in range(keep.shape[0]):
                at = count * (2 * z + held)
                keep[z, row : row + 1, lane : lane + count] = source[:, at : at + count]
                at = count * (2 * z + 1 - held)
                send[z, row : row + 1, lane : lane + count] = source[:, at : at + count]


def ff_weights_kernel(
    rows_up, rows_down, ids, first_ref, d_pre_ref, pre_ref, dz_ref, grads_ref, keep, send, held
):
    pre = pre_ref[...]
    hidden = 0.5 * pre * (1.0 + lax.erf(pre * (0.5**0.5)))
    d_pre = d_pre_ref[...]
    base = rows_up + rows_down
    for ref in (keep, send):
        ref[:, base:, :] = jnp.zeros((ref.shape[0], ref.shape[1] - base, ref.shape[2]), f32)
    spread_lanes(ids, keep, send, base, 0, rows_down, colsum(d_pre))
    for i in range(3):
        spread_lanes(ids, keep, send, base + 1 + i, 0, rows_up, grads_ref[i : i + 1])
    held[...] = dot3(first_ref[...], d_pre, 0, 0)
    spread(ids, keep, send, 0, rows_up, held)
    held[...] = dot3(hidden, dz_ref[...], 0, 0)
    spread(ids, keep, send, rows_up, rows_down, held)


def out_weights_kernel(att_ref, dz_ref, out):
    out[...] = dot3(att_ref[...], dz_ref[...], 1, 0)


def qkv_back_kernel(d0, d1, d2, d3, pq_ref, dpq_ref, kv_ref, key_ref, proj_ref, w_ref, *refs):
    d_qkv_out = refs[0]
    parts = refs[1:5]
    turned, rows_held = refs[5:]
    heads = pq_ref.shape[0] // 64
    width = heads * 64
    scale = HEAD_DIM**-0.25
    proj = split(proj_ref[...])
    dkv = (d0[...] + d1[...]) + (d2[...] + d3[...])
    for h in range(heads):
        lo, hi = 64 * h, 64 * h + 64
        turned[lo:hi] = scale * dot3s(proj, split(dpq_ref[lo:hi] * pq_ref[lo:hi]), 1, 0)
        pk = dkv[128 * h : 128 * h + 64] * kv_ref[128 * h : 128 * h + 64]
        turned[width + lo : width + hi] = scale * (
            dot3s(proj, split(pk), 1, 0) - key_ref[lo:hi] * colsum(pk)
        )
        turned[2 * width + lo : 2 * width + hi] = dkv[128 * h + 64 : 128 * h + 128]
    d_qkv = turned[...].T
    d_qkv_out[...] = d_qkv
    d_inputs = dot3(d_qkv, w_ref[...], 1, 1)
    rows = parts[0].shape[0]
    rows_held[...] = d_inputs
    ids = None
    for k in range(4):
        parts[k][...] = rows_held[rows * k : rows * (k + 1), :]


def qkv_weights_kernel(rows, ids, x_ref, d_ref, dbias_ref, grads_ref, keep, send, held):
    d_qkv = d_ref[...]
    lanes = keep.shape[2]
    for ref in (keep, send):
        ref[:, rows:, :] = jnp.zeros((ref.shape[0], ref.shape[1] - rows, lanes), f32)
        for z in range(ref.shape[0]):
            ref[z, rows : rows + 1, :] = colsum(d_qkv)
    for i in range(3):
        spread_lanes(ids, keep, send, rows + 1, rows * i, rows, grads_ref[i : i + 1])
    heads = dbias_ref.shape[0]
    for h in range(3):
        spread_lanes(ids, keep, send, rows + 2 + h, 0, 512, dbias_ref[h : h + 1])
    held[...] = dot3(x_ref[...], d_qkv, 0, 0)
    spread(ids, keep, send, 0, rows, held)


def sum_four_kernel(ids, p0, p1, p2, p3, dz_ref, out):
    out[...] = dz_ref[...] + ((p0[...] + p1[...]) + (p2[...] + p3[...]))


def place_kernel(ids, r0, r1, r2, r3, out):
    rows = r0.shape[0]
    for k, ref in enumerate((r0, r1, r2, r3)):
        out[pl.ds(pl.multiple_of(lax.bitwise_xor(ids[2], k) * rows, 8), rows), :] = ref[...]


def exchange(value, axes, count, k):
    return lax.ppermute(value, axes, [(i, i ^ k) for i in range(count)])


def swap(value):
    return lax.ppermute(value, ("core", "x"), [(0, 0), (1, 2), (2, 1), (3, 3)])


def from_group(value, members):
    return [value] + [exchange(value, GROUP, members, k) for k in range(1, members)]


def to_group(parts):
    return [parts[0]] + [
        exchange(parts[k], GROUP, len(parts), k) for k in range(1, len(parts))
    ]


def to_feat(value, ys):
    axes = ("y", "core", "x")
    got = []
    for k in range(2 * ys):
        ky, kc = divmod(k, 2)
        pairs = []
        for y in range(ys):
            for core in (0, 1):
                for x in (0, 1):
                    pairs.append(((y * 2 + core) * 2 + x, ((y ^ ky) * 2 + (x ^ kc)) * 2 + core))
        got.append(lax.ppermute(value, axes, pairs))
    return got


def body(
    ys,
    zs,
    inputs,
    cotangent,
    random_proj,
    position_bias,
    w_qkv,
    b_qkv,
    w_out,
    b_out,
    ln1_gain,
    ln1_bias,
    w_up,
    b_up,
    w_down,
    b_down,
    ln2_gain,
    ln2_bias,
):
    members = 2 * ys
    blocks = 2 * zs
    core = lax.axis_index("core")
    x_at, y_at, z_at = lax.axis_index("x"), lax.axis_index("y"), lax.axis_index("z")
    feat = 2 * y_at + core
    group = 2 * y_at + x_at
    block = 2 * z_at + core
    ids = jnp.stack([core, group, feat, block]).astype(jnp.int32)
    queries, width = inputs.shape
    rows = queries // members
    shard = w_qkv.shape[0]
    down = w_down.shape[0] // members
    heads = HEADS // members
    lanes = heads * HEAD_DIM
    span = position_bias.shape[1]

    qkv_cols = lax.dynamic_index_in_dim(
        w_qkv.reshape(shard, 3, members, lanes), feat, 2, keepdims=False
    ).reshape(shard, 3 * lanes)
    bias_rows = lax.dynamic_slice_in_dim(position_bias, feat * heads, heads, 0)
    full = 3 * lanes
    extra = jnp.concatenate(
        [
            jnp.pad(b_qkv[None], ((0, 0), (0, full - b_qkv.shape[0]))),
            jnp.pad(bias_rows, ((0, 0), (0, full - span))),
            jnp.zeros((7 - heads, full), f32),
        ],
        axis=0,
    )
    slab = swap(jnp.concatenate([qkv_cols, extra], axis=0))
    x = swap(inputs)
    slab_own = lax.all_gather(slab, "z", axis=0)
    slab_other = exchange(slab_own, "core", 2, 1)
    proj = lax.all_gather(random_proj, FEAT, axis=1, tiled=True)

    both = jnp.stack([slab_own[:, shard:], slab_other[:, shard:]], axis=1)
    both = jnp.where(core == 0, both, both[:, ::-1]).reshape(blocks, 8, full)
    b_all = both[:, 0, : b_qkv.shape[0]].reshape(3, members, lanes)
    b_cols = lax.dynamic_index_in_dim(b_all, group, 1, keepdims=False).reshape(1, full)
    bias_all = both[:, 1 : 1 + heads, :span].transpose(1, 0, 2).reshape(heads, blocks * span)
    window = lax.dynamic_slice_in_dim(bias_all, block * queries, (blocks + 1) * queries, 1)

    w_cols, pq, kv, keys = call(
        functools.partial(qkv_kernel, shard),
        [
            shape(width, full),
            shape(lanes, queries),
            shape(2 * lanes, queries),
            shape(lanes, queries),
        ],
        [ids, x, slab_own, slab_other, b_cols, proj],
        "qkv",
        flops=6 * queries * width * full,
        smem=1,
    )

    up_cols = lax.dynamic_index_in_dim(
        w_up.reshape(shard, blocks, members, down), feat, 2, keepdims=False
    ).reshape(shard, blocks * down)
    down_rows = lax.dynamic_slice_in_dim(w_down, feat * down, down, 0)
    up_part = lax.dynamic_slice_in_dim(b_up, feat * down, down, 0)
    vecs = [up_part, b_out, ln1_gain, ln1_bias, b_down, ln2_gain, ln2_bias]
    vec_rows = jnp.concatenate(
        [jnp.pad(v[None], ((0, 0), (0, width - v.shape[0]))) for v in vecs]
        + [jnp.zeros((1, width), f32)],
        axis=0,
    )
    ff_slab = swap(jnp.concatenate([up_cols, down_rows, vec_rows], axis=0))
    ff_own = lax.all_gather(ff_slab, "z", axis=0)
    ff_other = exchange(ff_own, "core", 2, 1)
    vec = jnp.stack([ff_own[:, shard + down :], ff_other[:, shard + down :]], axis=1)
    vec = jnp.where(core == 0, vec, vec[:, ::-1]).reshape(blocks, 8, width)
    vec = vec[:, :, :shard].transpose(1, 0, 2).reshape(8, width)

    if blocks == 2 * members:
        axes = ("y", "core", "z", "x")
        pairs = ([], [])
        for y in range(ys):
            for c in (0, 1):
                for z in range(zs):
                    for xx in (0, 1):
                        target = ((y * 2 + c) * zs + z) * 2 + xx
                        for which in (0, 1):
                            j = c ^ which
                            source = (((z >> 1) * 2 + (z & 1)) * zs + (2 * y + xx)) * 2 + j
                            pairs[which].append((source, target))
        a = lax.ppermute(w_out, axes, pairs[0])
        b = lax.ppermute(w_out, axes, pairs[1])
        w_rows = jnp.concatenate(
            [jnp.where(core == 0, a, b), jnp.where(core == 0, b, a)], axis=0
        )
    else:
        w_full = lax.all_gather(w_out, ("z", "x"), axis=0, tiled=True)
        w_rows = lax.dynamic_slice_in_dim(w_full, group * lanes, lanes, 0)

    stacked = blocks > 8
    order = jnp.stack([2 * (z_at ^ k) + core for k in range(zs)]).astype(jnp.int32)
    order = jnp.concatenate([order, order ^ 1])
    starts = (blocks - 1 - order) * queries
    kv_own = [kv] + [exchange(kv, "z", zs, k) for k in range(1, zs)]
    kv_other = [exchange(v, "core", 2, 1) for v in kv_own]
    kv_all = kv_own + kv_other
    if stacked:
        kv_all = jnp.stack(kv_all)
    got = attention(ids, starts, kv_all, pq, window, w_rows)
    kcat, vcat, att, den = got[:4]

    parts = to_group(got[4:])
    row_shape = shape(rows, width)
    first, norm_rows, inverse = call(
        norm_one_kernel,
        [row_shape, row_shape, shape(rows, 128)],
        [ids, *parts, x, vec],
        "norm_one",
        smem=1,
    )
    firsts = from_group(first, members)
    full_rows = shape(queries, blocks * down)
    got = call(
        functools.partial(forward_kernel, shard, down),
        [full_rows, shape(queries, width), shape(width, blocks * down), shape(blocks * down, width)]
        + [row_shape] * members,
        [ids, *firsts, ff_own, ff_other, vec],
        "forward",
        flops=12 * queries * width * blocks * down,
        smem=1,
    )
    pre, first_all, up_all, down_all = got[:4]
    parts = to_group(got[4:])
    cot_rows = swap(lax.dynamic_slice_in_dim(cotangent, feat * rows, rows, 0))
    out_rows, dz2, grads_two = call(
        norm_two_kernel,
        [row_shape, row_shape, shape(8, width)],
        [*parts, first, cot_rows, vec],
        "norm_two",
    )
    dzs = from_group(dz2, members)
    got = call(
        backward_kernel,
        [shape(queries, width), full_rows] + [row_shape] * members,
        [*dzs, pre, up_all, down_all],
        "backward",
        flops=12 * queries * width * blocks * down,
    )
    dz2_all, d_pre = got[:2]
    parts = to_group(got[2:])
    dz1, grads_one = call(
        norm_one_back_kernel,
        [row_shape, shape(8, width)],
        [*parts, dz2, norm_rows, inverse, vec],
        "norm_one_back",
    )
    dzs = from_group(dz1, members)

    stack = shape(zs, shard + down + 8, width)
    keep, send = call(
        functools.partial(ff_weights_kernel, shard, down),
        [stack, stack],
        [ids, first_all, d_pre, pre, dz2_all, grads_two],
        "ff_weights",
        scratch=[pltpu.VMEM((width, blocks * down), f32)],
        flops=12 * queries * width * blocks * down,
        smem=1,
    )
    ff_grads = keep + exchange(send, "core", 2, 1)
    ff_grads = lax.psum_scatter(ff_grads, "z", scatter_dimension=0, tiled=False)
    ff_grads = to_feat(ff_grads, ys)

    back = attention_back(
        ids, starts, kcat, vcat, pq, window, w_rows, att, den, dzs, stacked
    )
    dpq, dbias, dz1_all = back[-3:]
    if stacked:
        dkv_all = [back[0][i] for i in range(blocks)]
    else:
        dkv_all = back[:blocks]
    own = [
        dkv_all[k] + exchange(dkv_all[zs + k], "core", 2, 1) for k in range(zs)
    ]
    arrived = [own[0]] + [exchange(own[k], "z", zs, k) for k in range(1, zs)]
    while len(arrived) > 4:
        arrived = [a + b for a, b in zip(arrived[::2], arrived[1::2])]

    (d_out_part,) = call(
        out_weights_kernel,
        [shape(lanes, width)],
        [att, dz1_all],
        "out_weights",
        flops=6 * queries * lanes * width,
    )
    d_out_part = lax.psum_scatter(d_out_part, ("z", "core"), scatter_dimension=0, tiled=True)

    got = call(
        qkv_back_kernel,
        [shape(queries, full)] + [row_shape] * members,
        [*arrived, pq, dpq, kv, keys, proj, w_cols],
        "qkv_back",
        scratch=[pltpu.VMEM((full, queries), f32), pltpu.VMEM((queries, width), f32)],
        flops=6 * queries * width * full,
    )
    d_qkv = got[0]
    natural = jnp.stack(got[1:])
    parts = [
        lax.dynamic_index_in_dim(natural, group ^ k, 0, keepdims=False) for k in range(members)
    ]
    parts = to_group(parts)
    (d_input_rows,) = call(
        sum_four_kernel, [row_shape], [ids, *parts, dz1], "sum_rows", smem=1
    )

    table = jnp.zeros((heads, blocks * span), f32)
    table = lax.dynamic_update_slice_in_dim(table, dbias[:heads], block * queries, 1)
    stack = shape(zs, shard + 8, full)
    keep, send = call(
        functools.partial(qkv_weights_kernel, shard),
        [stack, stack],
        [ids, x, d_qkv, table, grads_one],
        "qkv_weights",
        scratch=[pltpu.VMEM((width, full), f32)],
        flops=6 * queries * width * full,
        smem=1,
    )
    qkv_grads = keep + exchange(send, "core", 2, 1)
    qkv_grads = lax.psum_scatter(qkv_grads, "z", scatter_dimension=0, tiled=False)
    qkv_grads = to_feat(qkv_grads, ys)

    def place(values, name):
        return call(
            place_kernel,
            [shape(members * values[0].shape[0], values[0].shape[1])],
            [ids, *values],
            name,
            smem=1,
        )[0]

    output = place(to_feat(out_rows, ys), "place_output")
    d_inputs = place(to_feat(d_input_rows, ys), "place_inputs")

    def natural_order(values):
        stack = jnp.stack(values)
        return jnp.stack(
            [lax.dynamic_index_in_dim(stack, feat ^ k, 0, keepdims=False) for k in range(members)]
        )

    ff_grads = natural_order(ff_grads)
    d_w_up = (
        ff_grads[:, :shard]
        .reshape(members, shard, blocks, down)
        .transpose(1, 2, 0, 3)
        .reshape(shard, w_up.shape[1])
    )
    d_w_down = ff_grads[:, shard : shard + down].reshape(members * down, width)
    ff_small = ff_grads[:, shard + down :]
    d_b_up = ff_small[:, 0, :down].reshape(members * down)
    ln_two = jnp.sum(ff_small[:, 1:4, :shard], axis=0)

    qkv_grads = natural_order(qkv_grads)
    d_w_qkv = (
        qkv_grads[:, :shard]
        .reshape(members, shard, 3, lanes)
        .transpose(1, 2, 0, 3)
        .reshape(shard, w_qkv.shape[1])
    )
    qkv_small = qkv_grads[:, shard:]
    d_b = qkv_small[:, 0].reshape(members, 3, lanes).transpose(1, 0, 2).reshape(-1)
    d_b_qkv = lax.dynamic_slice_in_dim(d_b, (2 * z_at + x_at) * b_qkv.shape[0], b_qkv.shape[0], 0)
    ln_one = jnp.sum(qkv_small[:, 1, : 3 * shard], axis=0).reshape(3, shard)
    d_position_bias = qkv_small[:, 2 : 2 + heads, :span].reshape(HEADS, span)

    if blocks == 2 * members:
        axes = ("y", "core", "z", "x")
        pieces = []
        for k in range(members):
            pairs = []
            for y in range(ys):
                for c in (0, 1):
                    for z in range(zs):
                        for xx in (0, 1):
                            source = ((y * 2 + c) * zs + z) * 2 + xx
                            q = (2 * (z % 2) + c) ^ k
                            pairs.append(
                                (source, (q * zs + (2 * y + xx)) * 2 + z // 2)
                            )
            pieces.append(lax.ppermute(d_out_part, axes, pairs))
        d_w_out = place(pieces, "place_out")
    else:
        all_out = lax.all_gather(d_out_part, ("y", "x", "z", "core"), axis=0, tiled=True)
        d_w_out = lax.dynamic_slice_in_dim(all_out, (2 * z_at + x_at) * shard, shard, 0)

    return (
        output,
        d_inputs,
        d_position_bias,
        d_w_qkv,
        d_b_qkv,
        d_w_out,
        ln_one[2],
        ln_one[0],
        ln_one[1],
        d_w_up,
        d_b_up,
        d_w_down,
        ln_two[2],
        ln_two[0],
        ln_two[1],
    )


def solution(mesh):
    feats, wides = mesh.shape["feat"], mesh.shape["wide"]
    ys, zs = feats // 2, wides // 2
    fine = Mesh(mesh.devices.reshape(ys, 2, zs, 2), ("y", "core", "z", "x"))
    wide = ("z", "x")
    mat, vector, lane = P(wide, None), P(wide), P(None, wide)
    return jax.shard_map(
        functools.partial(body, ys, zs),
        mesh=fine,
        in_specs=(mat, mat, P(None, FEAT), lane, mat, vector, mat, vector)
        + (vector, vector, mat, vector, mat, vector, vector, vector),
        out_specs=(mat, mat, lane, mat, vector, mat, vector, vector)
        + (vector, mat, vector, mat, vector, vector, vector),
        check_vma=False,
    )
```

```python
import functools
import math

import jax
import jax.numpy as jnp
from jax import lax
from jax.experimental import pallas as pl
from jax.experimental.pallas import tpu as pltpu
from jax.sharding import Mesh
from jax.sharding import PartitionSpec as P

HEADS = 12
HEAD_DIM = 64
FEATURES = 64
EPS = 1e-06
f32 = jnp.float32
bf16 = jnp.bfloat16

GROUP = ("y", "x")
FEAT = ("y", "core")
PLANE = ("zh", "x", "y", "core")
LINES = ("zh", "zl", "core")
CORE, MEMBER, OWN, HEAD, WIDE, PLACE = range(6)


def split(value):
    high = value.astype(bf16)
    return high, (value - high.astype(f32)).astype(bf16)


def dot(a, b, ca, cb):
    return lax.dot_general(a, b, (((ca,), (cb,)), ((), ())), preferred_element_type=f32)


def dot3s(a, b, ca, cb):
    return dot(a[0], b[0], ca, cb) + (dot(a[0], b[1], ca, cb) + dot(a[1], b[0], ca, cb))


def dot3(a, b, ca, cb):
    return dot3s(split(a), split(b), ca, cb)


def cost():
    return pl.CostEstimate(flops=1 << 20, bytes_accessed=1 << 10, transcendentals=0)


def tiled(dims):
    if len(dims) < 2:
        return 0
    return math.prod(dims[:-2]) * -(-dims[-2] // 8) * -(-dims[-1] // 128) * 4096


def call(kernel, outs, args, name, scratch=(), smem=0, room=8, limit=0, fetch=(), push=(), far=False, deep=False, early=False):
    held = sum(tiled(ref.shape) for ref in scratch)
    held += sum(size for size in map(lambda a: tiled(a.shape), [*args, *outs]) if size > 6 << 20)
    if deep and not far:
        fetch, push, limit = range(smem, len(args)), range(len(outs)), 60 << 20
    fetch, push = tuple(fetch), tuple(push)
    near = [pltpu.VMEM(args[i].shape, args[i].dtype) for i in fetch]
    near += [pltpu.VMEM(outs[i].shape, outs[i].dtype) for i in push]
    held += sum(args[i].size * args[i].dtype.itemsize for i in fetch)
    held += sum(outs[i].size * outs[i].dtype.itemsize for i in push)
    count = len(args) + len(outs)

    def moved(*refs):
        whole, own = list(refs[:count]), refs[count : count + len(scratch)]
        spare, sems = refs[count + len(scratch) : -1], refs[-1]
        copies, after = [], []
        for at, (i, ref) in enumerate(zip(fetch, spare)):
            copies.append(pltpu.make_async_copy(whole[i], ref, sems.at[at]))
            whole[i] = ref
        for at, (i, ref) in enumerate(zip(push, spare[len(fetch) :])):
            i += len(args)
            after.append(pltpu.make_async_copy(ref, whole[i], sems.at[len(fetch) + at]))
            whole[i] = ref
        for copy in copies:
            copy.start()
        for copy in copies:
            copy.wait()
        started = []

        def start(i):
            started.append(push.index(i))
            after[started[-1]].start()

        if early:
            kernel(*whole, *own, start=start)
        else:
            kernel(*whole, *own)
        for i, copy in enumerate(after):
            if i not in started:
                copy.start()
        for copy in after:
            copy.wait()

    def spec(i, which):
        return pl.BlockSpec(memory_space=pltpu.HBM if i in which else pltpu.VMEM)

    return pl.pallas_call(
        moved if near else kernel,
        out_shape=outs,
        in_specs=[pl.BlockSpec(memory_space=pltpu.SMEM)] * smem
        + [spec(i, range(len(args)) if far else fetch) for i in range(smem, len(args))],
        out_specs=[spec(i, push) for i in range(len(outs))],
        scratch_shapes=list(scratch)
        + near
        + ([pltpu.SemaphoreType.DMA((len(near),))] if near else []),
        compiler_params=pltpu.CompilerParams(vmem_limit_bytes=limit or held + (room << 20)),
        cost_estimate=cost(),
        name=name,
    )(*args)


def when(condition):
    if isinstance(condition, bool):
        return lambda run: run() if condition else None
    return pl.when(condition)


def shape(*dims, dtype=f32):
    return jax.ShapeDtypeStruct(dims, dtype)


def by_case(value, count, run):
    for i in range(count):
        pl.when(value == i)(functools.partial(run, i))


def pack_qkv_kernel(rows, members, ids, *refs):
    count = (len(refs) - members - 4) // 2 + 1
    sources, pieces = refs[:count], refs[count : count + members]
    wo, x_out, cot_out = refs[count + members : count + members + 3]
    held, sems = refs[count + members + 3 : -1], refs[-1]
    part = x_out.shape[0]
    at = pl.multiple_of(ids[OWN] * part, 8)
    copies = [
        pltpu.make_async_copy(source.at[pl.ds(at, part)], target, sems.at[i])
        for i, (source, target) in enumerate(zip(sources[:2], (x_out, cot_out)))
    ]
    copies += [
        pltpu.make_async_copy(source, target, sems.at[2 + i])
        for i, (source, target) in enumerate(zip(sources[2:], held))
    ]
    for copy in copies:
        copy.start()
    for copy in copies:
        copy.wait()
    w_ref, out_ref, bias_ref, b_ref, proj_ref, up_ref = held[:6]
    width = w_ref.shape[1] // 3
    lanes = width // members
    heads = bias_ref.shape[0] // members
    quarter = rows // members
    for piece in pieces:
        piece[quarter:, :] = jnp.zeros((8, 3 * lanes), f32)
        piece[quarter : quarter + 1, : b_ref.shape[0]] = b_ref[...].reshape(1, -1)
        for i, ref in enumerate(held[6:]):
            row, lane = (4, i) if i < 5 else (5, 0)
            piece[quarter + row : quarter + row + 1, lane * rows : (lane + 1) * rows] = ref[
                ...
            ].reshape(1, -1)
        piece[quarter + 5 : quarter + 6, rows : rows + up_ref.shape[0]] = up_ref[...].reshape(1, -1)
        per = 3 * lanes // HEAD_DIM
        for i in range(proj_ref.shape[0]):
            row, lane = quarter + 6 + i // per, HEAD_DIM * (i % per)
            piece[row : row + 1, lane : lane + HEAD_DIM] = proj_ref[i : i + 1]

    def own(f):
        first = quarter * f
        wo[...] = out_ref[first : first + quarter]

        def head(t):
            for k, piece in enumerate(pieces):
                to = t ^ k
                for p in range(3):
                    at = width * p + lanes * to
                    piece[:quarter, lanes * p : lanes * (p + 1)] = w_ref[
                        first : first + quarter, at : at + lanes
                    ]
                piece[quarter + 1 : quarter + 1 + heads, : bias_ref.shape[1]] = bias_ref[
                    heads * to : heads * (to + 1)
                ]

        by_case(ids[HEAD], members, head)

    by_case(ids[OWN], members, own)


def pack_ff_kernel(members, down, ids, up_ref, down_ref, out):
    rows = up_ref.shape[0]
    blocks = up_ref.shape[1] // (members * down)

    def case(i):
        for w in range(blocks):
            at = (w * members + i) * down
            out[:rows, down * w : down * (w + 1)] = up_ref[:, at : at + down]
        out[rows : rows + down, :] = down_ref[down * i : down * (i + 1)]

    by_case(ids[OWN], members, case)


def plane_place(ids, members, few, i):
    if not few:
        zh, rest = divmod(i, 2 * members)
        return zh, rest // members, rest % members
    other, j = divmod(i, members)
    member = lax.bitwise_xor(ids[MEMBER], j)
    return 0, lax.rem(member, 2), 2 * lax.div(member, 2) + lax.bitwise_xor(ids[CORE], other)


def qkv_kernel(rows, members, spans, few, ids, *refs):
    x_parts, refs = refs[:members], refs[members:]
    w_out, x_out, pq_out, kv_out, key_out, proj_out, bias_out, vec_out, extra, held, directions = refs[-11:]
    slabs = refs[:-11]
    slabs = list(slabs) if few else [slabs[0].at[i] for i in range(slabs[0].shape[0])]
    width = x_out.shape[1]
    blocks = extra.shape[0]
    full = w_out.shape[1]
    lanes = full // 3
    heads = lanes // HEAD_DIM
    quarter = rows // members
    part = x_parts[0].shape[0]
    for k, ref in enumerate(x_parts):
        at = pl.multiple_of(lax.bitwise_xor(ids[HEAD], k) * part, 8)
        x_out[pl.ds(at, part), :] = ref[...]
    for i, slab in enumerate(slabs):
        zh, x, f = plane_place(ids, members, few, i)
        for k in range(members):
            w = 2 * (members * zh + lax.bitwise_xor(ids[HEAD], k)) + x
            if i < 2 if few else f == 0:
                extra[w] = slab[k, quarter:]
            if quarter % 8 == 0:
                at = pl.multiple_of(w * rows + f * quarter, 8)
                w_out[pl.ds(at, quarter), :] = slab[k, :quarter]
            else:
                held[w * members + f] = slab[k, :quarter]
    if quarter % 8:
        for i in range(held.shape[0]):
            w_out[quarter * i : quarter * (i + 1)] = held[i]

    share = FEATURES // members
    per = full // HEAD_DIM
    for i, slab in enumerate(slabs):
        zh, x, f = plane_place(ids, members, few, i)
        if few or (zh, x) == (0, 0):
            for r in range(share):
                at, lane = quarter + 6 + r // per, HEAD_DIM * (r % per)
                directions[share * f + r] = slab[0, at : at + 1, lane : lane + HEAD_DIM]
    for r in range(FEATURES):
        proj_out[r : r + 1, :] = directions[r]
    bias_out[...] = jnp.zeros_like(bias_out)
    b_row = []
    for w in range(blocks):
        b_row.append(extra[w, 0:1, : spans[0]])
        count = spans[1]
        bias_out[:heads, count * w : count * (w + 1)] = extra[w, 1 : 1 + heads, :count]
        for i in range(6):
            row, lane = (4, i) if i < 5 else (5, 0)
            vec_out[1 + i : 2 + i, rows * w : rows * (w + 1)] = extra[
                w, row : row + 1, lane * rows : (lane + 1) * rows
            ]
    vec_out[7:8] = jnp.zeros((1, width), f32)
    b_row = jnp.concatenate(b_row, axis=1)

    def unit(g):
        count = spans[2]
        for w in range(blocks):
            vec_out[0:1, count * w : count * (w + 1)] = extra[
                w, 5:6, rows + count * g : rows + count * (g + 1)
            ]

    by_case(ids[MEMBER], members, unit)
    qkv = dot3(x_out[...], w_out[...], 1, 0)
    scale = HEAD_DIM**-0.25
    proj = split(proj_out[...])

    def head(t):
        bias = [b_row[:, width * p + lanes * t : width * p + lanes * (t + 1)] for p in range(3)]
        turned = (qkv + jnp.concatenate(bias, axis=1)).T
        for h in range(heads):
            lo, hi = HEAD_DIM * h, HEAD_DIM * (h + 1)
            q = turned[lo:hi] * scale
            k = turned[lanes + lo : lanes + hi] * scale
            pq_out[lo:hi] = jnp.exp(dot3s(proj, split(q), 1, 0))
            pk = dot3s(proj, split(k), 1, 0) - 0.5 * jnp.sum(k * k, axis=0, keepdims=True)
            kv_out[128 * h : 128 * h + 64] = jnp.exp(pk)
            kv_out[128 * h + 64 : 128 * h + 128] = turned[2 * lanes + lo : 2 * lanes + hi]
            key_out[lo:hi] = k

    by_case(ids[HEAD], members, head)


def rolled_rows(table, row):
    wide = jnp.broadcast_to(row, (8, row.shape[1]))
    return pltpu.roll(wide, 0, 1, stride=1, stride_axis=0)


def make_tables(tables, bias_ref, heads):
    length = bias_ref.shape[1]
    for h in range(heads):
        rows = rolled_rows(None, jnp.exp(bias_ref[h : h + 1]))
        tables[0, 8 * h : 8 * h + 8] = rows
        tables[1, 8 * h : 8 * h + 8] = pltpu.roll(rows, length - 64, 1)


def factor_tile(windows):
    first = lax.broadcasted_iota(jnp.int32, (8, 128), 1) < 64
    pairs = {}
    for g in range(8):
        for d in range(-3, 3):
            low = pltpu.roll(windows[d + 3], (8 * g + 64) % 128, 1)
            high = windows[d + 4] if g == 0 else pltpu.roll(windows[d + 4], 8 * g, 1)
            pairs[d, g] = jnp.where(first, low, high)
    rows = []
    for z in range(4):
        for g in range(8):
            rows.append(jnp.concatenate([pairs[-z, g], pairs[2 - z, g]], axis=1))
    return jnp.concatenate(rows, axis=0)


def window_sums(pairs):
    first = lax.broadcasted_iota(jnp.int32, (8, 128), 1) < 64
    sums = [jnp.zeros((8, 128), f32) for _ in range(7)]
    for g in range(8):
        for d in range(-3, 3):
            total = None
            for z in range(4):
                for p in range(2):
                    if 2 * p - z == d:
                        term = pairs[64 * z + 8 * g : 64 * z + 8 * g + 8, 128 * p : 128 * p + 128]
                        total = term if total is None else total + term
            low = pltpu.roll(jnp.where(first, total, 0.0), 64 - 8 * g, 1)
            high = jnp.where(first, 0.0, total)
            sums[d + 3] = sums[d + 3] + low
            sums[d + 4] = sums[d + 4] + (high if g == 0 else pltpu.roll(high, 128 - 8 * g, 1))
    return sums


def window_start(ids, members, groups, seg, length, n):
    if groups == 1:
        other, j = n // members, n % members
        member = lax.bitwise_xor(ids[MEMBER], j)
        zh, x = ids[PLACE] * 0, lax.rem(member, 2)
        f = 2 * lax.div(member, 2) + lax.bitwise_xor(ids[CORE], other)
    else:
        zh, x, f = n // (2 * members), lax.rem(lax.div(n, members), 2), lax.rem(n, members)
    own = ids[PLACE]
    away = 8 * members * (lax.div(own, 2 * members) - zh)
    away += members * (lax.rem(lax.div(own, members), 2) - x) + ids[OWN] - f
    start = away + length // (2 * seg) - 1
    odd = lax.rem(start, 2)
    return start - odd, odd


def window_at(start, d):
    return pl.multiple_of(start * 64 + 512 * d, 128)


def attention_kernel(groups, blocks, ids, *refs, start=None):
    nkv = blocks if groups == 1 else 1
    kv_refs = refs[:nkv]
    pq_ref, bias_ref = refs[nkv : nkv + 2]
    kcat, vcat, att_out, den_out = refs[nkv + 2 : nkv + 6]
    parts = refs[nkv + 6 : nkv + 10]
    tables, qcat, out_rows = refs[nkv + 10 :]
    heads = pq_ref.shape[0] // 64
    queries = pq_ref.shape[1]
    step = pl.program_id(0) if groups > 1 else 0

    @when(step == 0)
    def _():
        make_tables(tables, bias_ref, heads)
        for h in range(heads):
            high, low = split(pq_ref[64 * h : 64 * h + 64])
            qcat[h, 0:64] = high
            qcat[h, 64:128] = high
            qcat[h, 128:192] = low
        att_out[...] = jnp.zeros_like(att_out)
        den_out[...] = jnp.zeros_like(den_out)

    for n in range(blocks):
        block = kv_refs[n] if groups == 1 else kv_refs[0].at[n]
        for h in range(heads):
            for part, cat in ((0, kcat), (64, vcat)):
                high, low = split(block[128 * h + part : 128 * h + part + 64])
                cat[n, h, 0:64] = high
                cat[n, h, 64:128] = low
                cat[n, h, 128:192] = high

    if start is not None:
        start(0)
        start(1)

    def advance(n, carry):
        first, odd = window_start(ids, 4, groups, 64, bias_ref.shape[1], step * blocks + n)
        for h in range(heads):
            scores = dot(kcat[n, h], qcat[h], 0, 0)
            rows = slice(8 * h, 8 * h + 8)
            windows = [
                tables[odd, rows, pl.ds(window_at(first, d), 128)] for d in range(-3, 4)
            ]
            weight = scores * factor_tile(windows)
            high, low = split(weight)
            both = dot(vcat[n, h, 0:128], high, 1, 0)
            more = dot(vcat[n, h, 0:64], low, 1, 0)
            att_out[64 * h : 64 * h + 64] += both[0:64] + both[64:128] + more
            den_out[h : h + 1] += jnp.sum(weight, axis=0, keepdims=True)
        return carry

    lax.fori_loop(0, blocks, advance, 0)

    @when(step == groups - 1)
    def _():
        for h in range(heads):
            att_out[64 * h : 64 * h + 64] = att_out[64 * h : 64 * h + 64] / den_out[h : h + 1]
        out_rows[...] = att_out[...].T
        rows = queries // 4
        for k in range(4):
            first = pl.multiple_of(lax.bitwise_xor(ids[HEAD], k) * rows, 8)
            parts[k][...] = out_rows[pl.ds(first, rows), :]


def attention(ids, kv, pq, window):
    stacked = not isinstance(kv, list)
    count = kv.shape[0] if stacked else len(kv)
    blocks = 8 if stacked else count
    groups = count // blocks
    queries = pq.shape[1]
    heads = pq.shape[0] // 64
    cat = shape(count, heads, 192, queries, dtype=bf16)
    rows = shape(queries // 4, heads * 64)
    outs = [cat, cat, shape(heads * 64, queries), shape(8, queries)] + [rows] * 4
    scratch = [
        pltpu.VMEM((2, 8 * heads, window.shape[1]), f32),
        pltpu.VMEM((heads, 192, queries), bf16),
        pltpu.VMEM((queries, heads * 64), f32),
    ]
    kernel = functools.partial(attention_kernel, groups, blocks)
    if not stacked:
        return call(kernel, outs, [ids, *kv, pq, window], "attention", scratch, 1, deep=True, early=True)
    whole = lambda a: pl.BlockSpec(a.shape, lambda g, nd=len(a.shape): (0,) * nd)
    smem = pl.BlockSpec(memory_space=pltpu.SMEM)
    kv_spec = pl.BlockSpec((blocks,) + kv.shape[1:], lambda g: (g, 0, 0))
    cat_spec = pl.BlockSpec((blocks, heads, 192, queries), lambda g: (g, 0, 0, 0))
    return pl.pallas_call(
        kernel,
        grid=(groups,),
        out_shape=outs,
        in_specs=[smem, kv_spec, whole(pq), whole(window)],
        out_specs=[cat_spec, cat_spec] + [whole(a) for a in outs[2:]],
        scratch_shapes=scratch,
        compiler_params=pltpu.CompilerParams(vmem_limit_bytes=52 << 20),
        name="attention",
    )(ids, kv, pq, window)


def attention_back_kernel(groups, blocks, ids, *refs):
    kcat, vcat, pq_ref, bias_ref, att_ref, den_ref = refs[:6]
    grads = refs[6:10]
    if groups == 1:
        own, other, dpq_out, dbias_out, tables, qcat, gcat, gden, diag, grad_rows, dkv = refs[10:]
    else:
        dkv, dpq_out, dbias_out, tables, qcat, gcat, gden, diag, grad_rows = refs[10:]
    heads = pq_ref.shape[0] // 64
    queries = pq_ref.shape[1]
    step = pl.program_id(0) if groups > 1 else 0

    @when(step == 0)
    def _():
        rows = queries // 4
        for k in range(4):
            first = pl.multiple_of(lax.bitwise_xor(ids[HEAD], k) * rows, 8)
            grad_rows[pl.ds(first, rows), :] = grads[k][...]
        make_tables(tables, bias_ref, heads)
        d_att = grad_rows[...].T
        gden[...] = jnp.zeros_like(gden)
        for h in range(heads):
            lo, hi = 64 * h, 64 * h + 64
            for value, cat in ((pq_ref[lo:hi], qcat), (d_att[lo:hi] / den_ref[h : h + 1], gcat)):
                high, low = split(value)
                cat[h, 0:64] = high
                cat[h, 64:128] = high
                cat[h, 128:192] = low
            gden[h : h + 1] = -(
                jnp.sum(d_att[lo:hi] * att_ref[lo:hi], axis=0, keepdims=True) / den_ref[h : h + 1]
            )
        dpq_out[...] = jnp.zeros_like(dpq_out)
        diag[...] = jnp.zeros_like(diag)

    def advance(n, carry):
        start, odd = window_start(ids, 4, groups, 64, bias_ref.shape[1], step * blocks + n)
        for h in range(heads):
            scores = dot(kcat[n, h], qcat[h], 0, 0)
            rows = slice(8 * h, 8 * h + 8)
            factor = factor_tile(
                [tables[odd, rows, pl.ds(window_at(start, d), 128)] for d in range(-3, 4)]
            )
            d_weight = dot(vcat[n, h], gcat[h], 0, 0) + gden[h : h + 1]
            w_high, w_low = split(scores * factor)
            e_high, e_low = split(d_weight * factor)
            pairs = d_weight * scores
            both = dot(gcat[h, 64:192], w_high, 1, 1)
            dv = both[0:64] + both[64:128] + dot(gcat[h, 0:64], w_low, 1, 1)
            both = dot(qcat[h, 64:192], e_high, 1, 1)
            dk = both[0:64] + both[64:128] + dot(qcat[h, 0:64], e_low, 1, 1)
            both = dot(kcat[n, h, 0:128], e_high, 1, 0)
            dq = both[0:64] + both[64:128] + dot(kcat[n, h, 0:64], e_low, 1, 0)
            dpq_out[64 * h : 64 * h + 64] += dq
            dkv[n, 128 * h : 128 * h + 64] = dk
            dkv[n, 128 * h + 64 : 128 * h + 128] = dv
            for i, total in enumerate(window_sums(pairs)):
                diag[odd, rows, pl.ds(window_at(start, i - 3), 128)] += total
        return carry

    lax.fori_loop(0, blocks, advance, 0)

    @when(step == groups - 1)
    def _():
        if groups == 1:
            own[...] = dkv[: blocks // 2]
            other[...] = dkv[blocks // 2 :]
        length = diag.shape[2]
        dbias_out[...] = jnp.zeros_like(dbias_out)
        for h in range(heads):
            both = diag[0, 8 * h : 8 * h + 8] + pltpu.roll(diag[1, 8 * h : 8 * h + 8], 64, 1)
            total = both[0:1]
            for s in range(1, 8):
                total = total + pltpu.roll(both[s : s + 1], length - s, 1)
            dbias_out[h : h + 1] = total * jnp.exp(bias_ref[h : h + 1])


def attention_back(ids, kcat, vcat, pq, window, att, den, grads, stacked):
    count, heads, _, queries = kcat.shape
    blocks = 8 if stacked else count
    groups = count // blocks
    outs = [shape(heads * 64, queries), shape(8, window.shape[1])]
    args = [ids, kcat, vcat, pq, window, att, den] + list(grads)
    scratch = [
        pltpu.VMEM((2, 8 * heads, window.shape[1]), f32),
        pltpu.VMEM((heads, 192, queries), bf16),
        pltpu.VMEM((heads, 192, queries), bf16),
        pltpu.VMEM((8, queries), f32),
        pltpu.VMEM((2, 8 * heads, window.shape[1]), f32),
        pltpu.VMEM((queries, heads * 64), f32),
    ]
    kernel = functools.partial(attention_back_kernel, groups, blocks)
    if not stacked:
        half = shape(count // 2, heads * 128, queries)
        scratch.append(pltpu.VMEM((count, heads * 128, queries), f32))
        return call(kernel, [half, half] + outs, args, "attention_back", scratch, 1, deep=True)
    whole = lambda a: pl.BlockSpec(a.shape, lambda g, nd=len(a.shape): (0,) * nd)
    smem = pl.BlockSpec(memory_space=pltpu.SMEM)
    cat_spec = pl.BlockSpec((blocks, heads, 192, queries), lambda g: (g, 0, 0, 0))
    dkv_spec = pl.BlockSpec((blocks, heads * 128, queries), lambda g: (g, 0, 0))
    return pl.pallas_call(
        kernel,
        grid=(groups,),
        out_shape=[shape(count, heads * 128, queries)] + outs,
        in_specs=[smem, cat_spec, cat_spec] + [whole(a) for a in args[3:]],
        out_specs=[dkv_spec] + [whole(a) for a in outs],
        scratch_shapes=scratch,
        compiler_params=pltpu.CompilerParams(vmem_limit_bytes=52 << 20),
        name="attention_back",
    )(*args)


def normed(value):
    mean = jnp.mean(value, axis=1, keepdims=True)
    centered = value - mean
    var = jnp.mean(centered * centered, axis=1, keepdims=True)
    inverse = lax.rsqrt(var + EPS)
    return centered * inverse, inverse


def norm_back(upstream, n, inverse, gain):
    scaled = gain * upstream
    mean = jnp.mean(scaled, axis=1, keepdims=True)
    slope = jnp.mean(scaled * n, axis=1, keepdims=True)
    return (scaled - mean - n * slope) * inverse


def colsum(value):
    return jnp.sum(value, axis=0, keepdims=True)


def weights_out_kernel(rows, ids, *refs):
    out = refs[-1]
    members, quarter, _ = refs[0].shape
    for i, ref in enumerate(refs[:-1]):
        other, j = divmod(i, members)
        place = lax.bitwise_xor(ids[MEMBER], j)
        core = lax.bitwise_xor(ids[CORE], other)
        f = 2 * lax.div(place, 2) + core
        for k in range(members):
            w = 2 * lax.bitwise_xor(ids[HEAD], k) + lax.rem(place, 2)
            out[pl.ds(pl.multiple_of(rows * w + quarter * f, 8), quarter), :] = ref[k]


def norm_one_kernel(ids, a0, a1, a2, a3, x_ref, w_ref, vec_ref, *refs):
    first_out, n_out, inverse_out, att_out = refs
    lanes = a0.shape[1]

    def head(t):
        for k, ref in enumerate((a0, a1, a2, a3)):
            at = lanes * (t ^ k)
            att_out[:, at : at + lanes] = ref[...]

    by_case(ids[HEAD], 4, head)
    projected = dot3(att_out[...], w_ref[...], 1, 0)
    n, inverse = normed(x_ref[...] + (projected + vec_ref[1:2]))
    first_out[...] = n * vec_ref[2:3] + vec_ref[3:4]
    n_out[...] = n
    inverse_out[...] = jnp.broadcast_to(inverse, inverse_out.shape)


def norm_two_kernel(p0, p1, p2, p3, first_ref, cot_ref, vec_ref, rows_out, dz_out, grads_out):
    value = first_ref[...] + ((p0[...] + p1[...]) + (p2[...] + p3[...]) + vec_ref[4:5])
    n, inverse = normed(value)
    rows_out[...] = n * vec_ref[5:6] + vec_ref[6:7]
    up = cot_ref[...]
    dz = norm_back(up, n, inverse, vec_ref[5:6])
    dz_out[...] = dz
    grads_out[...] = jnp.zeros_like(grads_out)
    grads_out[0:1] = colsum(up * n)
    grads_out[1:2] = colsum(up)
    grads_out[2:3] = colsum(dz)


def norm_one_back_kernel(ids, p0, p1, p2, p3, dz_ref, n_ref, inverse_ref, w_ref, vec_ref, *refs):
    dz_out, grads_out = refs[:2]
    parts = refs[2:6]
    up = dz_ref[...] + ((p0[...] + p1[...]) + (p2[...] + p3[...]))
    n = n_ref[...]
    dz = norm_back(up, n, inverse_ref[:, 0:1], vec_ref[2:3])
    dz_out[...] = dz
    grads_out[...] = jnp.zeros_like(grads_out)
    grads_out[0:1] = colsum(up * n)
    grads_out[1:2] = colsum(up)
    grads_out[2:3] = colsum(dz)
    d_att = dot3(dz, w_ref[...], 1, 1)
    lanes = parts[0].shape[1]

    def case(i):
        for k in range(4):
            at = lanes * (i ^ k)
            parts[k][...] = d_att[:, at : at + lanes]

    by_case(ids[HEAD], 4, case)


def stack_kernel(*refs):
    for i, ref in enumerate(refs[:-1]):
        refs[-1][i] = ref[...]


def stack_rows(target, refs):
    rows = refs[0].shape[0]
    for k, ref in enumerate(refs):
        target[rows * k : rows * (k + 1), :] = ref[...]


def halves_of(slab, target, first, count):
    for w in range(slab.shape[0]):
        target[count * w : count * (w + 1)] = slab[w, first : first + count]


def forward_kernel(rows_up, rows_down, f0, f1, f2, f3, slab, vec_ref, *refs):
    pre_out, first_out = refs[:2]
    parts, (up, down) = refs[2:6], refs[6:]
    halves_of(slab, up, 0, rows_up)
    halves_of(slab, down, rows_up, rows_down)
    stack_rows(first_out, (f0, f1, f2, f3))
    pre = dot3(first_out[...], up[...], 1, 0) + vec_ref[0:1]
    pre_out[...] = pre
    hidden = 0.5 * pre * (1.0 + lax.erf(pre * (0.5**0.5)))
    branch = dot3(hidden, down[...], 1, 0)
    rows = f0.shape[0]
    for k in range(4):
        parts[k][...] = branch[rows * k : rows * (k + 1)]


def backward_kernel(rows_up, rows_down, z0, z1, z2, z3, pre_ref, slab, *refs):
    dz_out, d_pre_out = refs[:2]
    parts, (up, down) = refs[2:6], refs[6:]
    halves_of(slab, up, 0, rows_up)
    halves_of(slab, down, rows_up, rows_down)
    stack_rows(dz_out, (z0, z1, z2, z3))
    d_hidden = dot3(dz_out[...], down[...], 1, 1)
    pre = pre_ref[...]
    density = jnp.exp(-0.5 * pre * pre) * ((2.0 * jnp.pi) ** -0.5)
    d_pre = d_hidden * (0.5 * (1.0 + lax.erf(pre * (0.5**0.5))) + pre * density)
    d_pre_out[...] = d_pre
    d_first = dot3(d_pre, up[...], 1, 1)
    rows = z0.shape[0]
    for k in range(4):
        parts[k][...] = d_first[rows * k : rows * (k + 1)]


def ff_weights_kernel(rows_up, rows_down, first_ref, d_pre_ref, pre_ref, dz_ref, grads_ref, out):
    pre = pre_ref[...]
    hidden = 0.5 * pre * (1.0 + lax.erf(pre * (0.5**0.5)))
    d_pre = d_pre_ref[...]
    blocks = out.shape[0]
    base = rows_up + rows_down
    out[:, base:, :] = jnp.zeros((blocks, 8, out.shape[2]), f32)
    d_b_up = colsum(d_pre)
    up = dot3(first_ref[...], d_pre, 0, 0)
    down = dot3(hidden, dz_ref[...], 0, 0)
    for w in range(blocks):
        out[w, :rows_up, :] = up[rows_up * w : rows_up * (w + 1)]
        out[w, rows_up:base, :] = down[rows_down * w : rows_down * (w + 1)]
        out[w, base : base + 1, :rows_down] = d_b_up[:, rows_down * w : rows_down * (w + 1)]
        for i in range(3):
            out[w, base + 1 + i : base + 2 + i, :rows_up] = grads_ref[
                i : i + 1, rows_up * w : rows_up * (w + 1)
            ]


def shares(held, ids, outs):
    if len(outs) == 1:
        outs[0][...] = held[...]
        return
    members = held.shape[1]
    for other, out in enumerate(outs):
        core = lax.bitwise_xor(ids[CORE], other)
        for j in range(members):
            place = lax.bitwise_xor(ids[MEMBER], j)
            at = lax.rem(place, 2) * members + 2 * lax.div(place, 2) + core
            out[j] = held[at]


def out_weights_kernel(ids, att_ref, dz_ref, *refs):
    outs, held = refs[:-1], refs[-1]
    places, members, quarter, _ = held.shape
    value = dot3(att_ref[...], dz_ref[...], 0, 0)
    for place in range(places):
        zh, rest = divmod(place, 2 * members)
        x, f = divmod(rest, members)
        for z in range(members):
            at = ((2 * (members * zh + z) + x) * members + f) * quarter
            held[place, z] = value[at : at + quarter]
    shares(held, ids, outs)


def sum_cores_kernel(own, came, *outs):
    for j, out in enumerate(outs):
        out[...] = own[j] + came[j]


def qkv_back_kernel(ids, d0, d1, d2, d3, pq_ref, dpq_ref, kv_ref, key_ref, proj_ref, w_ref, *refs):
    d_qkv_out = refs[0]
    parts = refs[1:5]
    turned, rows_held = refs[5:]
    heads = pq_ref.shape[0] // 64
    width = heads * 64
    scale = HEAD_DIM**-0.25
    proj = split(proj_ref[...])
    dkv = (d0[...] + d1[...]) + (d2[...] + d3[...])
    for h in range(heads):
        lo, hi = 64 * h, 64 * h + 64
        turned[lo:hi] = scale * dot3s(proj, split(dpq_ref[lo:hi] * pq_ref[lo:hi]), 0, 0)
        pk = dkv[128 * h : 128 * h + 64] * kv_ref[128 * h : 128 * h + 64]
        turned[width + lo : width + hi] = scale * (
            dot3s(proj, split(pk), 0, 0) - key_ref[lo:hi] * colsum(pk)
        )
        turned[2 * width + lo : 2 * width + hi] = dkv[128 * h + 64 : 128 * h + 128]
    d_qkv = turned[...].T
    d_qkv_out[...] = d_qkv
    rows_held[...] = dot3(d_qkv, w_ref[...], 1, 1)
    rows = parts[0].shape[0]
    for k in range(4):
        first = pl.multiple_of(lax.bitwise_xor(ids[HEAD], k) * rows, 8)
        parts[k][...] = rows_held[pl.ds(first, rows), :]


def qkv_weights_kernel(rows, span, ids, x_ref, d_ref, dbias_ref, grads_ref, *refs):
    outs, held = refs[:-1], refs[-1]
    d_qkv = d_ref[...]
    places, members, _, full = held.shape
    quarter = rows // members
    held[:, :, quarter:, :] = jnp.zeros((places, members, 8, full), f32)
    d_b = colsum(d_qkv)
    weights = dot3(x_ref[...], d_qkv, 0, 0)
    for place in range(places):
        zh, rest = divmod(place, 2 * members)
        x, f = divmod(rest, members)
        for z in range(members):
            w = 2 * (members * zh + z) + x
            at = (w * members + f) * quarter
            held[place, z, :quarter] = weights[at : at + quarter]
            held[place, z, quarter : quarter + 1] = d_b
            for i in range(3):
                held[place, z, quarter + 1 : quarter + 2, rows * i : rows * (i + 1)] = grads_ref[
                    i : i + 1, rows * w : rows * (w + 1)
                ]
            held[place, z, quarter + 2 : quarter + 5, :span] = dbias_ref[
                0:3, span * w : span * (w + 1)
            ]
    shares(held, ids, outs)


def merge_kernel(rows, held, wo_ref, out, b_out, bias_out, vec_out):
    members = held.shape[0]
    refs = [held.at[t] for t in range(members)]
    r0, r1, r2, r3 = refs
    lanes = held.shape[2] // 3
    width = lanes * members
    span = bias_out.shape[1]
    quarter = rows // members
    total = (r0[quarter + 1 : quarter + 2] + r1[quarter + 1 : quarter + 2]) + (
        r2[quarter + 1 : quarter + 2] + r3[quarter + 1 : quarter + 2]
    )
    vec_out[...] = jnp.zeros_like(vec_out)
    for i in range(3):
        vec_out[i : i + 1] = total[:, rows * i : rows * (i + 1)]
    out[:, 3 * width :] = (wo_ref[0] + wo_ref[1]) + (wo_ref[2] + wo_ref[3])

    for t, ref in enumerate(refs):
        for p in range(3):
            at = width * p + lanes * t
            out[:, at : at + lanes] = ref[:quarter, lanes * p : lanes * (p + 1)]
            b_out[:, at : at + lanes] = ref[quarter : quarter + 1, lanes * p : lanes * (p + 1)]
        bias_out[3 * t : 3 * t + 3] = ref[quarter + 2 : quarter + 5, :span]


def place_weights_kernel(ids, r0, r1, r2, r3, w_out, wo_out):
    quarter = r0.shape[0]
    full = w_out.shape[1]

    def own(f):
        for k, ref in enumerate((r0, r1, r2, r3)):
            at = quarter * (f ^ k)
            w_out[at : at + quarter] = ref[:, :full]
            wo_out[at : at + quarter] = ref[:, full:]

    by_case(ids[OWN], 4, own)


def sum_kernel(*refs):
    total = refs[0][...]
    for ref in refs[1:-1]:
        total = total + ref[...]
    refs[-1][...] = total


def sum_four_kernel(p0, p1, p2, p3, dz_ref, out):
    out[...] = dz_ref[...] + ((p0[...] + p1[...]) + (p2[...] + p3[...]))


def place_kernel(ids, r0, r1, r2, r3, out):
    rows = r0.shape[0]
    for k, ref in enumerate((r0, r1, r2, r3)):
        out[pl.ds(pl.multiple_of(lax.bitwise_xor(ids[OWN], k) * rows, 8), rows), :] = ref[...]


def place_ff_kernel(rows, down, parts, up_out, down_out, b_out, vec_out):
    members = parts.shape[0]
    base = rows + down
    vec_out[...] = jnp.zeros_like(vec_out)
    total = parts[0, base + 1 : base + 4, :rows]
    for f in range(1, members):
        total = total + parts[f, base + 1 : base + 4, :rows]
    vec_out[0:3] = total
    for f in range(members):
        for w in range(up_out.shape[1] // (members * down)):
            at = (w * members + f) * down
            up_out[:, at : at + down] = parts[f, :rows, down * w : down * (w + 1)]
        down_out[down * f : down * (f + 1)] = parts[f, rows:base]
        b_out[:, down * f : down * (f + 1)] = parts[f, base : base + 1, :down]


def exchange(value, axes, count, k):
    return lax.ppermute(value, axes, [(i, i ^ k) for i in range(count)])


def swap(value):
    return lax.ppermute(value, ("core", "x"), [(0, 0), (1, 2), (2, 1), (3, 3)])


def place(ids, values, name):
    return call(
        place_kernel,
        [shape(len(values) * values[0].shape[0], values[0].shape[1])],
        [ids, *values],
        name,
        smem=1,
    )[0]


def gather(value, axes, count):
    return [value] + [exchange(value, axes, count, k) for k in range(1, count)]


def scatter(parts, axes):
    return [parts[0]] + [exchange(parts[k], axes, len(parts), k) for k in range(1, len(parts))]


def body(
    ys,
    zhs,
    inputs,
    cotangent,
    random_proj,
    position_bias,
    w_qkv,
    b_qkv,
    w_out,
    b_out,
    ln1_gain,
    ln1_bias,
    w_up,
    b_up,
    w_down,
    b_down,
    ln2_gain,
    ln2_bias,
):
    members = 2 * ys
    blocks = 2 * zhs * members
    places = 2 * zhs * members
    few = zhs == 1
    core = lax.axis_index("core")
    x_at, y_at = lax.axis_index("x"), lax.axis_index("y")
    zh_at, zl_at = lax.axis_index("zh"), lax.axis_index("zl")
    feat = 2 * y_at + core
    group = 2 * y_at + x_at
    wide = 2 * (members * zh_at + zl_at) + x_at
    place_at = (2 * zh_at + x_at) * members + feat
    ids = jnp.stack([core, group, feat, zl_at, wide, place_at]).astype(jnp.int32)
    queries, width = inputs.shape
    rows = queries // members
    shard = w_qkv.shape[0]
    quarter = shard // members
    down = w_down.shape[0] // members
    heads = HEADS // members
    lanes = heads * HEAD_DIM
    span = position_bias.shape[1]
    full = 3 * lanes
    length = queries * blocks
    row_shape = shape(rows, width)

    packed = [w_qkv, w_out, position_bias, b_qkv, random_proj.T]
    packed += [b_up, b_out, ln1_gain, ln1_bias, b_down, ln2_gain, ln2_bias]
    got = call(
        functools.partial(pack_qkv_kernel, shard, members),
        [shape(quarter + 8, full)] * members + [shape(quarter, width), row_shape, row_shape],
        [ids, inputs, cotangent] + packed,
        "pack_qkv",
        scratch=[pltpu.VMEM(a.shape, f32) for a in packed]
        + [pltpu.SemaphoreType.DMA((len(packed) + 2,))],
        smem=1,
        limit=60 << 20,
        far=True,
    )
    wo_piece, x_own, cot_rows = got[members:]
    pieces = scatter(got[:members], "zl")
    x_parts = gather(x_own, "zl", members)

    pack_ids, _ = lax.optimization_barrier((ids, x_own))
    (ff_slab,) = call(
        functools.partial(pack_ff_kernel, members, down),
        [shape(shard + down, width)],
        [pack_ids, w_up, w_down],
        "pack_ff",
        smem=1,
    )
    ff_slab, wo_piece, pieces, x_parts = lax.optimization_barrier(
        (swap(ff_slab), wo_piece, pieces, x_parts)
    )
    wo_parts = gather(wo_piece, "zl", members)
    ff_slab, wo_parts = lax.optimization_barrier((ff_slab, wo_parts))
    ff_slab = lax.all_gather(ff_slab, LINES, axis=0)
    slab = jnp.stack(pieces)
    if few:
        slabs = gather(slab, GROUP, members)
        slabs, wo_parts = lax.optimization_barrier((slabs, wo_parts))
        (wo_parts,) = call(
            stack_kernel, [shape(members, quarter, width)], wo_parts, "stack_out"
        )
        wo_own = gather(wo_parts, GROUP, members)
        slabs = slabs + [exchange(v, "core", 2, 1) for v in slabs]
    else:
        slabs = [lax.all_gather(slab, PLANE, axis=0)]
    spare = 1 if quarter % 8 == 0 else blocks * members
    got = call(
        functools.partial(qkv_kernel, shard, members, (b_qkv.shape[0], span, down), few),
        [
            shape(width, full),
            shape(queries, width),
            shape(lanes, queries),
            shape(2 * lanes, queries),
            shape(lanes, queries),
            shape(FEATURES, HEAD_DIM),
            shape(8, 2 * length),
            shape(8, width),
        ],
        [ids, *x_parts, *slabs],
        "qkv",
        scratch=[
            pltpu.VMEM((blocks, 8, full), f32),
            pltpu.VMEM((spare, quarter, full), f32),
            pltpu.VMEM((FEATURES, 1, HEAD_DIM), f32),
        ],
        smem=1,
    )
    w_cols, x, pq, kv, keys, proj, bias, vec = got

    if few:
        wo_own, kv = lax.optimization_barrier((wo_own, kv))
        kv_own = gather(kv, GROUP, members)
        kv_all = kv_own + [exchange(v, "core", 2, 1) for v in kv_own]
        wo_all = wo_own + [exchange(v, "core", 2, 1) for v in wo_own]
        (w_full,) = call(
            functools.partial(weights_out_kernel, shard),
            [shape(width, width)],
            [ids, *wo_all],
            "weights_out",
            smem=1,
        )
    else:
        kv_all = lax.all_gather(kv, PLANE, axis=0)
        w_full = lax.all_gather(w_out, ("zh", "zl", "x"), axis=0, tiled=True)

    got = attention(ids, kv_all, pq, bias)
    got, ff_slab, w_full = lax.optimization_barrier((got, ff_slab, w_full))
    kcat, vcat, att, den = got[:4]
    att_parts = scatter(got[4:], "zl")

    first, norm_rows, inverse, att_rows = call(
        norm_one_kernel,
        [row_shape, row_shape, shape(rows, 128), row_shape],
        [ids, *att_parts, x_own, w_full, vec],
        "norm_one",
        smem=1,
    )
    firsts = gather(first, GROUP, members)
    full_rows = shape(queries, blocks * down)
    ff_scratch = [
        pltpu.VMEM((width, blocks * down), f32),
        pltpu.VMEM((blocks * down, width), f32),
    ]
    got = call(
        functools.partial(forward_kernel, shard, down),
        [full_rows, shape(queries, width)] + [row_shape] * members,
        [*firsts, ff_slab, vec],
        "forward",
        scratch=ff_scratch,
    )
    pre, first_all = got[:2]
    parts = scatter(got[2:], GROUP)
    out_rows, dz2, grads_two = call(
        norm_two_kernel,
        [row_shape, row_shape, shape(8, width)],
        [*parts, first, cot_rows, vec],
        "norm_two",
    )
    dzs = gather(dz2, GROUP, members)
    got = call(
        functools.partial(backward_kernel, shard, down),
        [shape(queries, width), full_rows] + [row_shape] * members,
        [*dzs, pre, ff_slab],
        "backward",
        scratch=ff_scratch,
    )
    dz2_all, d_pre = got[:2]
    parts = scatter(got[2:], GROUP)

    (ff_grads,) = call(
        functools.partial(ff_weights_kernel, shard, down),
        [shape(blocks, shard + down + 8, width)],
        [first_all, d_pre, pre, dz2_all, grads_two],
        "ff_weights",
        push=(0,),
    )
    ff_grads, parts = lax.optimization_barrier((ff_grads, parts))

    head_rows = shape(rows, lanes)
    got = call(
        norm_one_back_kernel,
        [row_shape, shape(8, width)] + [head_rows] * members,
        [ids, *parts, dz2, norm_rows, inverse, w_full, vec],
        "norm_one_back",
        smem=1,
    )
    dz1, grads_one = got[:2]
    grads = scatter(got[2:], "zl")

    share = shape(members, members, quarter, width)
    out_shares = call(
        out_weights_kernel,
        [share, share] if few else [shape(places, members, quarter, width)],
        [ids, att_rows, dz1],
        "out_weights",
        scratch=[pltpu.VMEM((places, members, quarter, width), f32)],
        smem=1,
    )
    def sum_cores(own, other, name):
        came = exchange(other, "core", 2, 1)
        return call(sum_cores_kernel, [shape(*own.shape[1:])] * members, [own, came], name)

    if few:
        out_shares = sum_cores(*out_shares, "sum_out")
        grads, out_shares, ff_grads = lax.optimization_barrier((grads, out_shares, ff_grads))
        out_shares = scatter(out_shares, GROUP)
    else:
        grads, ff_grads = lax.optimization_barrier((grads, ff_grads))
    ff_grads = lax.psum_scatter(ff_grads, LINES, scatter_dimension=0, tiled=False)
    back = attention_back(ids, kcat, vcat, pq, bias, att, den, grads, not few)
    if few:
        back, out_shares = lax.optimization_barrier((back, out_shares))
        arrived = scatter(sum_cores(back[0], back[1], "sum_keys"), GROUP)
        out_shares, _ = lax.optimization_barrier((out_shares, arrived[0]))
        (out_grads,) = call(
            sum_kernel, [shape(members, quarter, width)], out_shares, "sum_out_plane"
        )
        out_grads = lax.all_to_all(out_grads, "zl", 0, 0, tiled=True)
        arrived, out_grads = lax.optimization_barrier((arrived, out_grads))
    else:
        arrived = lax.psum_scatter(back[0], PLANE, scatter_dimension=0, tiled=False)
        arrived = [arrived] + [jnp.zeros_like(arrived)] * 3
        out_grads = lax.psum_scatter(out_shares[0], PLANE, scatter_dimension=0, tiled=False)
        out_grads = lax.all_to_all(out_grads, "zl", 0, 0, tiled=True)
    dpq, dbias = back[-2:]

    got = call(
        qkv_back_kernel,
        [shape(queries, full)] + [row_shape] * members,
        [ids, *arrived, pq, dpq, kv, keys, proj, w_cols],
        "qkv_back",
        scratch=[pltpu.VMEM((full, queries), f32), pltpu.VMEM((queries, width), f32)],
        smem=1,
    )
    d_qkv = got[0]
    row_parts = scatter(got[1:], "zl")

    share = shape(members, members, quarter + 8, full)
    shares_out = call(
        functools.partial(qkv_weights_kernel, shard, span),
        [share, share] if few else [shape(places, members, quarter + 8, full)],
        [ids, x, d_qkv, dbias, grads_one],
        "qkv_weights",
        scratch=[pltpu.VMEM((places, members, quarter + 8, full), f32)],
        smem=1,
    )
    if few:
        mine = scatter(sum_cores(*shares_out, "sum_qkv"), GROUP)
        mine, row_parts, out_rows = lax.optimization_barrier((mine, row_parts, out_rows))
        (mine,) = call(sum_kernel, [shape(members, quarter + 8, full)], mine, "sum_qkv_plane")
    else:
        mine = lax.psum_scatter(shares_out[0], PLANE, scatter_dimension=0, tiled=False)
    ff_grads, mine = lax.optimization_barrier((ff_grads, mine))
    output = place(ids, gather(out_rows, FEAT, members), "place_output")
    mine = lax.all_to_all(mine, "zl", 0, 0, tiled=True)
    (d_input_rows,) = call(sum_four_kernel, [row_shape], [*row_parts, dz1], "sum_rows")
    d_inputs = place(ids, gather(d_input_rows, FEAT, members), "place_inputs")

    ff_parts = lax.all_gather(swap(ff_grads), FEAT, axis=0)
    d_w_up, d_w_down, d_b_up, ln_two = call(
        functools.partial(place_ff_kernel, shard, down),
        [shape(shard, w_up.shape[1]), shape(*w_down.shape), shape(1, b_up.shape[0]), shape(8, shard)],
        [ff_parts],
        "place_ff",
    )

    merged, d_b, d_position_bias, ln_one = call(
        functools.partial(merge_kernel, shard),
        [
            shape(quarter, 4 * width),
            shape(1, 3 * width),
            shape(*position_bias.shape),
            shape(8, shard),
        ],
        [mine, out_grads],
        "merge",
    )
    d_w_qkv, d_w_out = call(
        place_weights_kernel,
        [shape(*w_qkv.shape), shape(shard, width)],
        [ids, *gather(merged, FEAT, members)],
        "place_weights",
        smem=1,
    )
    count = b_qkv.shape[0]
    d_b_qkv = lax.dynamic_slice_in_dim(d_b[0], wide * count, count, 0)

    return (
        output,
        d_inputs,
        d_position_bias,
        d_w_qkv,
        d_b_qkv,
        d_w_out,
        ln_one[2],
        ln_one[0],
        ln_one[1],
        d_w_up,
        d_b_up[0],
        d_w_down,
        ln_two[2],
        ln_two[0],
        ln_two[1],
    )


def solution(mesh):
    feats, wides = mesh.shape["feat"], mesh.shape["wide"]
    ys, zhs = feats // 2, wides // (2 * feats)
    fine = Mesh(mesh.devices.reshape(ys, 2, zhs, feats, 2), ("y", "core", "zh", "zl", "x"))
    wide = ("zh", "zl", "x")
    mat, vector, lane = P(wide, None), P(wide), P(None, wide)
    return jax.shard_map(
        functools.partial(body, ys, zhs),
        mesh=fine,
        in_specs=(mat, mat, P(None, FEAT), lane, mat, vector, mat, vector)
        + (vector, vector, mat, vector, mat, vector, vector, vector),
        out_specs=(mat, mat, lane, mat, vector, mat, vector, vector)
        + (vector, mat, vector, mat, vector, vector, vector),
        check_vma=False,
    )
```

```python
import functools
import math

import jax
import jax.numpy as jnp
from jax import lax
from jax.experimental import pallas as pl
from jax.experimental.pallas import tpu as pltpu
from jax.sharding import Mesh
from jax.sharding import PartitionSpec as P

HEADS = 12
HEAD_DIM = 64
FEATURES = 64
EPS = 1e-06
f32 = jnp.float32
bf16 = jnp.bfloat16

GROUP = ("y", "x")
FEAT = ("y", "core")
PLANE = ("zh", "x", "y", "core")
LINES = ("zh", "zl", "core")
CORE, MEMBER, OWN, HEAD, WIDE, PLACE = range(6)


def split(value):
    high = value.astype(bf16)
    return high, (value - high.astype(f32)).astype(bf16)


def dot(a, b, ca, cb):
    return lax.dot_general(a, b, (((ca,), (cb,)), ((), ())), preferred_element_type=f32)


def dot3s(a, b, ca, cb):
    return dot(a[0], b[0], ca, cb) + (dot(a[0], b[1], ca, cb) + dot(a[1], b[0], ca, cb))


def dot3(a, b, ca, cb):
    return dot3s(split(a), split(b), ca, cb)


def cost():
    return pl.CostEstimate(flops=1 << 20, bytes_accessed=1 << 10, transcendentals=0)


def tiled(dims):
    if len(dims) < 2:
        return 0
    return math.prod(dims[:-2]) * -(-dims[-2] // 8) * -(-dims[-1] // 128) * 4096


def call(kernel, outs, args, name, scratch=(), smem=0, room=8, limit=0, fetch=(), push=(), far=False, deep=False, late=None):
    held = sum(tiled(ref.shape) for ref in scratch)
    held += sum(size for size in map(lambda a: tiled(a.shape), [*args, *outs]) if size > 6 << 20)
    if deep and not far:
        fetch, push, limit = range(smem, len(args)), range(len(outs)), 60 << 20
    fetch, push = tuple(fetch), tuple(push)
    near = [pltpu.VMEM(args[i].shape, args[i].dtype) for i in fetch]
    near += [pltpu.VMEM(outs[i].shape, outs[i].dtype) for i in push]
    held += sum(args[i].size * args[i].dtype.itemsize for i in fetch)
    held += sum(outs[i].size * outs[i].dtype.itemsize for i in push)
    count = len(args) + len(outs)

    def moved(*refs):
        whole, own = list(refs[:count]), refs[count : count + len(scratch)]
        spare, sems = refs[count + len(scratch) : -1], refs[-1]
        copies, after = [], []
        for at, (i, ref) in enumerate(zip(fetch, spare)):
            copies.append(pltpu.make_async_copy(whole[i], ref, sems.at[at]))
            whole[i] = ref
        for at, (i, ref) in enumerate(zip(push, spare[len(fetch) :])):
            i += len(args)
            after.append(pltpu.make_async_copy(ref, whole[i], sems.at[len(fetch) + at]))
            whole[i] = ref
        for copy in copies:
            copy.start()
        for i, copy in zip(fetch, copies):
            if late is None or i not in late:
                copy.wait()
        started = []

        def arrive(i):
            copies[fetch.index(i)].wait()

        def start(i):
            started.append(push.index(i))
            after[started[-1]].start()

        if late is not None:
            kernel(*whole, *own, arrive=arrive, start=start)
        else:
            kernel(*whole, *own)
        for i, copy in enumerate(after):
            if i not in started:
                copy.start()
        for copy in after:
            copy.wait()

    def spec(i, which):
        return pl.BlockSpec(memory_space=pltpu.HBM if i in which else pltpu.VMEM)

    return pl.pallas_call(
        moved if near else kernel,
        out_shape=outs,
        in_specs=[pl.BlockSpec(memory_space=pltpu.SMEM)] * smem
        + [spec(i, range(len(args)) if far else fetch) for i in range(smem, len(args))],
        out_specs=[spec(i, push) for i in range(len(outs))],
        scratch_shapes=list(scratch)
        + near
        + ([pltpu.SemaphoreType.DMA((len(near),))] if near else []),
        compiler_params=pltpu.CompilerParams(vmem_limit_bytes=limit or held + (room << 20)),
        cost_estimate=cost(),
        name=name,
    )(*args)


def when(condition):
    if isinstance(condition, bool):
        return lambda run: run() if condition else None
    return pl.when(condition)


def shape(*dims, dtype=f32):
    return jax.ShapeDtypeStruct(dims, dtype)


def by_case(value, count, run):
    for i in range(count):
        pl.when(value == i)(functools.partial(run, i))


def pack_qkv_kernel(rows, members, ids, *refs):
    count = (len(refs) - members - 3) // 2 + 1
    sources, pieces = refs[:count], refs[count : count + members]
    mixed, cot_out = refs[count + members : count + members + 2]
    held, sems = refs[count + members + 2 : -1], refs[-1]
    part = cot_out.shape[0]
    at = pl.multiple_of(ids[OWN] * part, 8)
    copies = [
        pltpu.make_async_copy(source.at[pl.ds(at, part)], target, sems.at[i])
        for i, (source, target) in enumerate(
            zip(sources[:2], (mixed.at[pl.ds(0, part)], cot_out))
        )
    ]
    copies += [
        pltpu.make_async_copy(source, target, sems.at[2 + i])
        for i, (source, target) in enumerate(zip(sources[2:], held))
    ]
    for copy in copies:
        copy.start()
    for copy in copies:
        copy.wait()
    w_ref, out_ref, bias_ref, b_ref, proj_ref, up_ref = held[:6]
    width = w_ref.shape[1] // 3
    lanes = width // members
    heads = bias_ref.shape[0] // members
    quarter = rows // members
    for piece in pieces:
        piece[quarter:, :] = jnp.zeros((8, 3 * lanes), f32)
        piece[quarter : quarter + 1, : b_ref.shape[0]] = b_ref[...].reshape(1, -1)
        for i, ref in enumerate(held[6:]):
            row, lane = (4, i) if i < 5 else (5, 0)
            piece[quarter + row : quarter + row + 1, lane * rows : (lane + 1) * rows] = ref[
                ...
            ].reshape(1, -1)
        piece[quarter + 5 : quarter + 6, rows : rows + up_ref.shape[0]] = up_ref[...].reshape(1, -1)
        per = 3 * lanes // HEAD_DIM
        for i in range(proj_ref.shape[0]):
            row, lane = quarter + 6 + i // per, HEAD_DIM * (i % per)
            piece[row : row + 1, lane : lane + HEAD_DIM] = proj_ref[i : i + 1]

    def own(f):
        first = quarter * f
        mixed[part : part + quarter] = out_ref[first : first + quarter]

        def head(t):
            for k, piece in enumerate(pieces):
                to = t ^ k
                for p in range(3):
                    at = width * p + lanes * to
                    piece[:quarter, lanes * p : lanes * (p + 1)] = w_ref[
                        first : first + quarter, at : at + lanes
                    ]
                piece[quarter + 1 : quarter + 1 + heads, : bias_ref.shape[1]] = bias_ref[
                    heads * to : heads * (to + 1)
                ]

        by_case(ids[HEAD], members, head)

    by_case(ids[OWN], members, own)


def pack_ff_kernel(members, down, ids, up_ref, down_ref, out):
    rows = up_ref.shape[0]
    blocks = up_ref.shape[1] // (members * down)

    def case(i):
        for w in range(blocks):
            at = (w * members + i) * down
            out[:rows, down * w : down * (w + 1)] = up_ref[:, at : at + down]
        out[rows : rows + down, :] = down_ref[down * i : down * (i + 1)]

    by_case(ids[OWN], members, case)


def plane_place(ids, members, few, i):
    if not few:
        zh, rest = divmod(i, 2 * members)
        return zh, rest // members, rest % members
    other, j = divmod(i, members)
    member = lax.bitwise_xor(ids[MEMBER], j)
    return 0, lax.rem(member, 2), 2 * lax.div(member, 2) + lax.bitwise_xor(ids[CORE], other)


def qkv_kernel(rows, members, spans, few, ids, *refs):
    mixed, refs = refs[0], refs[1:]
    w_out, x_out, pq_out, kv_out, key_out, proj_out, bias_out, vec_out, extra, held, directions = refs[-11:]
    slabs = refs[:-11]
    slabs = list(slabs) if few else [slabs[0].at[i] for i in range(slabs[0].shape[0])]
    width = x_out.shape[1]
    blocks = extra.shape[0]
    full = w_out.shape[1]
    lanes = full // 3
    heads = lanes // HEAD_DIM
    quarter = rows // members
    part = x_out.shape[0] // members
    for z in range(members):
        x_out[part * z : part * (z + 1), :] = mixed[z, :part]
    for i, slab in enumerate(slabs):
        zh, x, f = plane_place(ids, members, few, i)
        for k in range(members):
            w = 2 * (members * zh + lax.bitwise_xor(ids[HEAD], k)) + x
            if i < 2 if few else f == 0:
                extra[w] = slab[k, quarter:]
            if quarter % 8 == 0:
                at = pl.multiple_of(w * rows + f * quarter, 8)
                w_out[pl.ds(at, quarter), :] = slab[k, :quarter]
            else:
                held[w * members + f] = slab[k, :quarter]
    if quarter % 8:
        for i in range(held.shape[0]):
            w_out[quarter * i : quarter * (i + 1)] = held[i]

    share = FEATURES // members
    per = full // HEAD_DIM
    for i, slab in enumerate(slabs):
        zh, x, f = plane_place(ids, members, few, i)
        if few or (zh, x) == (0, 0):
            for r in range(share):
                at, lane = quarter + 6 + r // per, HEAD_DIM * (r % per)
                directions[share * f + r] = slab[0, at : at + 1, lane : lane + HEAD_DIM]
    for r in range(FEATURES):
        proj_out[r : r + 1, :] = directions[r]
    bias_out[...] = jnp.zeros_like(bias_out)
    b_row = []
    for w in range(blocks):
        b_row.append(extra[w, 0:1, : spans[0]])
        count = spans[1]
        bias_out[:heads, count * w : count * (w + 1)] = extra[w, 1 : 1 + heads, :count]
        for i in range(6):
            row, lane = (4, i) if i < 5 else (5, 0)
            vec_out[1 + i : 2 + i, rows * w : rows * (w + 1)] = extra[
                w, row : row + 1, lane * rows : (lane + 1) * rows
            ]
    vec_out[7:8] = jnp.zeros((1, width), f32)
    b_row = jnp.concatenate(b_row, axis=1)

    def unit(g):
        count = spans[2]
        for w in range(blocks):
            vec_out[0:1, count * w : count * (w + 1)] = extra[
                w, 5:6, rows + count * g : rows + count * (g + 1)
            ]

    by_case(ids[MEMBER], members, unit)
    qkv = dot3(x_out[...], w_out[...], 1, 0)
    scale = HEAD_DIM**-0.25
    proj = split(proj_out[...])

    def head(t):
        bias = [b_row[:, width * p + lanes * t : width * p + lanes * (t + 1)] for p in range(3)]
        turned = (qkv + jnp.concatenate(bias, axis=1)).T
        for h in range(heads):
            lo, hi = HEAD_DIM * h, HEAD_DIM * (h + 1)
            q = turned[lo:hi] * scale
            k = turned[lanes + lo : lanes + hi] * scale
            pq_out[lo:hi] = jnp.exp(dot3s(proj, split(q), 1, 0))
            pk = dot3s(proj, split(k), 1, 0) - 0.5 * jnp.sum(k * k, axis=0, keepdims=True)
            kv_out[128 * h : 128 * h + 64] = jnp.exp(pk)
            kv_out[128 * h + 64 : 128 * h + 128] = turned[2 * lanes + lo : 2 * lanes + hi]
            key_out[lo:hi] = k

    by_case(ids[HEAD], members, head)


def rolled_rows(table, row):
    wide = jnp.broadcast_to(row, (8, row.shape[1]))
    return pltpu.roll(wide, 0, 1, stride=1, stride_axis=0)


def make_tables(tables, bias_ref, heads):
    length = bias_ref.shape[1]
    for h in range(heads):
        rows = rolled_rows(None, jnp.exp(bias_ref[h : h + 1]))
        tables[0, 8 * h : 8 * h + 8] = rows
        tables[1, 8 * h : 8 * h + 8] = pltpu.roll(rows, length - 64, 1)


def factor_tile(windows):
    first = lax.broadcasted_iota(jnp.int32, (8, 128), 1) < 64
    pairs = {}
    for g in range(8):
        for d in range(-3, 3):
            low = pltpu.roll(windows[d + 3], (8 * g + 64) % 128, 1)
            high = windows[d + 4] if g == 0 else pltpu.roll(windows[d + 4], 8 * g, 1)
            pairs[d, g] = jnp.where(first, low, high)
    rows = []
    for z in range(4):
        for g in range(8):
            rows.append(jnp.concatenate([pairs[-z, g], pairs[2 - z, g]], axis=1))
    return jnp.concatenate(rows, axis=0)


def window_sums(pairs):
    first = lax.broadcasted_iota(jnp.int32, (8, 128), 1) < 64
    sums = [jnp.zeros((8, 128), f32) for _ in range(7)]
    for g in range(8):
        for d in range(-3, 3):
            total = None
            for z in range(4):
                for p in range(2):
                    if 2 * p - z == d:
                        term = pairs[64 * z + 8 * g : 64 * z + 8 * g + 8, 128 * p : 128 * p + 128]
                        total = term if total is None else total + term
            low = pltpu.roll(jnp.where(first, total, 0.0), 64 - 8 * g, 1)
            high = jnp.where(first, 0.0, total)
            sums[d + 3] = sums[d + 3] + low
            sums[d + 4] = sums[d + 4] + (high if g == 0 else pltpu.roll(high, 128 - 8 * g, 1))
    return sums


def window_start(ids, members, groups, seg, length, n):
    if groups == 1:
        other, j = n // members, n % members
        member = lax.bitwise_xor(ids[MEMBER], j)
        zh, x = ids[PLACE] * 0, lax.rem(member, 2)
        f = 2 * lax.div(member, 2) + lax.bitwise_xor(ids[CORE], other)
    else:
        zh, x, f = n // (2 * members), lax.rem(lax.div(n, members), 2), lax.rem(n, members)
    own = ids[PLACE]
    away = 8 * members * (lax.div(own, 2 * members) - zh)
    away += members * (lax.rem(lax.div(own, members), 2) - x) + ids[OWN] - f
    start = away + length // (2 * seg) - 1
    odd = lax.rem(start, 2)
    return start - odd, odd


def window_at(start, d):
    return pl.multiple_of(start * 64 + 512 * d, 128)


def attention_kernel(groups, blocks, ids, *refs, arrive=None, start=None):
    nkv = blocks if groups == 1 else 1
    kv_refs = refs[:nkv]
    pq_ref, bias_ref = refs[nkv : nkv + 2]
    kcat, vcat, att_out, den_out = refs[nkv + 2 : nkv + 6]
    parts = refs[nkv + 6 : nkv + 10]
    tables, qcat, out_rows = refs[nkv + 10 :]
    heads = pq_ref.shape[0] // 64
    queries = pq_ref.shape[1]
    step = pl.program_id(0) if groups > 1 else 0

    @when(step == 0)
    def _():
        make_tables(tables, bias_ref, heads)
        for h in range(heads):
            high, low = split(pq_ref[64 * h : 64 * h + 64])
            qcat[h, 0:64] = high
            qcat[h, 64:128] = high
            qcat[h, 128:192] = low
        att_out[...] = jnp.zeros_like(att_out)
        den_out[...] = jnp.zeros_like(den_out)

    for n in range(blocks):
        if arrive is not None:
            arrive(1 + n)
        block = kv_refs[n] if groups == 1 else kv_refs[0].at[n]
        for h in range(heads):
            for part, cat in ((0, kcat), (64, vcat)):
                high, low = split(block[128 * h + part : 128 * h + part + 64])
                cat[n, h, 0:64] = high
                cat[n, h, 64:128] = low
                cat[n, h, 128:192] = high

    if start is not None:
        start(0)
        start(1)

    def advance(n, carry):
        first, odd = window_start(ids, 4, groups, 64, bias_ref.shape[1], step * blocks + n)
        for h in range(heads):
            scores = dot(kcat[n, h], qcat[h], 0, 0)
            rows = slice(8 * h, 8 * h + 8)
            windows = [
                tables[odd, rows, pl.ds(window_at(first, d), 128)] for d in range(-3, 4)
            ]
            weight = scores * factor_tile(windows)
            high, low = split(weight)
            both = dot(vcat[n, h, 0:128], high, 1, 0)
            more = dot(vcat[n, h, 0:64], low, 1, 0)
            att_out[64 * h : 64 * h + 64] += both[0:64] + both[64:128] + more
            den_out[h : h + 1] += jnp.sum(weight, axis=0, keepdims=True)
        return carry

    lax.fori_loop(0, blocks, advance, 0)

    @when(step == groups - 1)
    def _():
        for h in range(heads):
            att_out[64 * h : 64 * h + 64] = att_out[64 * h : 64 * h + 64] / den_out[h : h + 1]
        out_rows[...] = att_out[...].T
        rows = queries // 4
        for k in range(4):
            first = pl.multiple_of(lax.bitwise_xor(ids[HEAD], k) * rows, 8)
            parts[k][...] = out_rows[pl.ds(first, rows), :]


def attention(ids, kv, pq, window):
    stacked = not isinstance(kv, list)
    count = kv.shape[0] if stacked else len(kv)
    blocks = 8 if stacked else count
    groups = count // blocks
    queries = pq.shape[1]
    heads = pq.shape[0] // 64
    cat = shape(count, heads, 192, queries, dtype=bf16)
    rows = shape(queries // 4, heads * 64)
    outs = [cat, cat, shape(heads * 64, queries), shape(8, queries)] + [rows] * 4
    scratch = [
        pltpu.VMEM((2, 8 * heads, window.shape[1]), f32),
        pltpu.VMEM((heads, 192, queries), bf16),
        pltpu.VMEM((queries, heads * 64), f32),
    ]
    kernel = functools.partial(attention_kernel, groups, blocks)
    if not stacked:
        return call(
            kernel,
            outs,
            [ids, *kv, pq, window],
            "attention",
            scratch,
            1,
            deep=True,
            late=range(1, 1 + count),
        )
    whole = lambda a: pl.BlockSpec(a.shape, lambda g, nd=len(a.shape): (0,) * nd)
    smem = pl.BlockSpec(memory_space=pltpu.SMEM)
    kv_spec = pl.BlockSpec((blocks,) + kv.shape[1:], lambda g: (g, 0, 0))
    cat_spec = pl.BlockSpec((blocks, heads, 192, queries), lambda g: (g, 0, 0, 0))
    return pl.pallas_call(
        kernel,
        grid=(groups,),
        out_shape=outs,
        in_specs=[smem, kv_spec, whole(pq), whole(window)],
        out_specs=[cat_spec, cat_spec] + [whole(a) for a in outs[2:]],
        scratch_shapes=scratch,
        compiler_params=pltpu.CompilerParams(vmem_limit_bytes=52 << 20),
        name="attention",
    )(ids, kv, pq, window)


def attention_back_kernel(groups, blocks, ids, *refs, arrive=None, start=None):
    kcat, vcat, pq_ref, bias_ref, att_ref, den_ref = refs[:6]
    grads = refs[6:10]
    if groups == 1:
        own, other, dpq_out, dbias_out, tables, qcat, gcat, gden, diag, grad_rows = refs[10:]
    else:
        dkv, dpq_out, dbias_out, tables, qcat, gcat, gden, diag, grad_rows = refs[10:]
    heads = pq_ref.shape[0] // 64
    queries = pq_ref.shape[1]
    step = pl.program_id(0) if groups > 1 else 0

    @when(step == 0)
    def _():
        rows = queries // 4
        for k in range(4):
            first = pl.multiple_of(lax.bitwise_xor(ids[HEAD], k) * rows, 8)
            grad_rows[pl.ds(first, rows), :] = grads[k][...]
        make_tables(tables, bias_ref, heads)
        d_att = grad_rows[...].T
        gden[...] = jnp.zeros_like(gden)
        for h in range(heads):
            lo, hi = 64 * h, 64 * h + 64
            for value, cat in ((pq_ref[lo:hi], qcat), (d_att[lo:hi] / den_ref[h : h + 1], gcat)):
                high, low = split(value)
                cat[h, 0:64] = high
                cat[h, 64:128] = high
                cat[h, 128:192] = low
            gden[h : h + 1] = -(
                jnp.sum(d_att[lo:hi] * att_ref[lo:hi], axis=0, keepdims=True) / den_ref[h : h + 1]
            )
        dpq_out[...] = jnp.zeros_like(dpq_out)
        diag[...] = jnp.zeros_like(diag)

    def advance(dkv, first, n, carry):
        begin, odd = window_start(ids, 4, groups, 64, bias_ref.shape[1], step * blocks + n)
        for h in range(heads):
            scores = dot(kcat[n, h], qcat[h], 0, 0)
            rows = slice(8 * h, 8 * h + 8)
            factor = factor_tile(
                [tables[odd, rows, pl.ds(window_at(begin, d), 128)] for d in range(-3, 4)]
            )
            d_weight = dot(vcat[n, h], gcat[h], 0, 0) + gden[h : h + 1]
            w_high, w_low = split(scores * factor)
            e_high, e_low = split(d_weight * factor)
            pairs = d_weight * scores
            both = dot(gcat[h, 64:192], w_high, 1, 1)
            dv = both[0:64] + both[64:128] + dot(gcat[h, 0:64], w_low, 1, 1)
            both = dot(qcat[h, 64:192], e_high, 1, 1)
            dk = both[0:64] + both[64:128] + dot(qcat[h, 0:64], e_low, 1, 1)
            both = dot(kcat[n, h, 0:128], e_high, 1, 0)
            dq = both[0:64] + both[64:128] + dot(kcat[n, h, 0:64], e_low, 1, 0)
            dpq_out[64 * h : 64 * h + 64] += dq
            dkv[n - first, 128 * h : 128 * h + 64] = dk
            dkv[n - first, 128 * h + 64 : 128 * h + 128] = dv
            for i, total in enumerate(window_sums(pairs)):
                diag[odd, rows, pl.ds(window_at(begin, i - 3), 128)] += total
        return carry

    if groups == 1:
        half = blocks // 2
        if arrive is not None:
            arrive(1)
            arrive(2)
        lax.fori_loop(half, blocks, functools.partial(advance, other, half), 0)
        if start is not None:
            start(1)
        lax.fori_loop(0, half, functools.partial(advance, own, 0), 0)
        if start is not None:
            start(0)
    else:
        lax.fori_loop(0, blocks, functools.partial(advance, dkv, 0), 0)

    @when(step == groups - 1)
    def _():
        length = diag.shape[2]
        dbias_out[...] = jnp.zeros_like(dbias_out)
        for h in range(heads):
            both = diag[0, 8 * h : 8 * h + 8] + pltpu.roll(diag[1, 8 * h : 8 * h + 8], 64, 1)
            total = both[0:1]
            for s in range(1, 8):
                total = total + pltpu.roll(both[s : s + 1], length - s, 1)
            dbias_out[h : h + 1] = total * jnp.exp(bias_ref[h : h + 1])


def attention_back(ids, kcat, vcat, pq, window, att, den, grads, stacked):
    count, heads, _, queries = kcat.shape
    blocks = 8 if stacked else count
    groups = count // blocks
    outs = [shape(heads * 64, queries), shape(8, window.shape[1])]
    args = [ids, kcat, vcat, pq, window, att, den] + list(grads)
    scratch = [
        pltpu.VMEM((2, 8 * heads, window.shape[1]), f32),
        pltpu.VMEM((heads, 192, queries), bf16),
        pltpu.VMEM((heads, 192, queries), bf16),
        pltpu.VMEM((8, queries), f32),
        pltpu.VMEM((2, 8 * heads, window.shape[1]), f32),
        pltpu.VMEM((queries, heads * 64), f32),
    ]
    kernel = functools.partial(attention_back_kernel, groups, blocks)
    if not stacked:
        half = shape(count // 2, heads * 128, queries)
        return call(
            kernel,
            [half, half] + outs,
            args,
            "attention_back",
            scratch,
            1,
            deep=True,
            late=(1, 2),
        )
    whole = lambda a: pl.BlockSpec(a.shape, lambda g, nd=len(a.shape): (0,) * nd)
    smem = pl.BlockSpec(memory_space=pltpu.SMEM)
    cat_spec = pl.BlockSpec((blocks, heads, 192, queries), lambda g: (g, 0, 0, 0))
    dkv_spec = pl.BlockSpec((blocks, heads * 128, queries), lambda g: (g, 0, 0))
    return pl.pallas_call(
        kernel,
        grid=(groups,),
        out_shape=[shape(count, heads * 128, queries)] + outs,
        in_specs=[smem, cat_spec, cat_spec] + [whole(a) for a in args[3:]],
        out_specs=[dkv_spec] + [whole(a) for a in outs],
        scratch_shapes=scratch,
        compiler_params=pltpu.CompilerParams(vmem_limit_bytes=52 << 20),
        name="attention_back",
    )(*args)


def normed(value):
    mean = jnp.mean(value, axis=1, keepdims=True)
    centered = value - mean
    var = jnp.mean(centered * centered, axis=1, keepdims=True)
    inverse = lax.rsqrt(var + EPS)
    return centered * inverse, inverse


def norm_back(upstream, n, inverse, gain):
    scaled = gain * upstream
    mean = jnp.mean(scaled, axis=1, keepdims=True)
    slope = jnp.mean(scaled * n, axis=1, keepdims=True)
    return (scaled - mean - n * slope) * inverse


def colsum(value):
    return jnp.sum(value, axis=0, keepdims=True)


def weights_out_kernel(rows, ids, *refs):
    out = refs[-1]
    members, quarter, _ = refs[0].shape
    for i, ref in enumerate(refs[:-1]):
        other, j = divmod(i, members)
        place = lax.bitwise_xor(ids[MEMBER], j)
        f = 2 * lax.div(place, 2) + lax.bitwise_xor(ids[CORE], other)
        for k in range(members):
            w = 2 * k + lax.rem(place, 2)
            out[pl.ds(pl.multiple_of(rows * w + quarter * f, 8), quarter), :] = ref[k]


def norm_one_kernel(ids, a0, a1, a2, a3, x_ref, w_ref, vec_ref, *refs):
    first_out, n_out, inverse_out, att_out = refs
    lanes = a0.shape[1]

    def head(t):
        for k, ref in enumerate((a0, a1, a2, a3)):
            at = lanes * (t ^ k)
            att_out[:, at : at + lanes] = ref[...]

    by_case(ids[HEAD], 4, head)
    projected = dot3(att_out[...], w_ref[...], 1, 0)
    n, inverse = normed(x_ref[: a0.shape[0]] + (projected + vec_ref[1:2]))
    first_out[...] = n * vec_ref[2:3] + vec_ref[3:4]
    n_out[...] = n
    inverse_out[...] = jnp.broadcast_to(inverse, inverse_out.shape)


def norm_two_kernel(p0, p1, p2, p3, first_ref, cot_ref, vec_ref, rows_out, dz_out, grads_out):
    value = first_ref[...] + ((p0[...] + p1[...]) + (p2[...] + p3[...]) + vec_ref[4:5])
    n, inverse = normed(value)
    rows_out[...] = n * vec_ref[5:6] + vec_ref[6:7]
    up = cot_ref[...]
    dz = norm_back(up, n, inverse, vec_ref[5:6])
    dz_out[...] = dz
    grads_out[...] = jnp.zeros_like(grads_out)
    grads_out[0:1] = colsum(up * n)
    grads_out[1:2] = colsum(up)
    grads_out[2:3] = colsum(dz)


def norm_one_back_kernel(ids, p0, p1, p2, p3, dz_ref, n_ref, inverse_ref, w_ref, vec_ref, *refs):
    dz_out, grads_out = refs[:2]
    parts = refs[2:6]
    up = dz_ref[...] + ((p0[...] + p1[...]) + (p2[...] + p3[...]))
    n = n_ref[...]
    dz = norm_back(up, n, inverse_ref[:, 0:1], vec_ref[2:3])
    dz_out[...] = dz
    grads_out[...] = jnp.zeros_like(grads_out)
    grads_out[0:1] = colsum(up * n)
    grads_out[1:2] = colsum(up)
    grads_out[2:3] = colsum(dz)
    d_att = dot3(dz, w_ref[...], 1, 1)
    lanes = parts[0].shape[1]

    def case(i):
        for k in range(4):
            at = lanes * (i ^ k)
            parts[k][...] = d_att[:, at : at + lanes]

    by_case(ids[HEAD], 4, case)


def stack_rest_kernel(first, source, out):
    out[...] = source[:, first : first + out.shape[1]]


def stack_kernel(*refs):
    for i, ref in enumerate(refs[:-1]):
        refs[-1][i] = ref[...]


def stack_rows(target, refs):
    rows = refs[0].shape[0]
    for k, ref in enumerate(refs):
        target[rows * k : rows * (k + 1), :] = ref[...]


def prepare_kernel(rows_up, slab, up_high, up_low, down_high, down_low):
    for first, count, high, low in (
        (0, rows_up, up_high, up_low),
        (rows_up, slab.shape[1] - rows_up, down_high, down_low),
    ):
        pieces = [slab[w, first : first + count] for w in range(slab.shape[0])]
        high[...], low[...] = split(jnp.concatenate(pieces, axis=0))


def forward_kernel(f0, f1, f2, f3, up_high, up_low, down_high, down_low, vec_ref, *refs):
    pre_out, first_out = refs[:2]
    parts = refs[2:6]
    stack_rows(first_out, (f0, f1, f2, f3))
    pre = dot3s(split(first_out[...]), (up_high[...], up_low[...]), 1, 0) + vec_ref[0:1]
    pre_out[...] = pre
    hidden = 0.5 * pre * (1.0 + lax.erf(pre * (0.5**0.5)))
    branch = dot3s(split(hidden), (down_high[...], down_low[...]), 1, 0)
    rows = f0.shape[0]
    for k in range(4):
        parts[k][...] = branch[rows * k : rows * (k + 1)]


def backward_kernel(z0, z1, z2, z3, pre_ref, up_high, up_low, down_high, down_low, *refs):
    dz_out, d_pre_out = refs[:2]
    parts = refs[2:6]
    stack_rows(dz_out, (z0, z1, z2, z3))
    d_hidden = dot3s(split(dz_out[...]), (down_high[...], down_low[...]), 1, 1)
    pre = pre_ref[...]
    density = jnp.exp(-0.5 * pre * pre) * ((2.0 * jnp.pi) ** -0.5)
    d_pre = d_hidden * (0.5 * (1.0 + lax.erf(pre * (0.5**0.5))) + pre * density)
    d_pre_out[...] = d_pre
    d_first = dot3s(split(d_pre), (up_high[...], up_low[...]), 1, 1)
    rows = z0.shape[0]
    for k in range(4):
        parts[k][...] = d_first[rows * k : rows * (k + 1)]


def ff_weights_kernel(rows_up, rows_down, first_ref, d_pre_ref, pre_ref, dz_ref, grads_ref, out):
    pre = pre_ref[...]
    hidden = 0.5 * pre * (1.0 + lax.erf(pre * (0.5**0.5)))
    d_pre = d_pre_ref[...]
    blocks = out.shape[0]
    base = rows_up + rows_down
    out[:, base:, :] = jnp.zeros((blocks, 8, out.shape[2]), f32)
    d_b_up = colsum(d_pre)
    up = dot3(first_ref[...], d_pre, 0, 0)
    down = dot3(hidden, dz_ref[...], 0, 0)
    for w in range(blocks):
        out[w, :rows_up, :] = up[rows_up * w : rows_up * (w + 1)]
        out[w, rows_up:base, :] = down[rows_down * w : rows_down * (w + 1)]
        out[w, base : base + 1, :rows_down] = d_b_up[:, rows_down * w : rows_down * (w + 1)]
        for i in range(3):
            out[w, base + 1 + i : base + 2 + i, :rows_up] = grads_ref[
                i : i + 1, rows_up * w : rows_up * (w + 1)
            ]


def shares(held, ids, outs):
    if len(outs) == 1:
        outs[0][...] = held[...]
        return
    members = held.shape[1]
    for other, out in enumerate(outs):
        core = lax.bitwise_xor(ids[CORE], other)
        for j in range(members):
            place = lax.bitwise_xor(ids[MEMBER], j)
            at = lax.rem(place, 2) * members + 2 * lax.div(place, 2) + core
            for k in range(members):
                out[j, k] = held[at, lax.bitwise_xor(ids[HEAD], k)]


def out_weights_kernel(ids, att_ref, dz_ref, *refs):
    outs, held = refs[:-1], refs[-1]
    places, members, quarter, _ = held.shape
    value = dot3(att_ref[...], dz_ref[...], 0, 0)
    for place in range(places):
        zh, rest = divmod(place, 2 * members)
        x, f = divmod(rest, members)
        for z in range(members):
            at = ((2 * (members * zh + z) + x) * members + f) * quarter
            held[place, z] = value[at : at + quarter]
    shares(held, ids, outs)


def sum_cores_kernel(own, came, *outs):
    for j, out in enumerate(outs):
        out[...] = own[j] + came[j]


def qkv_back_kernel(ids, d0, d1, d2, d3, pq_ref, dpq_ref, kv_ref, key_ref, proj_ref, w_ref, *refs):
    d_qkv_out = refs[0]
    parts = refs[1:5]
    turned, rows_held = refs[5:]
    heads = pq_ref.shape[0] // 64
    width = heads * 64
    scale = HEAD_DIM**-0.25
    proj = split(proj_ref[...])
    dkv = (d0[...] + d1[...]) + (d2[...] + d3[...])
    for h in range(heads):
        lo, hi = 64 * h, 64 * h + 64
        turned[lo:hi] = scale * dot3s(proj, split(dpq_ref[lo:hi] * pq_ref[lo:hi]), 0, 0)
        pk = dkv[128 * h : 128 * h + 64] * kv_ref[128 * h : 128 * h + 64]
        turned[width + lo : width + hi] = scale * (
            dot3s(proj, split(pk), 0, 0) - key_ref[lo:hi] * colsum(pk)
        )
        turned[2 * width + lo : 2 * width + hi] = dkv[128 * h + 64 : 128 * h + 128]
    d_qkv = turned[...].T
    d_qkv_out[...] = d_qkv
    rows_held[...] = dot3(d_qkv, w_ref[...], 1, 1)
    rows = parts[0].shape[0]
    for k in range(4):
        first = pl.multiple_of(lax.bitwise_xor(ids[HEAD], k) * rows, 8)
        parts[k][...] = rows_held[pl.ds(first, rows), :]


def qkv_weights_kernel(rows, span, ids, x_ref, d_ref, dbias_ref, grads_ref, *refs):
    outs, held = refs[:-1], refs[-1]
    d_qkv = d_ref[...]
    places, members, _, full = held.shape
    quarter = rows // members
    held[:, :, quarter:, :] = jnp.zeros((places, members, 8, full), f32)
    d_b = colsum(d_qkv)
    weights = dot3(x_ref[...], d_qkv, 0, 0)
    for place in range(places):
        zh, rest = divmod(place, 2 * members)
        x, f = divmod(rest, members)
        for z in range(members):
            w = 2 * (members * zh + z) + x
            at = (w * members + f) * quarter
            held[place, z, :quarter] = weights[at : at + quarter]
            held[place, z, quarter : quarter + 1] = d_b
            for i in range(3):
                held[place, z, quarter + 1 : quarter + 2, rows * i : rows * (i + 1)] = grads_ref[
                    i : i + 1, rows * w : rows * (w + 1)
                ]
            held[place, z, quarter + 2 : quarter + 5, :span] = dbias_ref[
                0:3, span * w : span * (w + 1)
            ]
    shares(held, ids, outs)


def merge_kernel(rows, ids, r0, r1, r2, r3, w0, w1, w2, w3, out, b_own, bias_out, *rest):
    refs, b_out = (r0, r1, r2, r3), rest[3]
    members = len(refs)
    lanes = r0.shape[1] // 3
    width = lanes * members
    span = bias_out.shape[1]
    quarter = rows // members
    total = (r0[quarter + 1 : quarter + 2] + r1[quarter + 1 : quarter + 2]) + (
        r2[quarter + 1 : quarter + 2] + r3[quarter + 1 : quarter + 2]
    )
    for i in range(3):
        rest[i][...] = total[:, rows * i : rows * (i + 1)].reshape(rows)
    out[:, 3 * width :] = (w0[...] + w1[...]) + (w2[...] + w3[...])

    def head(t):
        for k, ref in enumerate(refs):
            f = t ^ k
            for p in range(3):
                at = width * p + lanes * f
                out[:, at : at + lanes] = ref[:quarter, lanes * p : lanes * (p + 1)]
                b_out[:, at : at + lanes] = ref[
                    quarter : quarter + 1, lanes * p : lanes * (p + 1)
                ]
            bias_out[3 * f : 3 * f + 3] = ref[quarter + 2 : quarter + 5, :span]

    by_case(ids[HEAD], members, head)
    count = b_own.shape[0]

    def place(w):
        b_own[...] = b_out[:, count * w : count * (w + 1)].reshape(count)

    by_case(ids[WIDE], b_out.shape[1] // count, place)


def place_weights_kernel(ids, r0, r1, r2, r3, w_out, wo_out):
    quarter = r0.shape[0]
    full = w_out.shape[1]

    def own(f):
        for k, ref in enumerate((r0, r1, r2, r3)):
            at = quarter * (f ^ k)
            w_out[at : at + quarter] = ref[:, :full]
            wo_out[at : at + quarter] = ref[:, full:]

    by_case(ids[OWN], 4, own)


def sum_split_kernel(a, b, c, d, *outs):
    for k, out in enumerate(outs):
        out[...] = (a[k] + b[k]) + (c[k] + d[k])


def sum_kernel(*refs):
    total = refs[0][...]
    for ref in refs[1:-1]:
        total = total + ref[...]
    refs[-1][...] = total


def sum_four_kernel(p0, p1, p2, p3, dz_ref, out):
    out[...] = dz_ref[...] + ((p0[...] + p1[...]) + (p2[...] + p3[...]))


def place_kernel(ids, r0, r1, r2, r3, out):
    rows = r0.shape[0]
    for k, ref in enumerate((r0, r1, r2, r3)):
        out[pl.ds(pl.multiple_of(lax.bitwise_xor(ids[OWN], k) * rows, 8), rows), :] = ref[...]


def place_ff_kernel(rows, down, ids, r0, r1, r2, r3, up_out, down_out, b_all, v0, v1, v2, b_out):
    refs = (r0, r1, r2, r3)
    members = len(refs)
    base = rows + down
    total = r0[base + 1 : base + 4, :rows] + r1[base + 1 : base + 4, :rows]
    total = total + (r2[base + 1 : base + 4, :rows] + r3[base + 1 : base + 4, :rows])
    for i, out in enumerate((v0, v1, v2)):
        out[...] = total[i : i + 1].reshape(rows)

    def own(i):
        for k, ref in enumerate(refs):
            f = i ^ k
            for w in range(up_out.shape[1] // (members * down)):
                at = (w * members + f) * down
                up_out[:, at : at + down] = ref[:rows, down * w : down * (w + 1)]
            down_out[down * f : down * (f + 1)] = ref[rows:base]
            b_out[:, down * f : down * (f + 1)] = ref[base : base + 1, :down]

    by_case(ids[OWN], members, own)
    b_all[...] = b_out[...].reshape(b_all.shape)


def exchange(value, axes, count, k):
    return lax.ppermute(value, axes, [(i, i ^ k) for i in range(count)])


def swap(value):
    return lax.ppermute(value, ("core", "x"), [(0, 0), (1, 2), (2, 1), (3, 3)])


def place(ids, values, name):
    return call(
        place_kernel,
        [shape(len(values) * values[0].shape[0], values[0].shape[1])],
        [ids, *values],
        name,
        smem=1,
    )[0]


def gather(value, axes, count):
    return [value] + [exchange(value, axes, count, k) for k in range(1, count)]


def relay(value):
    came = exchange(value, "y", 2, 1)
    return [value, exchange(value, "core", 2, 1), came, exchange(came, "core", 2, 1)]


def scatter(parts, axes):
    return [parts[0]] + [exchange(parts[k], axes, len(parts), k) for k in range(1, len(parts))]


def body(
    ys,
    zhs,
    inputs,
    cotangent,
    random_proj,
    position_bias,
    w_qkv,
    b_qkv,
    w_out,
    b_out,
    ln1_gain,
    ln1_bias,
    w_up,
    b_up,
    w_down,
    b_down,
    ln2_gain,
    ln2_bias,
):
    members = 2 * ys
    blocks = 2 * zhs * members
    places = 2 * zhs * members
    few = zhs == 1
    core = lax.axis_index("core")
    x_at, y_at = lax.axis_index("x"), lax.axis_index("y")
    zh_at, zl_at = lax.axis_index("zh"), lax.axis_index("zl")
    feat = 2 * y_at + core
    group = 2 * y_at + x_at
    wide = 2 * (members * zh_at + zl_at) + x_at
    place_at = (2 * zh_at + x_at) * members + feat
    ids = jnp.stack([core, group, feat, zl_at, wide, place_at]).astype(jnp.int32)
    queries, width = inputs.shape
    rows = queries // members
    shard = w_qkv.shape[0]
    quarter = shard // members
    down = w_down.shape[0] // members
    heads = HEADS // members
    lanes = heads * HEAD_DIM
    span = position_bias.shape[1]
    full = 3 * lanes
    length = queries * blocks
    row_shape = shape(rows, width)

    packed = [w_qkv, w_out, position_bias, b_qkv, random_proj.T]
    packed += [b_up, b_out, ln1_gain, ln1_bias, b_down, ln2_gain, ln2_bias]
    got = call(
        functools.partial(pack_qkv_kernel, shard, members),
        [shape(quarter + 8, full)] * members + [shape(rows + -(-quarter // 8) * 8, width), row_shape],
        [ids, inputs, cotangent] + packed,
        "pack_qkv",
        scratch=[pltpu.VMEM(a.shape, f32) for a in packed]
        + [pltpu.SemaphoreType.DMA((len(packed) + 2,))],
        smem=1,
        limit=60 << 20,
        far=True,
    )
    mixed, cot_rows = got[members:]
    pieces = scatter(got[:members], "zl")
    pack_ids, _ = lax.optimization_barrier((ids, mixed))
    (ff_slab,) = call(
        functools.partial(pack_ff_kernel, members, down),
        [shape(shard + down, width)],
        [pack_ids, w_up, w_down],
        "pack_ff",
        smem=1,
    )
    ff_slab = swap(ff_slab)
    mixed_all = lax.all_gather(mixed, "zl", axis=0)
    pieces, ff_slab = lax.optimization_barrier((pieces, ff_slab))
    (slab,) = call(
        stack_kernel, [shape(members, quarter + 8, full)], pieces, "stack_pieces"
    )
    if few:
        slabs = gather(slab, GROUP, members)
    else:
        slabs = [lax.all_gather(slab, PLANE, axis=0)]
    slabs, mixed_all = lax.optimization_barrier((slabs, mixed_all))
    if few:
        slabs = slabs + [exchange(v, "core", 2, 1) for v in slabs]
    slabs, ff_slab = lax.optimization_barrier((slabs, ff_slab))
    ff_slab = lax.all_gather(ff_slab, LINES, axis=0)
    spare = 1 if quarter % 8 == 0 else blocks * members
    got = call(
        functools.partial(qkv_kernel, shard, members, (b_qkv.shape[0], span, down), few),
        [
            shape(width, full),
            shape(queries, width),
            shape(lanes, queries),
            shape(2 * lanes, queries),
            shape(lanes, queries),
            shape(FEATURES, HEAD_DIM),
            shape(8, 2 * length),
            shape(8, width),
        ],
        [ids, mixed_all, *slabs],
        "qkv",
        scratch=[
            pltpu.VMEM((blocks, 8, full), f32),
            pltpu.VMEM((spare, quarter, full), f32),
            pltpu.VMEM((FEATURES, 1, HEAD_DIM), f32),
        ],
        smem=1,
        deep=True,
    )
    w_cols, x, pq, kv, keys, proj, bias, vec = got

    if few:
        kv_own = gather(kv, GROUP, members)
        kv_all = kv_own + [exchange(v, "core", 2, 1) for v in kv_own]
        (wo_parts,) = call(
            functools.partial(stack_rest_kernel, rows),
            [shape(members, quarter, width)],
            [mixed_all],
            "stack_out",
        )
        wo_parts, _ = lax.optimization_barrier((wo_parts, kv_all))
        wo_own = gather(wo_parts, GROUP, members)
    else:
        kv_all = lax.all_gather(kv, PLANE, axis=0)
    got = attention(ids, kv_all, pq, bias)
    kcat, vcat, att, den = got[:4]
    att_parts = scatter(got[4:], "zl")
    if few:
        wo_own, _ = lax.optimization_barrier((wo_own, att_parts[1:]))
        wo_all = wo_own + [exchange(v, "core", 2, 1) for v in wo_own]
        (w_full,) = call(
            functools.partial(weights_out_kernel, shard),
            [shape(width, width)],
            [ids, *wo_all],
            "weights_out",
            smem=1,
        )
    else:
        w_full = lax.all_gather(w_out, ("zh", "zl", "x"), axis=0, tiled=True)

    first, norm_rows, inverse, att_rows = call(
        norm_one_kernel,
        [row_shape, row_shape, shape(rows, 128), row_shape],
        [ids, *att_parts, mixed, w_full, vec],
        "norm_one",
        smem=1,
    )
    first, ff_slab = lax.optimization_barrier((first, ff_slab))
    firsts = gather(first, GROUP, members)
    full_rows = shape(queries, blocks * down)
    ff_matrices = call(
        functools.partial(prepare_kernel, shard),
        [shape(width, blocks * down, dtype=bf16)] * 2
        + [shape(blocks * down, width, dtype=bf16)] * 2,
        [ff_slab],
        "prepare",
    )
    got = call(
        forward_kernel,
        [full_rows, shape(queries, width)] + [row_shape] * members,
        [*firsts, *ff_matrices, vec],
        "forward",
    )
    pre, first_all = got[:2]
    parts = scatter(got[2:], GROUP)
    out_rows, dz2, grads_two = call(
        norm_two_kernel,
        [row_shape, row_shape, shape(8, width)],
        [*parts, first, cot_rows, vec],
        "norm_two",
    )
    dzs = gather(dz2, GROUP, members)
    got = call(
        backward_kernel,
        [shape(queries, width), full_rows] + [row_shape] * members,
        [*dzs, pre, *ff_matrices],
        "backward",
    )
    dz2_all, d_pre = got[:2]
    parts = scatter(got[2:], GROUP)

    (ff_grads,) = call(
        functools.partial(ff_weights_kernel, shard, down),
        [shape(blocks, shard + down + 8, width)],
        [first_all, d_pre, pre, dz2_all, grads_two],
        "ff_weights",
        push=(0,),
    )
    ff_grads, parts = lax.optimization_barrier((ff_grads, parts))

    head_rows = shape(rows, lanes)
    got = call(
        norm_one_back_kernel,
        [row_shape, shape(8, width)] + [head_rows] * members,
        [ids, *parts, dz2, norm_rows, inverse, w_full, vec],
        "norm_one_back",
        smem=1,
    )
    dz1, grads_one = got[:2]
    grads = scatter(got[2:], "zl")

    share = shape(members, members, quarter, width)
    out_shares = call(
        out_weights_kernel,
        [share, share] if few else [shape(places, members, quarter, width)],
        [ids, att_rows, dz1],
        "out_weights",
        scratch=[pltpu.VMEM((places, members, quarter, width), f32)],
        smem=1,
    )
    def sum_cores(own, other, name):
        came = exchange(other, "core", 2, 1)
        return call(sum_cores_kernel, [shape(*own.shape[1:])] * members, [own, came], name)

    if few:
        out_shares = sum_cores(*out_shares, "sum_out")
        grads, out_shares, ff_grads = lax.optimization_barrier((grads, out_shares, ff_grads))
        out_shares = scatter(out_shares, GROUP)
    else:
        grads, ff_grads = lax.optimization_barrier((grads, ff_grads))
    ff_grads = lax.psum_scatter(ff_grads, LINES, scatter_dimension=0, tiled=False)
    out_came, out_core = exchange(out_rows, "y", 2, 1), exchange(out_rows, "core", 2, 1)
    back = attention_back(ids, kcat, vcat, pq, bias, att, den, grads, not few)
    back, out_came, out_core = lax.optimization_barrier((back, out_came, out_core))
    if few:
        back, out_shares = lax.optimization_barrier((back, out_shares))
        arrived = scatter(sum_cores(back[0], back[1], "sum_keys"), GROUP)
    else:
        arrived = lax.psum_scatter(back[0], PLANE, scatter_dimension=0, tiled=False)
        arrived = [arrived] + [jnp.zeros_like(arrived)] * 3
    dpq, dbias = back[-2:]
    out_grads = (
        call(sum_split_kernel, [shape(quarter, width)] * members, out_shares, "sum_out_plane")
        if few
        else [
            lax.dynamic_index_in_dim(
                lax.psum_scatter(out_shares[0], PLANE, scatter_dimension=0, tiled=False),
                zl_at ^ k,
                0,
                keepdims=False,
            )
            for k in range(members)
        ]
    )
    out_grads = scatter(out_grads, "zl")
    out_parts = [out_rows, out_core, out_came, exchange(out_came, "core", 2, 1)]
    output = place(ids, out_parts, "place_output")
    arrived, out_grads, output = lax.optimization_barrier((arrived, out_grads, output))

    got = call(
        qkv_back_kernel,
        [shape(queries, full)] + [row_shape] * members,
        [ids, *arrived, pq, dpq, kv, keys, proj, w_cols],
        "qkv_back",
        scratch=[pltpu.VMEM((full, queries), f32), pltpu.VMEM((queries, width), f32)],
        smem=1,
    )
    d_qkv = got[0]
    row_shares = got[1:]

    def split_plane(parts, piece, name):
        if few:
            return call(sum_split_kernel, [piece] * members, parts, name)
        part = lax.psum_scatter(parts[0], PLANE, scatter_dimension=0, tiled=False)
        return [
            lax.dynamic_index_in_dim(part, zl_at ^ k, 0, keepdims=False) for k in range(members)
        ]

    share = shape(members, members, quarter + 8, full)
    shares_out = call(
        functools.partial(qkv_weights_kernel, shard, span),
        [share, share] if few else [shape(places, members, quarter + 8, full)],
        [ids, x, d_qkv, dbias, grads_one],
        "qkv_weights",
        scratch=[pltpu.VMEM((places, members, quarter + 8, full), f32)],
        smem=1,
    )
    if few:
        shares_out = sum_cores(*shares_out, "sum_qkv")
    shares_out, row_shares = lax.optimization_barrier((shares_out, row_shares))
    mine = scatter(shares_out, GROUP) if few else shares_out
    row_parts = scatter(row_shares, "zl")
    mine, row_parts, ff_grads = lax.optimization_barrier((mine, row_parts, ff_grads))
    ff_grads = swap(ff_grads)
    (d_input_rows,) = call(sum_four_kernel, [row_shape], [*row_parts, dz1], "sum_rows")
    mine = split_plane(mine, shape(quarter + 8, full), "sum_qkv_plane")
    mine, d_input_rows = lax.optimization_barrier((mine, d_input_rows))
    mine = scatter(mine, "zl")
    input_came = exchange(d_input_rows, "y", 2, 1)
    mine, input_came, ff_grads = lax.optimization_barrier((mine, input_came, ff_grads))
    got = call(
        functools.partial(merge_kernel, shard),
        [
            shape(quarter, 4 * width),
            shape(*b_qkv.shape),
            shape(*position_bias.shape),
            shape(shard),
            shape(shard),
            shape(shard),
        ],
        [ids, *mine, *out_grads],
        "merge",
        scratch=[pltpu.VMEM((1, 3 * width), f32)],
        smem=1,
    )
    merged, d_b_qkv, d_position_bias, d_ln1_gain, d_ln1_bias, d_b_out = got
    ff_came, merged_came = exchange(ff_grads, "y", 2, 1), exchange(merged, "y", 2, 1)
    ff_came, merged_came = lax.optimization_barrier((ff_came, merged_came))

    def relayed(value, came):
        return [value, exchange(value, "core", 2, 1), came, exchange(came, "core", 2, 1)]

    d_inputs = place(ids, relayed(d_input_rows, input_came), "place_inputs")
    d_w_qkv, d_w_out = call(
        place_weights_kernel,
        [shape(*w_qkv.shape), shape(shard, width)],
        [ids, *relayed(merged, merged_came)],
        "place_weights",
        smem=1,
    )
    ff_parts = relayed(ff_grads, ff_came)
    got = call(
        functools.partial(place_ff_kernel, shard, down),
        [shape(shard, w_up.shape[1]), shape(*w_down.shape), shape(*b_up.shape)]
        + [shape(shard)] * 3,
        [ids, *ff_parts],
        "place_ff",
        scratch=[pltpu.VMEM((1, b_up.shape[0]), f32)],
        smem=1,
    )
    d_w_up, d_w_down, d_b_up, d_ln2_gain, d_ln2_bias, d_b_down = got

    return (
        output,
        d_inputs,
        d_position_bias,
        d_w_qkv,
        d_b_qkv,
        d_w_out,
        d_b_out,
        d_ln1_gain,
        d_ln1_bias,
        d_w_up,
        d_b_up,
        d_w_down,
        d_b_down,
        d_ln2_gain,
        d_ln2_bias,
    )


def solution(mesh):
    feats, wides = mesh.shape["feat"], mesh.shape["wide"]
    ys, zhs = feats // 2, wides // (2 * feats)
    fine = Mesh(mesh.devices.reshape(ys, 2, zhs, feats, 2), ("y", "core", "zh", "zl", "x"))
    wide = ("zh", "zl", "x")
    mat, vector, lane = P(wide, None), P(wide), P(None, wide)
    return jax.shard_map(
        functools.partial(body, ys, zhs),
        mesh=fine,
        in_specs=(mat, mat, P(None, FEAT), lane, mat, vector, mat, vector)
        + (vector, vector, mat, vector, mat, vector, vector, vector),
        out_specs=(mat, mat, lane, mat, vector, mat, vector, vector)
        + (vector, mat, vector, mat, vector, vector, vector),
        check_vma=False,
    )
```

```python
import functools
import math

import jax
import jax.numpy as jnp
from jax import lax
from jax.experimental import pallas as pl
from jax.experimental.pallas import tpu as pltpu
from jax.sharding import Mesh
from jax.sharding import PartitionSpec as P

HEADS = 12
HEAD_DIM = 64
FEATURES = 64
EPS = 1e-06
f32 = jnp.float32
bf16 = jnp.bfloat16

GROUP = ("y", "x")
FEAT = ("y", "core")
PLANE = ("zh", "x", "y", "core")
LINES = ("zh", "zl", "core")
CORE, MEMBER, OWN, HEAD, WIDE, PLACE = range(6)


def split(value):
    high = value.astype(bf16)
    return high, (value - high.astype(f32)).astype(bf16)


def dot(a, b, ca, cb):
    return lax.dot_general(a, b, (((ca,), (cb,)), ((), ())), preferred_element_type=f32)


def dot3s(a, b, ca, cb):
    return dot(a[0], b[0], ca, cb) + (dot(a[0], b[1], ca, cb) + dot(a[1], b[0], ca, cb))


def dot3(a, b, ca, cb):
    return dot3s(split(a), split(b), ca, cb)


def cost():
    return pl.CostEstimate(flops=1 << 20, bytes_accessed=1 << 10, transcendentals=0)


def tiled(dims):
    if len(dims) < 2:
        return 0
    return math.prod(dims[:-2]) * -(-dims[-2] // 8) * -(-dims[-1] // 128) * 4096


def call(kernel, outs, args, name, scratch=(), smem=0, room=8, limit=0, fetch=(), push=(), far=False, deep=False, late=None, stream=()):
    held = sum(tiled(ref.shape) for ref in scratch)
    held += sum(size for size in map(lambda a: tiled(a.shape), [*args, *outs]) if size > 6 << 20)
    if deep and not far:
        fetch = [i for i in range(smem, len(args)) if i not in stream]
        push, limit = range(len(outs)), 60 << 20
    fetch, push = tuple(fetch), tuple(push)
    near = [pltpu.VMEM(args[i].shape, args[i].dtype) for i in fetch]
    near += [pltpu.VMEM(outs[i].shape, outs[i].dtype) for i in push]
    held += sum(args[i].size * args[i].dtype.itemsize for i in fetch)
    held += sum(outs[i].size * outs[i].dtype.itemsize for i in push)
    count = len(args) + len(outs)
    flow = []
    if stream:
        first = args[stream[0]]
        flow = [
            pltpu.VMEM((len(stream),) + first.shape, first.dtype),
            pltpu.SemaphoreType.DMA((len(stream),)),
        ]

    def moved(*refs):
        whole, own = list(refs[:count]), refs[count : count + len(scratch)]
        spare, sems = refs[count + len(scratch) : -1 - len(flow)], refs[-1 - len(flow)]
        copies, after = [], []
        for at, (i, ref) in enumerate(zip(fetch, spare)):
            copies.append(pltpu.make_async_copy(whole[i], ref, sems.at[at]))
            whole[i] = ref
        for at, (i, ref) in enumerate(zip(push, spare[len(fetch) :])):
            i += len(args)
            after.append(pltpu.make_async_copy(ref, whole[i], sems.at[len(fetch) + at]))
            whole[i] = ref
        for copy in copies:
            copy.start()
        if flow:
            held, flow_sems = refs[-2:]
            for i, at in enumerate(stream):
                pltpu.make_async_copy(whole[at], held.at[i], flow_sems.at[i]).start()
        for i, copy in zip(fetch, copies):
            if late is None or i not in late:
                copy.wait()
        started = []

        def arrive(i):
            copies[fetch.index(i)].wait()

        def start(i):
            started.append(push.index(i))
            after[started[-1]].start()

        def wait(i):
            pltpu.make_async_copy(held.at[i], held.at[i], flow_sems.at[i]).wait()

        if flow:
            whole = [ref for i, ref in enumerate(whole) if i not in stream]
            kernel(*whole, *own, held=held, wait=wait, start=start)
        elif late is not None:
            kernel(*whole, *own, arrive=arrive, start=start)
        else:
            kernel(*whole, *own)
        for i, copy in enumerate(after):
            if i not in started:
                copy.start()
        for copy in after:
            copy.wait()

    def spec(i, which):
        return pl.BlockSpec(memory_space=pltpu.HBM if i in which else pltpu.VMEM)

    return pl.pallas_call(
        moved if near else kernel,
        out_shape=outs,
        in_specs=[pl.BlockSpec(memory_space=pltpu.SMEM)] * smem
        + [
            spec(i, range(len(args)) if far else (*fetch, *stream))
            for i in range(smem, len(args))
        ],
        out_specs=[spec(i, push) for i in range(len(outs))],
        scratch_shapes=list(scratch)
        + near
        + ([pltpu.SemaphoreType.DMA((len(near),))] if near else [])
        + flow,
        compiler_params=pltpu.CompilerParams(vmem_limit_bytes=limit or held + (room << 20)),
        cost_estimate=cost(),
        name=name,
    )(*args)


def when(condition):
    if isinstance(condition, bool):
        return lambda run: run() if condition else None
    return pl.when(condition)


def shape(*dims, dtype=f32):
    return jax.ShapeDtypeStruct(dims, dtype)


def by_case(value, count, run):
    for i in range(count):
        pl.when(value == i)(functools.partial(run, i))


def pack_qkv_kernel(rows, members, ids, *refs):
    count = (len(refs) - members - 3) // 2 + 1
    sources, pieces = refs[:count], refs[count : count + members]
    mixed, cot_out = refs[count + members : count + members + 2]
    held, sems = refs[count + members + 2 : -1], refs[-1]
    part = cot_out.shape[0]
    at = pl.multiple_of(ids[OWN] * part, 8)
    copies = [
        pltpu.make_async_copy(source.at[pl.ds(at, part)], target, sems.at[i])
        for i, (source, target) in enumerate(
            zip(sources[:2], (mixed.at[pl.ds(0, part)], cot_out))
        )
    ]
    copies += [
        pltpu.make_async_copy(source, target, sems.at[2 + i])
        for i, (source, target) in enumerate(zip(sources[2:], held))
    ]
    for copy in copies:
        copy.start()
    for copy in copies:
        copy.wait()
    w_ref, out_ref, bias_ref, b_ref, proj_ref, up_ref = held[:6]
    width = w_ref.shape[1] // 3
    lanes = width // members
    heads = bias_ref.shape[0] // members
    quarter = rows // members
    for piece in pieces:
        piece[quarter:, :] = jnp.zeros((8, 3 * lanes), f32)
        piece[quarter : quarter + 1, : b_ref.shape[0]] = b_ref[...].reshape(1, -1)
        for i, ref in enumerate(held[6:]):
            row, lane = (4, i) if i < 5 else (5, 0)
            piece[quarter + row : quarter + row + 1, lane * rows : (lane + 1) * rows] = ref[
                ...
            ].reshape(1, -1)
        piece[quarter + 5 : quarter + 6, rows : rows + up_ref.shape[0]] = up_ref[...].reshape(1, -1)
        per = 3 * lanes // HEAD_DIM
        for i in range(proj_ref.shape[0]):
            row, lane = quarter + 6 + i // per, HEAD_DIM * (i % per)
            piece[row : row + 1, lane : lane + HEAD_DIM] = proj_ref[i : i + 1]

    def own(f):
        first = quarter * f
        mixed[part : part + quarter] = out_ref[first : first + quarter]

        def head(t):
            for k, piece in enumerate(pieces):
                to = t ^ k
                for p in range(3):
                    at = width * p + lanes * to
                    piece[:quarter, lanes * p : lanes * (p + 1)] = w_ref[
                        first : first + quarter, at : at + lanes
                    ]
                piece[quarter + 1 : quarter + 1 + heads, : bias_ref.shape[1]] = bias_ref[
                    heads * to : heads * (to + 1)
                ]

        by_case(ids[HEAD], members, head)

    by_case(ids[OWN], members, own)


def pack_ff_kernel(members, down, ids, up_ref, down_ref, out):
    rows = up_ref.shape[0]
    blocks = up_ref.shape[1] // (members * down)

    def case(i):
        for w in range(blocks):
            at = (w * members + i) * down
            out[:rows, down * w : down * (w + 1)] = up_ref[:, at : at + down]
        out[rows : rows + down, :] = down_ref[down * i : down * (i + 1)]

    by_case(ids[OWN], members, case)


def plane_place(ids, members, few, i):
    if not few:
        zh, rest = divmod(i, 2 * members)
        return zh, rest // members, rest % members
    other, j = divmod(i, members)
    member = lax.bitwise_xor(ids[MEMBER], j)
    return 0, lax.rem(member, 2), 2 * lax.div(member, 2) + lax.bitwise_xor(ids[CORE], other)


def qkv_kernel(rows, members, spans, few, ids, *refs, arrive=None, start=None):
    mixed, refs = refs[0], refs[1:]
    w_out, x_out, pq_out, kv_out, key_out, proj_out, bias_out, vec_out, extra, held, directions = refs[-11:]
    slabs = refs[:-11]
    slabs = list(slabs) if few else [slabs[0].at[i] for i in range(slabs[0].shape[0])]
    width = x_out.shape[1]
    blocks = extra.shape[0]
    full = w_out.shape[1]
    lanes = full // 3
    heads = lanes // HEAD_DIM
    quarter = rows // members
    part = x_out.shape[0] // members
    for z in range(members):
        x_out[part * z : part * (z + 1), :] = mixed[z, :part]
    for i, slab in enumerate(slabs):
        if arrive is not None and few:
            arrive(2 + i)
        zh, x, f = plane_place(ids, members, few, i)
        for k in range(members):
            w = 2 * (members * zh + lax.bitwise_xor(ids[HEAD], k)) + x
            if i < 2 if few else f == 0:
                extra[w] = slab[k, quarter:]
            if quarter % 8 == 0:
                at = pl.multiple_of(w * rows + f * quarter, 8)
                w_out[pl.ds(at, quarter), :] = slab[k, :quarter]
            else:
                held[w * members + f] = slab[k, :quarter]
    if quarter % 8:
        for i in range(held.shape[0]):
            w_out[quarter * i : quarter * (i + 1)] = held[i]

    share = FEATURES // members
    per = full // HEAD_DIM
    for i, slab in enumerate(slabs):
        zh, x, f = plane_place(ids, members, few, i)
        if few or (zh, x) == (0, 0):
            for r in range(share):
                at, lane = quarter + 6 + r // per, HEAD_DIM * (r % per)
                directions[share * f + r] = slab[0, at : at + 1, lane : lane + HEAD_DIM]
    for r in range(FEATURES):
        proj_out[r : r + 1, :] = directions[r]
    bias_out[...] = jnp.zeros_like(bias_out)
    b_row = []
    for w in range(blocks):
        b_row.append(extra[w, 0:1, : spans[0]])
        count = spans[1]
        bias_out[:heads, count * w : count * (w + 1)] = extra[w, 1 : 1 + heads, :count]
        for i in range(6):
            row, lane = (4, i) if i < 5 else (5, 0)
            vec_out[1 + i : 2 + i, rows * w : rows * (w + 1)] = extra[
                w, row : row + 1, lane * rows : (lane + 1) * rows
            ]
    vec_out[7:8] = jnp.zeros((1, width), f32)
    b_row = jnp.concatenate(b_row, axis=1)

    def unit(g):
        count = spans[2]
        for w in range(blocks):
            vec_out[0:1, count * w : count * (w + 1)] = extra[
                w, 5:6, rows + count * g : rows + count * (g + 1)
            ]

    by_case(ids[MEMBER], members, unit)
    if start is not None:
        for i in (0, 1, 5, 6, 7):
            start(i)
    qkv = dot3(x_out[...], w_out[...], 1, 0)
    scale = HEAD_DIM**-0.25
    proj = split(proj_out[...])

    def head(t):
        bias = [b_row[:, width * p + lanes * t : width * p + lanes * (t + 1)] for p in range(3)]
        turned = (qkv + jnp.concatenate(bias, axis=1)).T
        for h in range(heads):
            lo, hi = HEAD_DIM * h, HEAD_DIM * (h + 1)
            q = turned[lo:hi] * scale
            k = turned[lanes + lo : lanes + hi] * scale
            pq_out[lo:hi] = jnp.exp(dot3s(proj, split(q), 1, 0))
            pk = dot3s(proj, split(k), 1, 0) - 0.5 * jnp.sum(k * k, axis=0, keepdims=True)
            kv_out[128 * h : 128 * h + 64] = jnp.exp(pk)
            kv_out[128 * h + 64 : 128 * h + 128] = turned[2 * lanes + lo : 2 * lanes + hi]
            key_out[lo:hi] = k

    by_case(ids[HEAD], members, head)


def rolled_rows(table, row):
    wide = jnp.broadcast_to(row, (8, row.shape[1]))
    return pltpu.roll(wide, 0, 1, stride=1, stride_axis=0)


def make_tables(tables, bias_ref, heads):
    length = bias_ref.shape[1]
    for h in range(heads):
        rows = rolled_rows(None, jnp.exp(bias_ref[h : h + 1]))
        tables[0, 8 * h : 8 * h + 8] = rows
        tables[1, 8 * h : 8 * h + 8] = pltpu.roll(rows, length - 64, 1)


def factor_tile(windows):
    first = lax.broadcasted_iota(jnp.int32, (8, 128), 1) < 64
    pairs = {}
    for g in range(8):
        for d in range(-3, 3):
            low = pltpu.roll(windows[d + 3], (8 * g + 64) % 128, 1)
            high = windows[d + 4] if g == 0 else pltpu.roll(windows[d + 4], 8 * g, 1)
            pairs[d, g] = jnp.where(first, low, high)
    rows = []
    for z in range(4):
        for g in range(8):
            rows.append(jnp.concatenate([pairs[-z, g], pairs[2 - z, g]], axis=1))
    return jnp.concatenate(rows, axis=0)


def window_sums(pairs):
    first = lax.broadcasted_iota(jnp.int32, (8, 128), 1) < 64
    sums = [jnp.zeros((8, 128), f32) for _ in range(7)]
    for g in range(8):
        for d in range(-3, 3):
            total = None
            for z in range(4):
                for p in range(2):
                    if 2 * p - z == d:
                        term = pairs[64 * z + 8 * g : 64 * z + 8 * g + 8, 128 * p : 128 * p + 128]
                        total = term if total is None else total + term
            low = pltpu.roll(jnp.where(first, total, 0.0), 64 - 8 * g, 1)
            high = jnp.where(first, 0.0, total)
            sums[d + 3] = sums[d + 3] + low
            sums[d + 4] = sums[d + 4] + (high if g == 0 else pltpu.roll(high, 128 - 8 * g, 1))
    return sums


def window_start(ids, members, groups, seg, length, n):
    if groups == 1:
        other, j = n // members, n % members
        member = lax.bitwise_xor(ids[MEMBER], j)
        zh, x = ids[PLACE] * 0, lax.rem(member, 2)
        f = 2 * lax.div(member, 2) + lax.bitwise_xor(ids[CORE], other)
    else:
        zh, x, f = n // (2 * members), lax.rem(lax.div(n, members), 2), lax.rem(n, members)
    own = ids[PLACE]
    away = 8 * members * (lax.div(own, 2 * members) - zh)
    away += members * (lax.rem(lax.div(own, members), 2) - x) + ids[OWN] - f
    start = away + length // (2 * seg) - 1
    odd = lax.rem(start, 2)
    return start - odd, odd


def window_at(start, d):
    return pl.multiple_of(start * 64 + 512 * d, 128)


def split_block(block, h, kcat, vcat):
    for part, cat in ((0, kcat), (64, vcat)):
        high, low = split(block[128 * h + part : 128 * h + part + 64])
        cat[h, 0:64] = high
        cat[h, 64:128] = low
        cat[h, 128:192] = high


def attention_kernel(groups, blocks, ids, *refs, held=None, wait=None, start=None):
    if groups > 1:
        held, refs = refs[0], refs[1:]
    pq_ref, bias_ref, att_out, den_out = refs[:4]
    parts = refs[4:8]
    tables, qcat, out_rows, kcat, vcat = refs[8:]
    heads = pq_ref.shape[0] // 64
    queries = pq_ref.shape[1]
    step = pl.program_id(0) if groups > 1 else 0

    @when(step == 0)
    def _():
        make_tables(tables, bias_ref, heads)
        for h in range(heads):
            high, low = split(pq_ref[64 * h : 64 * h + 64])
            qcat[h, 0:64] = high
            qcat[h, 64:128] = high
            qcat[h, 128:192] = low
        att_out[...] = jnp.zeros_like(att_out)
        den_out[...] = jnp.zeros_like(den_out)

    def advance(n, carry):
        first, odd = window_start(ids, 4, groups, 64, bias_ref.shape[1], step * blocks + n)
        if wait is not None:
            wait(n)
        for h in range(heads):
            split_block(held.at[n], h, kcat.at[n], vcat.at[n])
            scores = dot(kcat[n, h], qcat[h], 0, 0)
            rows = slice(8 * h, 8 * h + 8)
            windows = [
                tables[odd, rows, pl.ds(window_at(first, d), 128)] for d in range(-3, 4)
            ]
            weight = scores * factor_tile(windows)
            high, low = split(weight)
            both = dot(vcat[n, h, 0:128], high, 1, 0)
            more = dot(vcat[n, h, 0:64], low, 1, 0)
            att_out[64 * h : 64 * h + 64] += both[0:64] + both[64:128] + more
            den_out[h : h + 1] += jnp.sum(weight, axis=0, keepdims=True)
        return carry

    lax.fori_loop(0, blocks, advance, 0, unroll=2)

    @when(step == groups - 1)
    def _():
        for h in range(heads):
            att_out[64 * h : 64 * h + 64] = att_out[64 * h : 64 * h + 64] / den_out[h : h + 1]
        out_rows[...] = att_out[...].T
        rows = queries // 4
        for k in range(4):
            first = pl.multiple_of(lax.bitwise_xor(ids[HEAD], k) * rows, 8)
            parts[k][...] = out_rows[pl.ds(first, rows), :]


def attention(ids, kv, pq, window):
    stacked = not isinstance(kv, list)
    count = kv.shape[0] if stacked else len(kv)
    blocks = 8 if stacked else count
    groups = count // blocks
    queries = pq.shape[1]
    heads = pq.shape[0] // 64
    rows = shape(queries // 4, heads * 64)
    outs = [shape(heads * 64, queries), shape(8, queries)] + [rows] * 4
    scratch = [
        pltpu.VMEM((2, 8 * heads, window.shape[1]), f32),
        pltpu.VMEM((heads, 192, queries), bf16),
        pltpu.VMEM((queries, heads * 64), f32),
        pltpu.VMEM((blocks, heads, 192, queries), bf16),
        pltpu.VMEM((blocks, heads, 192, queries), bf16),
    ]
    kernel = functools.partial(attention_kernel, groups, blocks)
    if not stacked:
        args = [ids, *kv, pq, window]
        stream = range(1, 1 + count)
        return call(kernel, outs, args, "attention", scratch, 1, deep=True, stream=stream)
    whole = lambda a: pl.BlockSpec(a.shape, lambda g, nd=len(a.shape): (0,) * nd)
    smem = pl.BlockSpec(memory_space=pltpu.SMEM)
    kv_spec = pl.BlockSpec((blocks,) + kv.shape[1:], lambda g: (g, 0, 0))
    return pl.pallas_call(
        kernel,
        grid=(groups,),
        out_shape=outs,
        in_specs=[smem, kv_spec, whole(pq), whole(window)],
        out_specs=[whole(a) for a in outs],
        scratch_shapes=scratch,
        compiler_params=pltpu.CompilerParams(vmem_limit_bytes=52 << 20),
        name="attention",
    )(ids, kv, pq, window)


def attention_back_kernel(groups, blocks, ids, *refs, held=None, wait=None, start=None):
    if groups > 1:
        held, refs = refs[0], refs[1:]
    pq_ref, bias_ref, att_ref, den_ref = refs[:4]
    grads = refs[4:8]
    if groups == 1:
        own, other, dpq_out, dbias_out = refs[8:12]
    else:
        dkv, dpq_out, dbias_out = refs[8:11]
    tables, qcat, gcat, gden, diag, grad_rows, kcat, vcat = refs[-8:]
    heads = pq_ref.shape[0] // 64
    queries = pq_ref.shape[1]
    step = pl.program_id(0) if groups > 1 else 0

    @when(step == 0)
    def _():
        rows = queries // 4
        for k in range(4):
            first = pl.multiple_of(lax.bitwise_xor(ids[HEAD], k) * rows, 8)
            grad_rows[pl.ds(first, rows), :] = grads[k][...]
        make_tables(tables, bias_ref, heads)
        d_att = grad_rows[...].T
        gden[...] = jnp.zeros_like(gden)
        for h in range(heads):
            lo, hi = 64 * h, 64 * h + 64
            for value, cat in ((pq_ref[lo:hi], qcat), (d_att[lo:hi] / den_ref[h : h + 1], gcat)):
                high, low = split(value)
                cat[h, 0:64] = high
                cat[h, 64:128] = high
                cat[h, 128:192] = low
            gden[h : h + 1] = -(
                jnp.sum(d_att[lo:hi] * att_ref[lo:hi], axis=0, keepdims=True) / den_ref[h : h + 1]
            )
        dpq_out[...] = jnp.zeros_like(dpq_out)
        diag[...] = jnp.zeros_like(diag)

    def advance(dkv, first, n, carry):
        begin, odd = window_start(ids, 4, groups, 64, bias_ref.shape[1], step * blocks + n)
        if wait is not None:
            wait(n)
        for h in range(heads):
            split_block(held.at[n], h, kcat.at[n], vcat.at[n])
            scores = dot(kcat[n, h], qcat[h], 0, 0)
            rows = slice(8 * h, 8 * h + 8)
            factor = factor_tile(
                [tables[odd, rows, pl.ds(window_at(begin, d), 128)] for d in range(-3, 4)]
            )
            d_weight = dot(vcat[n, h], gcat[h], 0, 0) + gden[h : h + 1]
            w_high, w_low = split(scores * factor)
            e_high, e_low = split(d_weight * factor)
            pairs = d_weight * scores
            both = dot(gcat[h, 64:192], w_high, 1, 1)
            dv = both[0:64] + both[64:128] + dot(gcat[h, 0:64], w_low, 1, 1)
            both = dot(qcat[h, 64:192], e_high, 1, 1)
            dk = both[0:64] + both[64:128] + dot(qcat[h, 0:64], e_low, 1, 1)
            both = dot(kcat[n, h, 0:128], e_high, 1, 0)
            dq = both[0:64] + both[64:128] + dot(kcat[n, h, 0:64], e_low, 1, 0)
            dpq_out[64 * h : 64 * h + 64] += dq
            dkv[n - first, 128 * h : 128 * h + 64] = dk
            dkv[n - first, 128 * h + 64 : 128 * h + 128] = dv
            for i, total in enumerate(window_sums(pairs)):
                diag[odd, rows, pl.ds(window_at(begin, i - 3), 128)] += total
        return carry

    if groups == 1:
        half = blocks // 2
        lax.fori_loop(half, blocks, functools.partial(advance, other, half), 0, unroll=2)
        if start is not None:
            start(1)
        lax.fori_loop(0, half, functools.partial(advance, own, 0), 0, unroll=2)
        if start is not None:
            start(0)
    else:
        lax.fori_loop(0, blocks, functools.partial(advance, dkv, 0), 0)

    @when(step == groups - 1)
    def _():
        length = diag.shape[2]
        dbias_out[...] = jnp.zeros_like(dbias_out)
        for h in range(heads):
            both = diag[0, 8 * h : 8 * h + 8] + pltpu.roll(diag[1, 8 * h : 8 * h + 8], 64, 1)
            total = both[0:1]
            for s in range(1, 8):
                total = total + pltpu.roll(both[s : s + 1], length - s, 1)
            dbias_out[h : h + 1] = total * jnp.exp(bias_ref[h : h + 1])


def attention_back(ids, kv, pq, window, att, den, grads):
    stacked = not isinstance(kv, list)
    count = kv.shape[0] if stacked else len(kv)
    blocks = 8 if stacked else count
    groups = count // blocks
    queries = pq.shape[1]
    heads = pq.shape[0] // 64
    outs = [shape(heads * 64, queries), shape(8, window.shape[1])]
    scratch = [
        pltpu.VMEM((2, 8 * heads, window.shape[1]), f32),
        pltpu.VMEM((heads, 192, queries), bf16),
        pltpu.VMEM((heads, 192, queries), bf16),
        pltpu.VMEM((8, queries), f32),
        pltpu.VMEM((2, 8 * heads, window.shape[1]), f32),
        pltpu.VMEM((queries, heads * 64), f32),
        pltpu.VMEM((blocks, heads, 192, queries), bf16),
        pltpu.VMEM((blocks, heads, 192, queries), bf16),
    ]
    kernel = functools.partial(attention_back_kernel, groups, blocks)
    small = [pq, window, att, den] + list(grads)
    if not stacked:
        half = shape(count // 2, heads * 128, queries)
        return call(
            kernel,
            [half, half] + outs,
            [ids, *kv] + small,
            "attention_back",
            scratch,
            1,
            deep=True,
            stream=range(1, 1 + count),
        )
    whole = lambda a: pl.BlockSpec(a.shape, lambda g, nd=len(a.shape): (0,) * nd)
    smem = pl.BlockSpec(memory_space=pltpu.SMEM)
    kv_spec = pl.BlockSpec((blocks, heads * 128, queries), lambda g: (g, 0, 0))
    return pl.pallas_call(
        kernel,
        grid=(groups,),
        out_shape=[shape(count, heads * 128, queries)] + outs,
        in_specs=[smem, kv_spec] + [whole(a) for a in small],
        out_specs=[kv_spec] + [whole(a) for a in outs],
        scratch_shapes=scratch,
        compiler_params=pltpu.CompilerParams(vmem_limit_bytes=52 << 20),
        name="attention_back",
    )(ids, kv, *small)


def normed(value):
    mean = jnp.mean(value, axis=1, keepdims=True)
    centered = value - mean
    var = jnp.mean(centered * centered, axis=1, keepdims=True)
    inverse = lax.rsqrt(var + EPS)
    return centered * inverse, inverse


def norm_back(upstream, n, inverse, gain):
    scaled = gain * upstream
    mean = jnp.mean(scaled, axis=1, keepdims=True)
    slope = jnp.mean(scaled * n, axis=1, keepdims=True)
    return (scaled - mean - n * slope) * inverse


def colsum(value):
    return jnp.sum(value, axis=0, keepdims=True)


def weights_out_kernel(rows, ids, *refs):
    out = refs[-1]
    members, quarter, _ = refs[0].shape
    for i, ref in enumerate(refs[:-1]):
        other, j = divmod(i, members)
        place = lax.bitwise_xor(ids[MEMBER], j)
        f = 2 * lax.div(place, 2) + lax.bitwise_xor(ids[CORE], other)
        for k in range(members):
            w = 2 * k + lax.rem(place, 2)
            out[pl.ds(pl.multiple_of(rows * w + quarter * f, 8), quarter), :] = ref[k]


def norm_one_kernel(ids, a0, a1, a2, a3, x_ref, w_ref, vec_ref, *refs):
    first_out, n_out, inverse_out, att_out = refs
    lanes = a0.shape[1]

    def head(t):
        for k, ref in enumerate((a0, a1, a2, a3)):
            at = lanes * (t ^ k)
            att_out[:, at : at + lanes] = ref[...]

    by_case(ids[HEAD], 4, head)
    projected = dot3(att_out[...], w_ref[...], 1, 0)
    n, inverse = normed(x_ref[: a0.shape[0]] + (projected + vec_ref[1:2]))
    first_out[...] = n * vec_ref[2:3] + vec_ref[3:4]
    n_out[...] = n
    inverse_out[...] = jnp.broadcast_to(inverse, inverse_out.shape)


def norm_two_kernel(p0, p1, p2, p3, first_ref, cot_ref, vec_ref, rows_out, dz_out, grads_out):
    value = first_ref[...] + ((p0[...] + p1[...]) + (p2[...] + p3[...]) + vec_ref[4:5])
    n, inverse = normed(value)
    rows_out[...] = n * vec_ref[5:6] + vec_ref[6:7]
    up = cot_ref[...]
    dz = norm_back(up, n, inverse, vec_ref[5:6])
    dz_out[...] = dz
    grads_out[...] = jnp.zeros_like(grads_out)
    grads_out[0:1] = colsum(up * n)
    grads_out[1:2] = colsum(up)
    grads_out[2:3] = colsum(dz)


def norm_one_back_kernel(ids, p0, p1, p2, p3, dz_ref, n_ref, inverse_ref, w_ref, vec_ref, *refs):
    dz_out, grads_out = refs[:2]
    parts = refs[2:6]
    up = dz_ref[...] + ((p0[...] + p1[...]) + (p2[...] + p3[...]))
    n = n_ref[...]
    dz = norm_back(up, n, inverse_ref[:, 0:1], vec_ref[2:3])
    dz_out[...] = dz
    grads_out[...] = jnp.zeros_like(grads_out)
    grads_out[0:1] = colsum(up * n)
    grads_out[1:2] = colsum(up)
    grads_out[2:3] = colsum(dz)
    d_att = dot3(dz, w_ref[...], 1, 1)
    lanes = parts[0].shape[1]

    def case(i):
        for k in range(4):
            at = lanes * (i ^ k)
            parts[k][...] = d_att[:, at : at + lanes]

    by_case(ids[HEAD], 4, case)


def stack_rest_kernel(first, source, out):
    out[...] = source[:, first : first + out.shape[1]]


def stack_kernel(*refs):
    for i, ref in enumerate(refs[:-1]):
        refs[-1][i] = ref[...]


def stack_rows(target, refs):
    rows = refs[0].shape[0]
    for k, ref in enumerate(refs):
        target[rows * k : rows * (k + 1), :] = ref[...]


def prepare_kernel(rows_up, slab, up_high, up_low, down_high, down_low):
    for first, count, high, low in (
        (0, rows_up, up_high, up_low),
        (rows_up, slab.shape[1] - rows_up, down_high, down_low),
    ):
        pieces = [slab[w, first : first + count] for w in range(slab.shape[0])]
        high[...], low[...] = split(jnp.concatenate(pieces, axis=0))


def forward_kernel(f0, f1, f2, f3, up_high, up_low, down_high, down_low, vec_ref, *refs):
    pre_out, first_out = refs[:2]
    parts = refs[2:6]
    stack_rows(first_out, (f0, f1, f2, f3))
    pre = dot3s(split(first_out[...]), (up_high[...], up_low[...]), 1, 0) + vec_ref[0:1]
    pre_out[...] = pre
    hidden = 0.5 * pre * (1.0 + lax.erf(pre * (0.5**0.5)))
    branch = dot3s(split(hidden), (down_high[...], down_low[...]), 1, 0)
    rows = f0.shape[0]
    for k in range(4):
        parts[k][...] = branch[rows * k : rows * (k + 1)]


def backward_kernel(z0, z1, z2, z3, pre_ref, up_high, up_low, down_high, down_low, *refs):
    dz_out, d_pre_out = refs[:2]
    parts = refs[2:6]
    stack_rows(dz_out, (z0, z1, z2, z3))
    d_hidden = dot3s(split(dz_out[...]), (down_high[...], down_low[...]), 1, 1)
    pre = pre_ref[...]
    density = jnp.exp(-0.5 * pre * pre) * ((2.0 * jnp.pi) ** -0.5)
    d_pre = d_hidden * (0.5 * (1.0 + lax.erf(pre * (0.5**0.5))) + pre * density)
    d_pre_out[...] = d_pre
    d_first = dot3s(split(d_pre), (up_high[...], up_low[...]), 1, 1)
    rows = z0.shape[0]
    for k in range(4):
        parts[k][...] = d_first[rows * k : rows * (k + 1)]


def ff_weights_kernel(rows_up, rows_down, first_ref, d_pre_ref, pre_ref, dz_ref, grads_ref, out):
    pre = pre_ref[...]
    hidden = 0.5 * pre * (1.0 + lax.erf(pre * (0.5**0.5)))
    d_pre = d_pre_ref[...]
    blocks = out.shape[0]
    base = rows_up + rows_down
    out[:, base:, :] = jnp.zeros((blocks, 8, out.shape[2]), f32)
    d_b_up = colsum(d_pre)
    up = dot3(first_ref[...], d_pre, 0, 0)
    down = dot3(hidden, dz_ref[...], 0, 0)
    for w in range(blocks):
        out[w, :rows_up, :] = up[rows_up * w : rows_up * (w + 1)]
        out[w, rows_up:base, :] = down[rows_down * w : rows_down * (w + 1)]
        out[w, base : base + 1, :rows_down] = d_b_up[:, rows_down * w : rows_down * (w + 1)]
        for i in range(3):
            out[w, base + 1 + i : base + 2 + i, :rows_up] = grads_ref[
                i : i + 1, rows_up * w : rows_up * (w + 1)
            ]


def shares(held, ids, outs):
    if len(outs) == 1:
        outs[0][...] = held[...]
        return
    members = held.shape[1]
    for other, out in enumerate(outs):
        core = lax.bitwise_xor(ids[CORE], other)
        for j in range(members):
            place = lax.bitwise_xor(ids[MEMBER], j)
            at = lax.rem(place, 2) * members + 2 * lax.div(place, 2) + core
            for k in range(members):
                out[j, k] = held[at, lax.bitwise_xor(ids[HEAD], k)]


def out_weights_kernel(ids, att_ref, dz_ref, *refs):
    outs, held = refs[:-1], refs[-1]
    places, members, quarter, _ = held.shape
    value = dot3(att_ref[...], dz_ref[...], 0, 0)
    for place in range(places):
        zh, rest = divmod(place, 2 * members)
        x, f = divmod(rest, members)
        for z in range(members):
            at = ((2 * (members * zh + z) + x) * members + f) * quarter
            held[place, z] = value[at : at + quarter]
    shares(held, ids, outs)


def sum_cores_kernel(own, came, *outs):
    for j, out in enumerate(outs):
        out[...] = own[j] + came[j]


def qkv_back_kernel(ids, d0, d1, d2, d3, pq_ref, dpq_ref, kv_ref, key_ref, proj_ref, w_ref, *refs):
    d_qkv_out, rows_out, turned = refs
    heads = pq_ref.shape[0] // 64
    width = heads * 64
    scale = HEAD_DIM**-0.25
    proj = split(proj_ref[...])
    dkv = (d0[...] + d1[...]) + (d2[...] + d3[...])
    for h in range(heads):
        lo, hi = 64 * h, 64 * h + 64
        turned[lo:hi] = scale * dot3s(proj, split(dpq_ref[lo:hi] * pq_ref[lo:hi]), 0, 0)
        pk = dkv[128 * h : 128 * h + 64] * kv_ref[128 * h : 128 * h + 64]
        turned[width + lo : width + hi] = scale * (
            dot3s(proj, split(pk), 0, 0) - key_ref[lo:hi] * colsum(pk)
        )
        turned[2 * width + lo : 2 * width + hi] = dkv[128 * h + 64 : 128 * h + 128]
    d_qkv = turned[...].T
    d_qkv_out[...] = d_qkv
    rows_out[...] = dot3(d_qkv, w_ref[...], 1, 1)


def qkv_weights_kernel(rows, span, ids, x_ref, d_ref, dbias_ref, grads_ref, *refs):
    outs, held = refs[:-1], refs[-1]
    d_qkv = d_ref[...]
    places, members, _, full = held.shape
    quarter = rows // members
    held[:, :, quarter:, :] = jnp.zeros((places, members, 8, full), f32)
    d_b = colsum(d_qkv)
    weights = dot3(x_ref[...], d_qkv, 0, 0)
    for place in range(places):
        zh, rest = divmod(place, 2 * members)
        x, f = divmod(rest, members)
        for z in range(members):
            w = 2 * (members * zh + z) + x
            at = (w * members + f) * quarter
            held[place, z, :quarter] = weights[at : at + quarter]
            held[place, z, quarter : quarter + 1] = d_b
            for i in range(3):
                held[place, z, quarter + 1 : quarter + 2, rows * i : rows * (i + 1)] = grads_ref[
                    i : i + 1, rows * w : rows * (w + 1)
                ]
            held[place, z, quarter + 2 : quarter + 5, :span] = dbias_ref[
                0:3, span * w : span * (w + 1)
            ]
    shares(held, ids, outs)


def merge_kernel(rows, skip, ids, r0, r1, r2, r3, w0, w1, w2, w3, out, b_own, bias_out, *rest):
    refs, b_out = (r0, r1, r2, r3), rest[3]
    members = len(refs)
    lanes = r0.shape[1] // 3
    width = lanes * members
    span = bias_out.shape[1]
    quarter = rows // members
    total = (r0[quarter + 1 : quarter + 2] + r1[quarter + 1 : quarter + 2]) + (
        r2[quarter + 1 : quarter + 2] + r3[quarter + 1 : quarter + 2]
    )
    for i in range(3):
        rest[i][...] = total[:, rows * i : rows * (i + 1)].reshape(rows)
    last = slice(skip, skip + quarter)
    out[:, 3 * width :] = (w0[last] + w1[last]) + (w2[last] + w3[last])

    def head(t):
        for k, ref in enumerate(refs):
            f = t ^ k
            for p in range(3):
                at = width * p + lanes * f
                out[:, at : at + lanes] = ref[:quarter, lanes * p : lanes * (p + 1)]
                b_out[:, at : at + lanes] = ref[
                    quarter : quarter + 1, lanes * p : lanes * (p + 1)
                ]
            bias_out[3 * f : 3 * f + 3] = ref[quarter + 2 : quarter + 5, :span]

    by_case(ids[HEAD], members, head)
    count = b_own.shape[0]

    def place(w):
        b_own[...] = b_out[:, count * w : count * (w + 1)].reshape(count)

    by_case(ids[WIDE], b_out.shape[1] // count, place)


def place_weights_kernel(ids, r0, r1, r2, r3, w_out, wo_out):
    quarter = r0.shape[0]
    full = w_out.shape[1]

    def own(f):
        for k, ref in enumerate((r0, r1, r2, r3)):
            at = quarter * (f ^ k)
            w_out[at : at + quarter] = ref[:, :full]
            wo_out[at : at + quarter] = ref[:, full:]

    by_case(ids[OWN], 4, own)


def sum_split_kernel(a, b, c, d, *outs):
    for k, out in enumerate(outs):
        out[...] = (a[k] + b[k]) + (c[k] + d[k])


def sum_mixed_kernel(ids, a, b, c, d, rows_ref, *outs):
    rows = rows_ref.shape[0] // len(outs)
    quarter = a.shape[1]
    for k, out in enumerate(outs):
        at = pl.multiple_of(lax.bitwise_xor(ids[HEAD], k) * rows, 8)
        out[:rows] = rows_ref[pl.ds(at, rows), :]
        out[rows : rows + quarter] = (a[k] + b[k]) + (c[k] + d[k])


def sum_kernel(*refs):
    total = refs[0][...]
    for ref in refs[1:-1]:
        total = total + ref[...]
    refs[-1][...] = total


def sum_four_kernel(p0, p1, p2, p3, dz_ref, out):
    rows = out.shape[0]
    out[...] = dz_ref[...] + ((p0[:rows] + p1[:rows]) + (p2[:rows] + p3[:rows]))


def place_kernel(ids, r0, r1, r2, r3, out):
    rows = r0.shape[0]
    for k, ref in enumerate((r0, r1, r2, r3)):
        out[pl.ds(pl.multiple_of(lax.bitwise_xor(ids[OWN], k) * rows, 8), rows), :] = ref[...]


def place_ff_kernel(rows, down, ids, r0, r1, r2, r3, up_out, down_out, b_all, v0, v1, v2, b_out):
    refs = (r0, r1, r2, r3)
    members = len(refs)
    base = rows + down
    total = r0[base + 1 : base + 4, :rows] + r1[base + 1 : base + 4, :rows]
    total = total + (r2[base + 1 : base + 4, :rows] + r3[base + 1 : base + 4, :rows])
    for i, out in enumerate((v0, v1, v2)):
        out[...] = total[i : i + 1].reshape(rows)

    def own(i):
        for k, ref in enumerate(refs):
            f = i ^ k
            for w in range(up_out.shape[1] // (members * down)):
                at = (w * members + f) * down
                up_out[:, at : at + down] = ref[:rows, down * w : down * (w + 1)]
            down_out[down * f : down * (f + 1)] = ref[rows:base]
            b_out[:, down * f : down * (f + 1)] = ref[base : base + 1, :down]

    by_case(ids[OWN], members, own)
    b_all[...] = b_out[...].reshape(b_all.shape)


def exchange(value, axes, count, k):
    return lax.ppermute(value, axes, [(i, i ^ k) for i in range(count)])


def swap(value):
    return lax.ppermute(value, ("core", "x"), [(0, 0), (1, 2), (2, 1), (3, 3)])


def place(ids, values, name):
    return call(
        place_kernel,
        [shape(len(values) * values[0].shape[0], values[0].shape[1])],
        [ids, *values],
        name,
        smem=1,
    )[0]


def gather(value, axes, count):
    return [value] + [exchange(value, axes, count, k) for k in range(1, count)]


def relay(value):
    came = exchange(value, "y", 2, 1)
    return [value, exchange(value, "core", 2, 1), came, exchange(came, "core", 2, 1)]


def scatter(parts, axes):
    return [parts[0]] + [exchange(parts[k], axes, len(parts), k) for k in range(1, len(parts))]


def body(
    ys,
    zhs,
    inputs,
    cotangent,
    random_proj,
    position_bias,
    w_qkv,
    b_qkv,
    w_out,
    b_out,
    ln1_gain,
    ln1_bias,
    w_up,
    b_up,
    w_down,
    b_down,
    ln2_gain,
    ln2_bias,
):
    members = 2 * ys
    blocks = 2 * zhs * members
    places = 2 * zhs * members
    few = zhs == 1
    core = lax.axis_index("core")
    x_at, y_at = lax.axis_index("x"), lax.axis_index("y")
    zh_at, zl_at = lax.axis_index("zh"), lax.axis_index("zl")
    feat = 2 * y_at + core
    group = 2 * y_at + x_at
    wide = 2 * (members * zh_at + zl_at) + x_at
    place_at = (2 * zh_at + x_at) * members + feat
    ids = jnp.stack([core, group, feat, zl_at, wide, place_at]).astype(jnp.int32)
    queries, width = inputs.shape
    rows = queries // members
    shard = w_qkv.shape[0]
    quarter = shard // members
    down = w_down.shape[0] // members
    heads = HEADS // members
    lanes = heads * HEAD_DIM
    span = position_bias.shape[1]
    full = 3 * lanes
    length = queries * blocks
    row_shape = shape(rows, width)

    packed = [w_qkv, w_out, position_bias, b_qkv, random_proj.T]
    packed += [b_up, b_out, ln1_gain, ln1_bias, b_down, ln2_gain, ln2_bias]
    got = call(
        functools.partial(pack_qkv_kernel, shard, members),
        [shape(quarter + 8, full)] * members + [shape(rows + -(-quarter // 8) * 8, width), row_shape],
        [ids, inputs, cotangent] + packed,
        "pack_qkv",
        scratch=[pltpu.VMEM(a.shape, f32) for a in packed]
        + [pltpu.SemaphoreType.DMA((len(packed) + 2,))],
        smem=1,
        limit=60 << 20,
        far=True,
    )
    mixed, cot_rows = got[members:]
    pieces = scatter(got[:members], "zl")
    pack_ids, _ = lax.optimization_barrier((ids, mixed))
    (ff_slab,) = call(
        functools.partial(pack_ff_kernel, members, down),
        [shape(shard + down, width)],
        [pack_ids, w_up, w_down],
        "pack_ff",
        smem=1,
    )
    ff_slab = swap(ff_slab)
    mixed_all = lax.all_gather(mixed, "zl", axis=0)
    pieces, ff_slab = lax.optimization_barrier((pieces, ff_slab))
    (slab,) = call(
        stack_kernel, [shape(members, quarter + 8, full)], pieces, "stack_pieces"
    )
    if few:
        slabs = gather(slab, GROUP, members)
    else:
        slabs = [lax.all_gather(slab, PLANE, axis=0)]
    slabs, mixed_all = lax.optimization_barrier((slabs, mixed_all))
    if few:
        slabs = slabs + [exchange(v, "core", 2, 1) for v in slabs]
    slabs, ff_slab = lax.optimization_barrier((slabs, ff_slab))
    ff_slab = lax.all_gather(ff_slab, LINES, axis=0)
    spare = 1 if quarter % 8 == 0 else blocks * members
    got = call(
        functools.partial(qkv_kernel, shard, members, (b_qkv.shape[0], span, down), few),
        [
            shape(width, full),
            shape(queries, width),
            shape(lanes, queries),
            shape(2 * lanes, queries),
            shape(lanes, queries),
            shape(FEATURES, HEAD_DIM),
            shape(8, 2 * length),
            shape(8, width),
        ],
        [ids, mixed_all, *slabs],
        "qkv",
        scratch=[
            pltpu.VMEM((blocks, 8, full), f32),
            pltpu.VMEM((spare, quarter, full), f32),
            pltpu.VMEM((FEATURES, 1, HEAD_DIM), f32),
        ],
        smem=1,
        deep=True,
        late=range(2, 2 + len(slabs)) if few else (),
    )
    w_cols, x, pq, kv, keys, proj, bias, vec = got

    if few:
        kv_own = gather(kv, GROUP, members)
        kv_all = kv_own + [exchange(v, "core", 2, 1) for v in kv_own]
        (wo_parts,) = call(
            functools.partial(stack_rest_kernel, rows),
            [shape(members, quarter, width)],
            [mixed_all],
            "stack_out",
        )
        wo_parts, _ = lax.optimization_barrier((wo_parts, kv_all))
        wo_own = gather(wo_parts, GROUP, members)
    else:
        kv_all = lax.all_gather(kv, PLANE, axis=0)
    got = attention(ids, kv_all, pq, bias)
    att, den = got[:2]
    att_parts = scatter(got[2:], "zl")
    if few:
        wo_own, _ = lax.optimization_barrier((wo_own, att_parts[2]))
        wo_all = wo_own + [exchange(v, "core", 2, 1) for v in wo_own]
        (w_full,) = call(
            functools.partial(weights_out_kernel, shard),
            [shape(width, width)],
            [ids, *wo_all],
            "weights_out",
            smem=1,
        )
    else:
        w_full = lax.all_gather(w_out, ("zh", "zl", "x"), axis=0, tiled=True)

    first, norm_rows, inverse, att_rows = call(
        norm_one_kernel,
        [row_shape, row_shape, shape(rows, 128), row_shape],
        [ids, *att_parts, mixed, w_full, vec],
        "norm_one",
        smem=1,
    )
    first, ff_slab = lax.optimization_barrier((first, ff_slab))
    firsts = gather(first, GROUP, members)
    full_rows = shape(queries, blocks * down)
    ff_matrices = call(
        functools.partial(prepare_kernel, shard),
        [shape(width, blocks * down, dtype=bf16)] * 2
        + [shape(blocks * down, width, dtype=bf16)] * 2,
        [ff_slab],
        "prepare",
    )
    got = call(
        forward_kernel,
        [full_rows, shape(queries, width)] + [row_shape] * members,
        [*firsts, *ff_matrices, vec],
        "forward",
    )
    pre, first_all = got[:2]
    parts = scatter(got[2:], GROUP)
    out_rows, dz2, grads_two = call(
        norm_two_kernel,
        [row_shape, row_shape, shape(8, width)],
        [*parts, first, cot_rows, vec],
        "norm_two",
    )
    dzs = gather(dz2, GROUP, members)
    got = call(
        backward_kernel,
        [shape(queries, width), full_rows] + [row_shape] * members,
        [*dzs, pre, *ff_matrices],
        "backward",
    )
    dz2_all, d_pre = got[:2]
    parts = scatter(got[2:], GROUP)

    (ff_grads,) = call(
        functools.partial(ff_weights_kernel, shard, down),
        [shape(blocks, shard + down + 8, width)],
        [first_all, d_pre, pre, dz2_all, grads_two],
        "ff_weights",
        push=(0,),
    )
    ff_grads, parts = lax.optimization_barrier((ff_grads, parts))

    head_rows = shape(rows, lanes)
    got = call(
        norm_one_back_kernel,
        [row_shape, shape(8, width)] + [head_rows] * members,
        [ids, *parts, dz2, norm_rows, inverse, w_full, vec],
        "norm_one_back",
        smem=1,
    )
    dz1, grads_one = got[:2]
    grads = scatter(got[2:], "zl")

    share = shape(members, members, quarter, width)
    out_shares = call(
        out_weights_kernel,
        [share, share] if few else [shape(places, members, quarter, width)],
        [ids, att_rows, dz1],
        "out_weights",
        scratch=[pltpu.VMEM((places, members, quarter, width), f32)],
        smem=1,
    )
    def sum_cores(own, other, name):
        came = exchange(other, "core", 2, 1)
        return call(sum_cores_kernel, [shape(*own.shape[1:])] * members, [own, came], name)

    if few:
        out_shares = sum_cores(*out_shares, "sum_out")
        grads, out_shares, ff_grads = lax.optimization_barrier((grads, out_shares, ff_grads))
        out_shares = scatter(out_shares, GROUP)
    else:
        grads, ff_grads = lax.optimization_barrier((grads, ff_grads))
    ff_grads = lax.psum_scatter(ff_grads, LINES, scatter_dimension=0, tiled=False)
    out_came, out_core = exchange(out_rows, "y", 2, 1), exchange(out_rows, "core", 2, 1)
    back = attention_back(ids, kv_all, pq, bias, att, den, grads)
    back, out_came, out_core = lax.optimization_barrier((back, out_came, out_core))
    if few:
        back, out_shares = lax.optimization_barrier((back, out_shares))
        arrived = scatter(sum_cores(back[0], back[1], "sum_keys"), GROUP)
    else:
        arrived = lax.psum_scatter(back[0], PLANE, scatter_dimension=0, tiled=False)
        arrived = [arrived] + [jnp.zeros_like(arrived)] * 3
    dpq, dbias = back[-2:]
    out_parts = [out_rows, out_core, out_came, exchange(out_came, "core", 2, 1)]
    output = place(ids, out_parts, "place_output")
    arrived, output = lax.optimization_barrier((arrived, output))

    got = call(
        qkv_back_kernel,
        [shape(queries, full), shape(queries, width)],
        [ids, *arrived, pq, dpq, kv, keys, proj, w_cols],
        "qkv_back",
        scratch=[pltpu.VMEM((full, queries), f32)],
        smem=1,
    )
    d_qkv = got[0]
    piece = shape(rows + -(-quarter // 8) * 8, width)
    if few:
        mixed_grads = call(
            sum_mixed_kernel, [piece] * members, [ids, *out_shares, got[1]], "sum_mixed", smem=1
        )
    else:
        part = lax.psum_scatter(out_shares[0], PLANE, scatter_dimension=0, tiled=False)
        part = jnp.concatenate(
            [got[1].reshape(members, rows, width), part], axis=1
        )
        part = jnp.pad(part, ((0, 0), (0, piece.shape[0] - part.shape[1]), (0, 0)))
        mixed_grads = [
            lax.dynamic_index_in_dim(part, zl_at ^ k, 0, keepdims=False) for k in range(members)
        ]

    def split_plane(parts, piece, name):
        if few:
            return call(sum_split_kernel, [piece] * members, parts, name)
        part = lax.psum_scatter(parts[0], PLANE, scatter_dimension=0, tiled=False)
        return [
            lax.dynamic_index_in_dim(part, zl_at ^ k, 0, keepdims=False) for k in range(members)
        ]

    share = shape(members, members, quarter + 8, full)
    shares_out = call(
        functools.partial(qkv_weights_kernel, shard, span),
        [share, share] if few else [shape(places, members, quarter + 8, full)],
        [ids, x, d_qkv, dbias, grads_one],
        "qkv_weights",
        scratch=[pltpu.VMEM((places, members, quarter + 8, full), f32)],
        smem=1,
    )
    if few:
        shares_out = sum_cores(*shares_out, "sum_qkv")
    shares_out, mixed_grads, ff_grads = lax.optimization_barrier(
        (shares_out, mixed_grads, ff_grads)
    )
    ff_grads = swap(ff_grads)
    mine = scatter(shares_out, GROUP) if few else shares_out
    mixed_grads = scatter(mixed_grads, "zl")
    mine, mixed_grads = lax.optimization_barrier((mine, mixed_grads))
    mine = split_plane(mine, shape(quarter + 8, full), "sum_qkv_plane")
    mine, ff_grads = lax.optimization_barrier((mine, ff_grads))
    (d_input_rows,) = call(sum_four_kernel, [row_shape], [*mixed_grads, dz1], "sum_rows")
    ff_came = exchange(ff_grads, "y", 2, 1)
    input_came = exchange(d_input_rows, "y", 2, 1)
    mine = scatter(mine, "zl")
    got = call(
        functools.partial(merge_kernel, shard, rows),
        [
            shape(quarter, 4 * width),
            shape(*b_qkv.shape),
            shape(*position_bias.shape),
            shape(shard),
            shape(shard),
            shape(shard),
        ],
        [ids, *mine, *mixed_grads],
        "merge",
        scratch=[pltpu.VMEM((1, 3 * width), f32)],
        smem=1,
    )
    merged, d_b_qkv, d_position_bias, d_ln1_gain, d_ln1_bias, d_b_out = got
    merged_came = exchange(merged, "y", 2, 1)
    ff_came, merged_came, input_came = lax.optimization_barrier(
        (ff_came, merged_came, input_came)
    )

    def relayed(value, came):
        return [value, exchange(value, "core", 2, 1), came, exchange(came, "core", 2, 1)]

    d_inputs = place(ids, relayed(d_input_rows, input_came), "place_inputs")
    d_w_qkv, d_w_out = call(
        place_weights_kernel,
        [shape(*w_qkv.shape), shape(shard, width)],
        [ids, *relayed(merged, merged_came)],
        "place_weights",
        smem=1,
    )
    ff_parts = relayed(ff_grads, ff_came)
    got = call(
        functools.partial(place_ff_kernel, shard, down),
        [shape(shard, w_up.shape[1]), shape(*w_down.shape), shape(*b_up.shape)]
        + [shape(shard)] * 3,
        [ids, *ff_parts],
        "place_ff",
        scratch=[pltpu.VMEM((1, b_up.shape[0]), f32)],
        smem=1,
    )
    d_w_up, d_w_down, d_b_up, d_ln2_gain, d_ln2_bias, d_b_down = got

    return (
        output,
        d_inputs,
        d_position_bias,
        d_w_qkv,
        d_b_qkv,
        d_w_out,
        d_b_out,
        d_ln1_gain,
        d_ln1_bias,
        d_w_up,
        d_b_up,
        d_w_down,
        d_b_down,
        d_ln2_gain,
        d_ln2_bias,
    )


def solution(mesh):
    feats, wides = mesh.shape["feat"], mesh.shape["wide"]
    ys, zhs = feats // 2, wides // (2 * feats)
    fine = Mesh(mesh.devices.reshape(ys, 2, zhs, feats, 2), ("y", "core", "zh", "zl", "x"))
    wide = ("zh", "zl", "x")
    mat, vector, lane = P(wide, None), P(wide), P(None, wide)
    return jax.shard_map(
        functools.partial(body, ys, zhs),
        mesh=fine,
        in_specs=(mat, mat, P(None, FEAT), lane, mat, vector, mat, vector)
        + (vector, vector, mat, vector, mat, vector, vector, vector),
        out_specs=(mat, mat, lane, mat, vector, mat, vector, vector)
        + (vector, mat, vector, mat, vector, vector, vector),
        check_vma=False,
    )
```

```python
import functools
import math

import jax
import jax.numpy as jnp
from jax import lax
from jax.experimental import pallas as pl
from jax.experimental.pallas import tpu as pltpu
from jax.sharding import Mesh
from jax.sharding import PartitionSpec as P

HEADS = 12
HEAD_DIM = 64
FEATURES = 64
EPS = 1e-06
f32 = jnp.float32
bf16 = jnp.bfloat16

GROUP = ("y", "x")
FEAT = ("y", "core")
PLANE = ("zh", "x", "y", "core")
LINES = ("zh", "zl", "core")
CORE, MEMBER, OWN, HEAD, WIDE, PLACE = range(6)


def split(value):
    high = value.astype(bf16)
    return high, (value - high.astype(f32)).astype(bf16)


def dot(a, b, ca, cb):
    return lax.dot_general(a, b, (((ca,), (cb,)), ((), ())), preferred_element_type=f32)


def dot3s(a, b, ca, cb):
    return dot(a[0], b[0], ca, cb) + (dot(a[0], b[1], ca, cb) + dot(a[1], b[0], ca, cb))


def dot3(a, b, ca, cb):
    return dot3s(split(a), split(b), ca, cb)


def cost():
    return pl.CostEstimate(flops=1 << 20, bytes_accessed=1 << 10, transcendentals=0)


def tiled(dims):
    if len(dims) < 2:
        return 0
    return math.prod(dims[:-2]) * -(-dims[-2] // 8) * -(-dims[-1] // 128) * 4096


def call(kernel, outs, args, name, scratch=(), smem=0, room=8, limit=0, fetch=(), push=(), far=False, deep=False, late=None, stream=()):
    held = sum(tiled(ref.shape) for ref in scratch)
    held += sum(size for size in map(lambda a: tiled(a.shape), [*args, *outs]) if size > 4 << 20)
    if deep and not far:
        fetch = [i for i in range(smem, len(args)) if i not in stream]
        push, limit = range(len(outs)), 60 << 20
    fetch, push = tuple(fetch), tuple(push)
    near = [pltpu.VMEM(args[i].shape, args[i].dtype) for i in fetch]
    near += [pltpu.VMEM(outs[i].shape, outs[i].dtype) for i in push]
    held += sum(args[i].size * args[i].dtype.itemsize for i in fetch)
    held += sum(outs[i].size * outs[i].dtype.itemsize for i in push)
    count = len(args) + len(outs)
    flow = []
    if stream:
        first = args[stream[0]]
        flow = [
            pltpu.VMEM((len(stream),) + first.shape, first.dtype),
            pltpu.SemaphoreType.DMA((len(stream),)),
        ]

    def moved(*refs):
        whole, own = list(refs[:count]), refs[count : count + len(scratch)]
        spare, sems = refs[count + len(scratch) : -1 - len(flow)], refs[-1 - len(flow)]
        copies, after = [], []
        for at, (i, ref) in enumerate(zip(fetch, spare)):
            copies.append(pltpu.make_async_copy(whole[i], ref, sems.at[at]))
            whole[i] = ref
        for at, (i, ref) in enumerate(zip(push, spare[len(fetch) :])):
            i += len(args)
            after.append(pltpu.make_async_copy(ref, whole[i], sems.at[len(fetch) + at]))
            whole[i] = ref
        for copy in copies:
            copy.start()
        if flow:
            held, flow_sems = refs[-2:]
            for i, at in enumerate(stream):
                pltpu.make_async_copy(whole[at], held.at[i], flow_sems.at[i]).start()
        for i, copy in zip(fetch, copies):
            if late is None or i not in late:
                copy.wait()
        started = []

        def arrive(i):
            copies[fetch.index(i)].wait()

        def start(i):
            started.append(push.index(i))
            after[started[-1]].start()

        def wait(i):
            pltpu.make_async_copy(held.at[i], held.at[i], flow_sems.at[i]).wait()

        if flow:
            whole = [ref for i, ref in enumerate(whole) if i not in stream]
            kernel(*whole, *own, held=held, wait=wait, start=start)
        elif late is not None:
            kernel(*whole, *own, arrive=arrive, start=start)
        else:
            kernel(*whole, *own)
        for i, copy in enumerate(after):
            if i not in started:
                copy.start()
        for copy in after:
            copy.wait()

    def spec(i, which):
        return pl.BlockSpec(memory_space=pltpu.HBM if i in which else pltpu.VMEM)

    return pl.pallas_call(
        moved if near else kernel,
        out_shape=outs,
        in_specs=[pl.BlockSpec(memory_space=pltpu.SMEM)] * smem
        + [
            spec(i, range(len(args)) if far else (*fetch, *stream))
            for i in range(smem, len(args))
        ],
        out_specs=[spec(i, push) for i in range(len(outs))],
        scratch_shapes=list(scratch)
        + near
        + ([pltpu.SemaphoreType.DMA((len(near),))] if near else [])
        + flow,
        compiler_params=pltpu.CompilerParams(vmem_limit_bytes=limit or held + (room << 20)),
        cost_estimate=cost(),
        name=name,
    )(*args)


def when(condition):
    if isinstance(condition, bool):
        return lambda run: run() if condition else None
    return pl.when(condition)


def shape(*dims, dtype=f32):
    return jax.ShapeDtypeStruct(dims, dtype)


def by_case(value, count, run):
    for i in range(count):
        pl.when(value == i)(functools.partial(run, i))


def pack_qkv_kernel(rows, members, ids, *refs):
    count = (len(refs) - members - 3) // 2 + 1
    sources, pieces = refs[:count], refs[count : count + members]
    mixed, cot_out = refs[count + members : count + members + 2]
    held, sems = refs[count + members + 2 : -1], refs[-1]
    part = cot_out.shape[0]
    at = pl.multiple_of(ids[OWN] * part, 8)
    copies = [
        pltpu.make_async_copy(source.at[pl.ds(at, part)], target, sems.at[i])
        for i, (source, target) in enumerate(
            zip(sources[:2], (mixed.at[pl.ds(0, part)], cot_out))
        )
    ]
    quarter = rows // members
    for i, (source, target) in enumerate(zip(sources[2:], held)):
        if source.shape != target.shape:
            source = source.at[pl.ds(pl.multiple_of(ids[OWN] * quarter, 8), quarter)]
        copies.append(pltpu.make_async_copy(source, target, sems.at[2 + i]))
    for copy in copies:
        copy.start()
    for copy in copies:
        copy.wait()
    w_ref, out_ref, bias_ref, b_ref, proj_ref, up_ref = held[:6]
    width = w_ref.shape[1] // 3
    lanes = width // members
    heads = bias_ref.shape[0] // members
    for piece in pieces:
        piece[quarter:, :] = jnp.zeros((8, 3 * lanes), f32)
        piece[quarter : quarter + 1, : b_ref.shape[0]] = b_ref[...].reshape(1, -1)
        for i, ref in enumerate(held[6:]):
            row, lane = (4, i) if i < 5 else (5, 0)
            piece[quarter + row : quarter + row + 1, lane * rows : (lane + 1) * rows] = ref[
                ...
            ].reshape(1, -1)
        piece[quarter + 5 : quarter + 6, rows : rows + up_ref.shape[0]] = up_ref[...].reshape(1, -1)
        per = 3 * lanes // HEAD_DIM
        for i in range(proj_ref.shape[0]):
            row, lane = quarter + 6 + i // per, HEAD_DIM * (i % per)
            piece[row : row + 1, lane : lane + HEAD_DIM] = proj_ref[i : i + 1]

    def own(f):
        first = 0 if w_ref.shape[0] == quarter else quarter * f
        mixed[part : part + quarter] = out_ref[first : first + quarter]

        def head(t):
            for k, piece in enumerate(pieces):
                to = t ^ k
                for p in range(3):
                    at = width * p + lanes * to
                    piece[:quarter, lanes * p : lanes * (p + 1)] = w_ref[
                        first : first + quarter, at : at + lanes
                    ]
                piece[quarter + 1 : quarter + 1 + heads, : bias_ref.shape[1]] = bias_ref[
                    heads * to : heads * (to + 1)
                ]

        by_case(ids[HEAD], members, head)

    by_case(ids[OWN], members, own)


def pack_ff_kernel(members, down, ids, up_ref, down_ref, out):
    rows = up_ref.shape[0]
    blocks = up_ref.shape[1] // (members * down)

    def case(i):
        for w in range(blocks):
            at = (w * members + i) * down
            out[:rows, down * w : down * (w + 1)] = up_ref[:, at : at + down]
        out[rows : rows + down, :] = down_ref[down * i : down * (i + 1)]

    by_case(ids[OWN], members, case)


def plane_place(ids, members, few, i):
    if not few:
        zh, rest = divmod(i, 2 * members)
        return zh, rest // members, rest % members
    other, j = divmod(i, members)
    member = lax.bitwise_xor(ids[MEMBER], j)
    return 0, lax.rem(member, 2), 2 * lax.div(member, 2) + lax.bitwise_xor(ids[CORE], other)


def qkv_kernel(rows, members, spans, few, ids, *refs, arrive=None, start=None):
    mixed, refs = refs[0], refs[1:]
    w_out, x_out, pq_out, kv_out, key_out, proj_out, bias_out, vec_out, extra, held, directions = refs[-11:]
    slabs = refs[:-11]
    slabs = list(slabs) if few else [slabs[0].at[i] for i in range(slabs[0].shape[0])]
    width = x_out.shape[1]
    blocks = extra.shape[0]
    full = w_out.shape[1]
    lanes = full // 3
    heads = lanes // HEAD_DIM
    quarter = rows // members
    part = x_out.shape[0] // members
    for z in range(members):
        x_out[part * z : part * (z + 1), :] = mixed[z, :part]
    for i, slab in enumerate(slabs):
        if arrive is not None and few:
            arrive(2 + i)
        zh, x, f = plane_place(ids, members, few, i)
        for k in range(members):
            w = 2 * (members * zh + lax.bitwise_xor(ids[HEAD], k)) + x
            if i < 2 if few else f == 0:
                extra[w] = slab[k, quarter:]
            if quarter % 8 == 0:
                at = pl.multiple_of(w * rows + f * quarter, 8)
                w_out[pl.ds(at, quarter), :] = slab[k, :quarter]
            else:
                held[w * members + f] = slab[k, :quarter]
    if quarter % 8:
        for i in range(held.shape[0]):
            w_out[quarter * i : quarter * (i + 1)] = held[i]

    share = FEATURES // members
    per = full // HEAD_DIM
    for i, slab in enumerate(slabs):
        zh, x, f = plane_place(ids, members, few, i)
        if few or (zh, x) == (0, 0):
            for r in range(share):
                at, lane = quarter + 6 + r // per, HEAD_DIM * (r % per)
                directions[share * f + r] = slab[0, at : at + 1, lane : lane + HEAD_DIM]
    for r in range(FEATURES):
        proj_out[r : r + 1, :] = directions[r]
    bias_out[...] = jnp.zeros_like(bias_out)
    b_row = []
    for w in range(blocks):
        b_row.append(extra[w, 0:1, : spans[0]])
        count = spans[1]
        bias_out[:heads, count * w : count * (w + 1)] = extra[w, 1 : 1 + heads, :count]
        for i in range(6):
            row, lane = (4, i) if i < 5 else (5, 0)
            vec_out[1 + i : 2 + i, rows * w : rows * (w + 1)] = extra[
                w, row : row + 1, lane * rows : (lane + 1) * rows
            ]
    vec_out[7:8] = jnp.zeros((1, width), f32)
    b_row = jnp.concatenate(b_row, axis=1)

    def unit(g):
        count = spans[2]
        for w in range(blocks):
            vec_out[0:1, count * w : count * (w + 1)] = extra[
                w, 5:6, rows + count * g : rows + count * (g + 1)
            ]

    by_case(ids[MEMBER], members, unit)
    if start is not None:
        for i in (0, 1, 5, 6, 7):
            start(i)
    qkv = dot3(x_out[...], w_out[...], 1, 0)
    scale = HEAD_DIM**-0.25
    proj = split(proj_out[...])

    def head(t):
        bias = [b_row[:, width * p + lanes * t : width * p + lanes * (t + 1)] for p in range(3)]
        turned = (qkv + jnp.concatenate(bias, axis=1)).T
        for h in range(heads):
            lo, hi = HEAD_DIM * h, HEAD_DIM * (h + 1)
            q = turned[lo:hi] * scale
            k = turned[lanes + lo : lanes + hi] * scale
            pq_out[lo:hi] = jnp.exp(dot3s(proj, split(q), 1, 0))
            pk = dot3s(proj, split(k), 1, 0) - 0.5 * jnp.sum(k * k, axis=0, keepdims=True)
            kv_out[128 * h : 128 * h + 64] = jnp.exp(pk)
            kv_out[128 * h + 64 : 128 * h + 128] = turned[2 * lanes + lo : 2 * lanes + hi]
            key_out[lo:hi] = k

    by_case(ids[HEAD], members, head)


def rolled_rows(table, row):
    wide = jnp.broadcast_to(row, (8, row.shape[1]))
    return pltpu.roll(wide, 0, 1, stride=1, stride_axis=0)


def make_tables(tables, bias_ref, heads):
    length = bias_ref.shape[1]
    for h in range(heads):
        rows = rolled_rows(None, jnp.exp(bias_ref[h : h + 1]))
        tables[0, 8 * h : 8 * h + 8] = rows
        tables[1, 8 * h : 8 * h + 8] = pltpu.roll(rows, length - 64, 1)


def factor_tile(windows):
    first = lax.broadcasted_iota(jnp.int32, (8, 128), 1) < 64
    pairs = {}
    for g in range(8):
        for d in range(-3, 3):
            low = pltpu.roll(windows[d + 3], (8 * g + 64) % 128, 1)
            high = windows[d + 4] if g == 0 else pltpu.roll(windows[d + 4], 8 * g, 1)
            pairs[d, g] = jnp.where(first, low, high)
    rows = []
    for z in range(4):
        for g in range(8):
            rows.append(jnp.concatenate([pairs[-z, g], pairs[2 - z, g]], axis=1))
    return jnp.concatenate(rows, axis=0)


def window_sums(pairs):
    first = lax.broadcasted_iota(jnp.int32, (8, 128), 1) < 64
    sums = [jnp.zeros((8, 128), f32) for _ in range(7)]
    for g in range(8):
        for d in range(-3, 3):
            total = None
            for z in range(4):
                for p in range(2):
                    if 2 * p - z == d:
                        term = pairs[64 * z + 8 * g : 64 * z + 8 * g + 8, 128 * p : 128 * p + 128]
                        total = term if total is None else total + term
            low = pltpu.roll(jnp.where(first, total, 0.0), 64 - 8 * g, 1)
            high = jnp.where(first, 0.0, total)
            sums[d + 3] = sums[d + 3] + low
            sums[d + 4] = sums[d + 4] + (high if g == 0 else pltpu.roll(high, 128 - 8 * g, 1))
    return sums


def window_start(ids, members, groups, seg, length, n):
    if groups == 1:
        other, j = n // members, n % members
        member = lax.bitwise_xor(ids[MEMBER], j)
        zh, x = ids[PLACE] * 0, lax.rem(member, 2)
        f = 2 * lax.div(member, 2) + lax.bitwise_xor(ids[CORE], other)
    else:
        zh, x, f = n // (2 * members), lax.rem(lax.div(n, members), 2), lax.rem(n, members)
    own = ids[PLACE]
    away = 8 * members * (lax.div(own, 2 * members) - zh)
    away += members * (lax.rem(lax.div(own, members), 2) - x) + ids[OWN] - f
    start = away + length // (2 * seg) - 1
    odd = lax.rem(start, 2)
    return start - odd, odd


def window_at(start, d):
    return pl.multiple_of(start * 64 + 512 * d, 128)


def split_block(block, h, kcat, vcat):
    for part, cat in ((0, kcat), (64, vcat)):
        high, low = split(block[128 * h + part : 128 * h + part + 64])
        cat[h, 0:64] = high
        cat[h, 64:128] = low
        cat[h, 128:192] = high


def attention_kernel(groups, blocks, ids, *refs, held=None, wait=None, start=None):
    if groups > 1:
        held, refs = refs[0], refs[1:]
    pq_ref, bias_ref, att_out, den_out = refs[:4]
    parts = refs[4:8]
    tables, qcat, out_rows, kcat, vcat = refs[8:]
    heads = pq_ref.shape[0] // 64
    queries = pq_ref.shape[1]
    step = pl.program_id(0) if groups > 1 else 0

    @when(step == 0)
    def _():
        make_tables(tables, bias_ref, heads)
        for h in range(heads):
            high, low = split(pq_ref[64 * h : 64 * h + 64])
            qcat[h, 0:64] = high
            qcat[h, 64:128] = high
            qcat[h, 128:192] = low
        att_out[...] = jnp.zeros_like(att_out)
        den_out[...] = jnp.zeros_like(den_out)

    def advance(n, carry):
        first, odd = window_start(ids, 4, groups, 64, bias_ref.shape[1], step * blocks + n)
        if wait is not None:
            wait(n)
        for h in range(heads):
            split_block(held.at[n], h, kcat.at[n], vcat.at[n])
            scores = dot(kcat[n, h], qcat[h], 0, 0)
            rows = slice(8 * h, 8 * h + 8)
            windows = [
                tables[odd, rows, pl.ds(window_at(first, d), 128)] for d in range(-3, 4)
            ]
            weight = scores * factor_tile(windows)
            high, low = split(weight)
            both = dot(vcat[n, h, 0:128], high, 1, 0)
            more = dot(vcat[n, h, 0:64], low, 1, 0)
            att_out[64 * h : 64 * h + 64] += both[0:64] + both[64:128] + more
            den_out[h : h + 1] += jnp.sum(weight, axis=0, keepdims=True)
        return carry

    lax.fori_loop(0, blocks, advance, 0, unroll=2)

    @when(step == groups - 1)
    def _():
        for h in range(heads):
            att_out[64 * h : 64 * h + 64] = att_out[64 * h : 64 * h + 64] / den_out[h : h + 1]
        out_rows[...] = att_out[...].T
        rows = queries // 4
        for k in range(4):
            first = pl.multiple_of(lax.bitwise_xor(ids[HEAD], k) * rows, 8)
            parts[k][...] = out_rows[pl.ds(first, rows), :]


def attention(ids, kv, pq, window):
    stacked = not isinstance(kv, list)
    count = kv.shape[0] if stacked else len(kv)
    blocks = 8 if stacked else count
    groups = count // blocks
    queries = pq.shape[1]
    heads = pq.shape[0] // 64
    rows = shape(queries // 4, heads * 64)
    outs = [shape(heads * 64, queries), shape(8, queries)] + [rows] * 4
    scratch = [
        pltpu.VMEM((2, 8 * heads, window.shape[1]), f32),
        pltpu.VMEM((heads, 192, queries), bf16),
        pltpu.VMEM((queries, heads * 64), f32),
        pltpu.VMEM((blocks, heads, 192, queries), bf16),
        pltpu.VMEM((blocks, heads, 192, queries), bf16),
    ]
    kernel = functools.partial(attention_kernel, groups, blocks)
    if not stacked:
        args = [ids, *kv, pq, window]
        stream = range(1, 1 + count)
        return call(kernel, outs, args, "attention", scratch, 1, deep=True, stream=stream)
    whole = lambda a: pl.BlockSpec(a.shape, lambda g, nd=len(a.shape): (0,) * nd)
    smem = pl.BlockSpec(memory_space=pltpu.SMEM)
    kv_spec = pl.BlockSpec((blocks,) + kv.shape[1:], lambda g: (g, 0, 0))
    return pl.pallas_call(
        kernel,
        grid=(groups,),
        out_shape=outs,
        in_specs=[smem, kv_spec, whole(pq), whole(window)],
        out_specs=[whole(a) for a in outs],
        scratch_shapes=scratch,
        compiler_params=pltpu.CompilerParams(vmem_limit_bytes=52 << 20),
        name="attention",
    )(ids, kv, pq, window)


def attention_back_kernel(groups, blocks, ids, *refs, held=None, wait=None, start=None):
    if groups > 1:
        held, refs = refs[0], refs[1:]
    pq_ref, bias_ref, att_ref, den_ref = refs[:4]
    grads = refs[4:8]
    if groups == 1:
        own, other, dpq_out, dbias_out = refs[8:12]
    else:
        dkv, dpq_out, dbias_out = refs[8:11]
    tables, qcat, gcat, gden, diag, grad_rows, kcat, vcat = refs[-8:]
    heads = pq_ref.shape[0] // 64
    queries = pq_ref.shape[1]
    step = pl.program_id(0) if groups > 1 else 0

    @when(step == 0)
    def _():
        rows = queries // 4
        for k in range(4):
            first = pl.multiple_of(lax.bitwise_xor(ids[HEAD], k) * rows, 8)
            grad_rows[pl.ds(first, rows), :] = grads[k][...]
        make_tables(tables, bias_ref, heads)
        d_att = grad_rows[...].T
        gden[...] = jnp.zeros_like(gden)
        for h in range(heads):
            lo, hi = 64 * h, 64 * h + 64
            for value, cat in ((pq_ref[lo:hi], qcat), (d_att[lo:hi] / den_ref[h : h + 1], gcat)):
                high, low = split(value)
                cat[h, 0:64] = high
                cat[h, 64:128] = high
                cat[h, 128:192] = low
            gden[h : h + 1] = -(
                jnp.sum(d_att[lo:hi] * att_ref[lo:hi], axis=0, keepdims=True) / den_ref[h : h + 1]
            )
        dpq_out[...] = jnp.zeros_like(dpq_out)
        diag[...] = jnp.zeros_like(diag)

    def advance(dkv, first, n, carry):
        begin, odd = window_start(ids, 4, groups, 64, bias_ref.shape[1], step * blocks + n)
        if wait is not None:
            wait(n)
        for h in range(heads):
            split_block(held.at[n], h, kcat.at[n], vcat.at[n])
            scores = dot(kcat[n, h], qcat[h], 0, 0)
            rows = slice(8 * h, 8 * h + 8)
            factor = factor_tile(
                [tables[odd, rows, pl.ds(window_at(begin, d), 128)] for d in range(-3, 4)]
            )
            d_weight = dot(vcat[n, h], gcat[h], 0, 0) + gden[h : h + 1]
            w_high, w_low = split(scores * factor)
            e_high, e_low = split(d_weight * factor)
            pairs = d_weight * scores
            both = dot(gcat[h, 64:192], w_high, 1, 1)
            dv = both[0:64] + both[64:128] + dot(gcat[h, 0:64], w_low, 1, 1)
            both = dot(qcat[h, 64:192], e_high, 1, 1)
            dk = both[0:64] + both[64:128] + dot(qcat[h, 0:64], e_low, 1, 1)
            both = dot(kcat[n, h, 0:128], e_high, 1, 0)
            dq = both[0:64] + both[64:128] + dot(kcat[n, h, 0:64], e_low, 1, 0)
            dpq_out[64 * h : 64 * h + 64] += dq
            dkv[n - first, 128 * h : 128 * h + 64] = dk
            dkv[n - first, 128 * h + 64 : 128 * h + 128] = dv
            for i, total in enumerate(window_sums(pairs)):
                diag[odd, rows, pl.ds(window_at(begin, i - 3), 128)] += total
        return carry

    if groups == 1:
        half = blocks // 2
        lax.fori_loop(half, blocks, functools.partial(advance, other, half), 0, unroll=2)
        if start is not None:
            start(1)
        lax.fori_loop(0, half, functools.partial(advance, own, 0), 0, unroll=2)
        if start is not None:
            start(0)
    else:
        lax.fori_loop(0, blocks, functools.partial(advance, dkv, 0), 0)

    @when(step == groups - 1)
    def _():
        length = diag.shape[2]
        dbias_out[...] = jnp.zeros_like(dbias_out)
        for h in range(heads):
            both = diag[0, 8 * h : 8 * h + 8] + pltpu.roll(diag[1, 8 * h : 8 * h + 8], 64, 1)
            total = both[0:1]
            for s in range(1, 8):
                total = total + pltpu.roll(both[s : s + 1], length - s, 1)
            dbias_out[h : h + 1] = total * jnp.exp(bias_ref[h : h + 1])


def attention_back(ids, kv, pq, window, att, den, grads):
    stacked = not isinstance(kv, list)
    count = kv.shape[0] if stacked else len(kv)
    blocks = 8 if stacked else count
    groups = count // blocks
    queries = pq.shape[1]
    heads = pq.shape[0] // 64
    outs = [shape(heads * 64, queries), shape(8, window.shape[1])]
    scratch = [
        pltpu.VMEM((2, 8 * heads, window.shape[1]), f32),
        pltpu.VMEM((heads, 192, queries), bf16),
        pltpu.VMEM((heads, 192, queries), bf16),
        pltpu.VMEM((8, queries), f32),
        pltpu.VMEM((2, 8 * heads, window.shape[1]), f32),
        pltpu.VMEM((queries, heads * 64), f32),
        pltpu.VMEM((blocks, heads, 192, queries), bf16),
        pltpu.VMEM((blocks, heads, 192, queries), bf16),
    ]
    kernel = functools.partial(attention_back_kernel, groups, blocks)
    small = [pq, window, att, den] + list(grads)
    if not stacked:
        half = shape(count // 2, heads * 128, queries)
        return call(
            kernel,
            [half, half] + outs,
            [ids, *kv] + small,
            "attention_back",
            scratch,
            1,
            deep=True,
            stream=range(1, 1 + count),
        )
    whole = lambda a: pl.BlockSpec(a.shape, lambda g, nd=len(a.shape): (0,) * nd)
    smem = pl.BlockSpec(memory_space=pltpu.SMEM)
    kv_spec = pl.BlockSpec((blocks, heads * 128, queries), lambda g: (g, 0, 0))
    return pl.pallas_call(
        kernel,
        grid=(groups,),
        out_shape=[shape(count, heads * 128, queries)] + outs,
        in_specs=[smem, kv_spec] + [whole(a) for a in small],
        out_specs=[kv_spec] + [whole(a) for a in outs],
        scratch_shapes=scratch,
        compiler_params=pltpu.CompilerParams(vmem_limit_bytes=52 << 20),
        name="attention_back",
    )(ids, kv, *small)


def normed(value):
    mean = jnp.mean(value, axis=1, keepdims=True)
    centered = value - mean
    var = jnp.mean(centered * centered, axis=1, keepdims=True)
    inverse = lax.rsqrt(var + EPS)
    return centered * inverse, inverse


def norm_back(upstream, n, inverse, gain):
    scaled = gain * upstream
    mean = jnp.mean(scaled, axis=1, keepdims=True)
    slope = jnp.mean(scaled * n, axis=1, keepdims=True)
    return (scaled - mean - n * slope) * inverse


def colsum(value):
    return jnp.sum(value, axis=0, keepdims=True)


def weights_out_kernel(rows, ids, *refs):
    out = refs[-1]
    members, quarter, _ = refs[0].shape
    for i, ref in enumerate(refs[:-1]):
        other, j = divmod(i, members)
        place = lax.bitwise_xor(ids[MEMBER], j)
        f = 2 * lax.div(place, 2) + lax.bitwise_xor(ids[CORE], other)
        for k in range(members):
            w = 2 * k + lax.rem(place, 2)
            out[pl.ds(pl.multiple_of(rows * w + quarter * f, 8), quarter), :] = ref[k]


def norm_one_kernel(ids, a0, a1, a2, a3, x_ref, w_ref, vec_ref, *refs):
    first_out, n_out, inverse_out, att_out = refs
    lanes = a0.shape[1]

    def head(t):
        for k, ref in enumerate((a0, a1, a2, a3)):
            at = lanes * (t ^ k)
            att_out[:, at : at + lanes] = ref[...]

    by_case(ids[HEAD], 4, head)
    projected = dot3(att_out[...], w_ref[...], 1, 0)
    n, inverse = normed(x_ref[: a0.shape[0]] + (projected + vec_ref[1:2]))
    first_out[...] = n * vec_ref[2:3] + vec_ref[3:4]
    n_out[...] = n
    inverse_out[...] = jnp.broadcast_to(inverse, inverse_out.shape)


def norm_two_kernel(p0, p1, p2, p3, first_ref, cot_ref, vec_ref, rows_out, dz_out, grads_out):
    value = first_ref[...] + ((p0[...] + p1[...]) + (p2[...] + p3[...]) + vec_ref[4:5])
    n, inverse = normed(value)
    rows_out[...] = n * vec_ref[5:6] + vec_ref[6:7]
    up = cot_ref[...]
    dz = norm_back(up, n, inverse, vec_ref[5:6])
    dz_out[...] = dz
    grads_out[...] = jnp.zeros_like(grads_out)
    grads_out[0:1] = colsum(up * n)
    grads_out[1:2] = colsum(up)
    grads_out[2:3] = colsum(dz)


def norm_one_back_kernel(ids, p0, p1, p2, p3, dz_ref, n_ref, inverse_ref, w_ref, vec_ref, *refs):
    dz_out, grads_out = refs[:2]
    parts = refs[2:6]
    up = dz_ref[...] + ((p0[...] + p1[...]) + (p2[...] + p3[...]))
    n = n_ref[...]
    dz = norm_back(up, n, inverse_ref[:, 0:1], vec_ref[2:3])
    dz_out[...] = dz
    grads_out[...] = jnp.zeros_like(grads_out)
    grads_out[0:1] = colsum(up * n)
    grads_out[1:2] = colsum(up)
    grads_out[2:3] = colsum(dz)
    d_att = dot3(dz, w_ref[...], 1, 1)
    lanes = parts[0].shape[1]

    def case(i):
        for k in range(4):
            at = lanes * (i ^ k)
            parts[k][...] = d_att[:, at : at + lanes]

    by_case(ids[HEAD], 4, case)


def stack_rest_kernel(first, source, out):
    out[...] = source[:, first : first + out.shape[1]]


def copy_kernel(source, out):
    out[...] = source[...]


def stack_kernel(*refs):
    for i, ref in enumerate(refs[:-1]):
        refs[-1][i] = ref[...]


def stack_rows(target, refs):
    rows = refs[0].shape[0]
    for k, ref in enumerate(refs):
        target[rows * k : rows * (k + 1), :] = ref[...]


def prepare_kernel(rows_up, slab, up_high, up_low, down_high, down_low):
    for first, count, high, low in (
        (0, rows_up, up_high, up_low),
        (rows_up, slab.shape[1] - rows_up, down_high, down_low),
    ):
        pieces = [slab[w, first : first + count] for w in range(slab.shape[0])]
        high[...], low[...] = split(jnp.concatenate(pieces, axis=0))


def forward_kernel(f0, f1, f2, f3, up_high, up_low, down_high, down_low, vec_ref, *refs):
    pre_out, first_out = refs[:2]
    parts = refs[2:6]
    stack_rows(first_out, (f0, f1, f2, f3))
    pre = dot3s(split(first_out[...]), (up_high[...], up_low[...]), 1, 0) + vec_ref[0:1]
    pre_out[...] = pre
    hidden = 0.5 * pre * (1.0 + lax.erf(pre * (0.5**0.5)))
    branch = dot3s(split(hidden), (down_high[...], down_low[...]), 1, 0)
    rows = f0.shape[0]
    for k in range(4):
        parts[k][...] = branch[rows * k : rows * (k + 1)]


def backward_kernel(z0, z1, z2, z3, pre_ref, up_high, up_low, down_high, down_low, *refs):
    dz_out, d_pre_out = refs[:2]
    parts = refs[2:6]
    stack_rows(dz_out, (z0, z1, z2, z3))
    d_hidden = dot3s(split(dz_out[...]), (down_high[...], down_low[...]), 1, 1)
    pre = pre_ref[...]
    density = jnp.exp(-0.5 * pre * pre) * ((2.0 * jnp.pi) ** -0.5)
    d_pre = d_hidden * (0.5 * (1.0 + lax.erf(pre * (0.5**0.5))) + pre * density)
    d_pre_out[...] = d_pre
    d_first = dot3s(split(d_pre), (up_high[...], up_low[...]), 1, 1)
    rows = z0.shape[0]
    for k in range(4):
        parts[k][...] = d_first[rows * k : rows * (k + 1)]


def ff_weights_kernel(rows_up, rows_down, first_ref, d_pre_ref, pre_ref, dz_ref, out, b_out):
    pre = pre_ref[...]
    hidden = 0.5 * pre * (1.0 + lax.erf(pre * (0.5**0.5)))
    d_pre = d_pre_ref[...]
    b_out[...] = jnp.broadcast_to(colsum(d_pre), b_out.shape)
    up = dot3(first_ref[...], d_pre, 0, 0)
    down = dot3(hidden, dz_ref[...], 0, 0)
    for w in range(out.shape[0]):
        out[w, :rows_up, :] = up[rows_up * w : rows_up * (w + 1)]
        out[w, rows_up:, :] = down[rows_down * w : rows_down * (w + 1)]


def share(ids, outs, places, members, write):
    if len(outs) == 1:
        for place in range(places):
            for z in range(members):
                write(outs[0].at[place, z], place, z)
        return

    def case(core):
        for place in range(places):
            x, f = divmod(place, members)
            j = lax.bitwise_xor(ids[MEMBER], 2 * (f // 2) + x)
            for z in range(members):
                target = outs[core ^ (f % 2)].at[j, lax.bitwise_xor(ids[HEAD], z)]
                write(target, place, z)

    by_case(ids[CORE], 2, case)


def shard_of(place, z, members):
    zh, rest = divmod(place, 2 * members)
    return 2 * (members * zh + z) + rest // members, rest % members


def out_weights_kernel(places, members, ids, att_ref, dz_ref, *outs):
    quarter = outs[0].shape[2]
    a_high, a_low = split(att_ref[...])
    d_high, d_low = split(dz_ref[...])
    value = dot(
        jnp.concatenate([a_high, a_low, a_high], axis=0),
        jnp.concatenate([d_high, d_high, d_low], axis=0),
        0,
        0,
    )

    def write(target, place, z):
        w, f = shard_of(place, z, members)
        at = (w * members + f) * quarter
        target[...] = value[at : at + quarter]

    share(ids, outs, places, members, write)


def sum_cores_kernel(own, came, *outs):
    for j, out in enumerate(outs):
        out[...] = own[j] + came[j]


def qkv_back_kernel(
    rows, span, places, ids, d0, d1, d2, d3, pq_ref, dpq_ref, kv_ref, key_ref, proj_ref, w_ref, *refs
):
    x_ref, dbias_ref, grads_ref, late_ref, up_ref, rows_out = refs[:6]
    outs, turned, up_rows = refs[6:-2], refs[-2], refs[-1]
    heads = pq_ref.shape[0] // 64
    width = heads * 64
    scale = HEAD_DIM**-0.25
    proj = split(proj_ref[...])
    dkv = (d0[...] + d1[...]) + (d2[...] + d3[...])
    for h in range(heads):
        lo, hi = 64 * h, 64 * h + 64
        turned[lo:hi] = scale * dot3s(proj, split(dpq_ref[lo:hi] * pq_ref[lo:hi]), 0, 0)
        pk = dkv[128 * h : 128 * h + 64] * kv_ref[128 * h : 128 * h + 64]
        turned[width + lo : width + hi] = scale * (
            dot3s(proj, split(pk), 0, 0) - key_ref[lo:hi] * colsum(pk)
        )
        turned[2 * width + lo : 2 * width + hi] = dkv[128 * h + 64 : 128 * h + 128]
    d_qkv = turned[...].T
    d_split = split(d_qkv)
    rows_out[...] = dot3s(d_split, split(w_ref[...]), 1, 1)

    members = outs[0].shape[1]
    quarter = rows // members
    d_b = colsum(d_qkv)
    weights = dot3s(split(x_ref[...]), d_split, 0, 0)

    up_rows[...] = jnp.zeros_like(up_rows)
    down = up_ref.shape[1] // up_rows.shape[0]

    def unit(g):
        for w in range(up_rows.shape[0]):
            up_rows[w : w + 1, down * g : down * (g + 1)] = up_ref[0:1, down * w : down * (w + 1)]

    by_case(ids[MEMBER], members, unit)

    def write(target, place, z):
        w, f = shard_of(place, z, members)
        at = (w * members + f) * quarter
        target[:quarter] = weights[at : at + quarter]
        target[quarter:] = jnp.zeros((8, d_b.shape[1]), f32)
        target[quarter : quarter + 1] = d_b
        for i in range(3):
            target[quarter + 1 : quarter + 2, rows * i : rows * (i + 1)] = grads_ref[
                i : i + 1, rows * w : rows * (w + 1)
            ]
            target[quarter + 6 : quarter + 7, rows * i : rows * (i + 1)] = late_ref[
                i : i + 1, rows * w : rows * (w + 1)
            ]
        target[quarter + 2 : quarter + 5, :span] = dbias_ref[0:3, span * w : span * (w + 1)]
        target[quarter + 5 : quarter + 6, : members * down] = up_rows[w : w + 1, : members * down]

    share(ids, outs, places, members, write)


def merge_kernel(rows, skip, ids, r0, r1, r2, r3, w0, w1, w2, w3, out, b_own, bias_out, *rest):
    refs, b_out = (r0, r1, r2, r3), rest[7]
    members = len(refs)
    lanes = r0.shape[1] // 3
    width = lanes * members
    span = bias_out.shape[1]
    quarter = rows // members
    total = (r0[quarter:] + r1[quarter:]) + (r2[quarter:] + r3[quarter:])
    for i in range(3):
        rest[i][...] = total[1:2, rows * i : rows * (i + 1)].reshape(rows)
        rest[3 + i][...] = total[6:7, rows * i : rows * (i + 1)].reshape(rows)
    rest[6][...] = total[5:6, : rest[6].shape[0]].reshape(rest[6].shape)
    last = slice(skip, skip + quarter)
    out[:, 3 * width :] = (w0[last] + w1[last]) + (w2[last] + w3[last])

    def head(t):
        for k, ref in enumerate(refs):
            f = t ^ k
            for p in range(3):
                at = width * p + lanes * f
                out[:, at : at + lanes] = ref[:quarter, lanes * p : lanes * (p + 1)]
                b_out[:, at : at + lanes] = ref[
                    quarter : quarter + 1, lanes * p : lanes * (p + 1)
                ]
            bias_out[3 * f : 3 * f + 3] = ref[quarter + 2 : quarter + 5, :span]

    by_case(ids[HEAD], members, head)
    count = b_own.shape[0]

    def place(w):
        b_own[...] = b_out[:, count * w : count * (w + 1)].reshape(count)

    by_case(ids[WIDE], b_out.shape[1] // count, place)


def place_weights_kernel(ids, r0, r1, r2, r3, w_out, wo_out):
    quarter = r0.shape[0]
    full = w_out.shape[1]

    def own(f):
        for k, ref in enumerate((r0, r1, r2, r3)):
            at = quarter * (f ^ k)
            w_out[at : at + quarter] = ref[:, :full]
            wo_out[at : at + quarter] = ref[:, full:]

    by_case(ids[OWN], 4, own)


def sum_split_kernel(a, b, c, d, *outs):
    for k, out in enumerate(outs):
        out[...] = (a[k] + b[k]) + (c[k] + d[k])


def sum_mixed_kernel(ids, a, b, c, d, rows_ref, *outs):
    rows = rows_ref.shape[0] // len(outs)
    quarter = a.shape[1]
    for k, out in enumerate(outs):
        at = pl.multiple_of(lax.bitwise_xor(ids[HEAD], k) * rows, 8)
        out[:rows] = rows_ref[pl.ds(at, rows), :]
        out[rows : rows + quarter] = (a[k] + b[k]) + (c[k] + d[k])


def sum_kernel(*refs):
    total = refs[0][...]
    for ref in refs[1:-1]:
        total = total + ref[...]
    refs[-1][...] = total


def sum_four_kernel(p0, p1, p2, p3, dz_ref, out):
    rows = out.shape[0]
    out[...] = dz_ref[...] + ((p0[:rows] + p1[:rows]) + (p2[:rows] + p3[:rows]))


def place_kernel(ids, r0, r1, r2, r3, out):
    rows = r0.shape[0]
    for k, ref in enumerate((r0, r1, r2, r3)):
        out[pl.ds(pl.multiple_of(lax.bitwise_xor(ids[OWN], k) * rows, 8), rows), :] = ref[...]


def place_ff_kernel(rows, down, ids, r0, r1, r2, r3, up_out, down_out):
    refs = (r0, r1, r2, r3)
    members = len(refs)

    def own(i):
        for k, ref in enumerate(refs):
            f = i ^ k
            for w in range(up_out.shape[1] // (members * down)):
                at = (w * members + f) * down
                up_out[:, at : at + down] = ref[:rows, down * w : down * (w + 1)]
            down_out[down * f : down * (f + 1)] = ref[rows:]

    by_case(ids[OWN], members, own)


def exchange(value, axes, count, k):
    return lax.ppermute(value, axes, [(i, i ^ k) for i in range(count)])


def swap(value):
    return lax.ppermute(value, ("core", "x"), [(0, 0), (1, 2), (2, 1), (3, 3)])


def place(ids, values, name):
    return call(
        place_kernel,
        [shape(len(values) * values[0].shape[0], values[0].shape[1])],
        [ids, *values],
        name,
        smem=1,
    )[0]


def gather(value, axes, count):
    return [value] + [exchange(value, axes, count, k) for k in range(1, count)]


def relay(value):
    came = exchange(value, "y", 2, 1)
    return [value, exchange(value, "core", 2, 1), came, exchange(came, "core", 2, 1)]


def scatter(parts, axes):
    return [parts[0]] + [exchange(parts[k], axes, len(parts), k) for k in range(1, len(parts))]


def body(
    ys,
    zhs,
    inputs,
    cotangent,
    random_proj,
    position_bias,
    w_qkv,
    b_qkv,
    w_out,
    b_out,
    ln1_gain,
    ln1_bias,
    w_up,
    b_up,
    w_down,
    b_down,
    ln2_gain,
    ln2_bias,
):
    members = 2 * ys
    blocks = 2 * zhs * members
    places = 2 * zhs * members
    few = zhs == 1
    core = lax.axis_index("core")
    x_at, y_at = lax.axis_index("x"), lax.axis_index("y")
    zh_at, zl_at = lax.axis_index("zh"), lax.axis_index("zl")
    feat = 2 * y_at + core
    group = 2 * y_at + x_at
    wide = 2 * (members * zh_at + zl_at) + x_at
    place_at = (2 * zh_at + x_at) * members + feat
    ids = jnp.stack([core, group, feat, zl_at, wide, place_at]).astype(jnp.int32)
    queries, width = inputs.shape
    rows = queries // members
    shard = w_qkv.shape[0]
    quarter = shard // members
    down = w_down.shape[0] // members
    heads = HEADS // members
    lanes = heads * HEAD_DIM
    span = position_bias.shape[1]
    full = 3 * lanes
    length = queries * blocks
    row_shape = shape(rows, width)

    packed = [w_qkv, w_out, position_bias, b_qkv, random_proj.T]
    packed += [b_up, b_out, ln1_gain, ln1_bias, b_down, ln2_gain, ln2_bias]
    got = call(
        functools.partial(pack_qkv_kernel, shard, members),
        [shape(quarter + 8, full)] * members + [shape(rows + -(-quarter // 8) * 8, width), row_shape],
        [ids, inputs, cotangent] + packed,
        "pack_qkv",
        scratch=[
            pltpu.VMEM((quarter, a.shape[1]) if i < 2 and quarter % 8 == 0 else a.shape, f32)
            for i, a in enumerate(packed)
        ]
        + [pltpu.SemaphoreType.DMA((len(packed) + 2,))],
        smem=1,
        limit=60 << 20,
        far=True,
    )
    mixed, cot_rows = got[members:]
    pieces = scatter(got[:members], "zl")
    pack_ids, _ = lax.optimization_barrier((ids, mixed))
    (ff_slab,) = call(
        functools.partial(pack_ff_kernel, members, down),
        [shape(shard + down, width)],
        [pack_ids, w_up, w_down],
        "pack_ff",
        smem=1,
    )
    ff_slab = swap(ff_slab)
    mixed_all = lax.all_gather(mixed, "zl", axis=0)
    pieces, ff_slab = lax.optimization_barrier((pieces, ff_slab))
    (slab,) = call(
        stack_kernel, [shape(members, quarter + 8, full)], pieces, "stack_pieces"
    )
    if few:
        slabs = gather(slab, GROUP, members)
    else:
        slabs = [lax.all_gather(slab, PLANE, axis=0)]
    slabs, mixed_all = lax.optimization_barrier((slabs, mixed_all))
    if few:
        slabs = slabs + [exchange(v, "core", 2, 1) for v in slabs]
    slabs, ff_slab = lax.optimization_barrier((slabs, ff_slab))
    ff_slab = lax.all_gather(ff_slab, LINES, axis=0)
    spare = 1 if quarter % 8 == 0 else blocks * members
    got = call(
        functools.partial(qkv_kernel, shard, members, (b_qkv.shape[0], span, down), few),
        [
            shape(width, full),
            shape(queries, width),
            shape(lanes, queries),
            shape(2 * lanes, queries),
            shape(lanes, queries),
            shape(FEATURES, HEAD_DIM),
            shape(8, 2 * length),
            shape(8, width),
        ],
        [ids, mixed_all, *slabs],
        "qkv",
        scratch=[
            pltpu.VMEM((blocks, 8, full), f32),
            pltpu.VMEM((spare, quarter, full), f32),
            pltpu.VMEM((FEATURES, 1, HEAD_DIM), f32),
        ],
        smem=1,
        deep=True,
        late=range(2, 2 + len(slabs)) if few else (),
    )
    w_cols, x, pq, kv, keys, proj, bias, vec = got

    if few:
        kv_own = gather(kv, GROUP, members)
        kv_all = kv_own + [exchange(v, "core", 2, 1) for v in kv_own]
        (wo_parts,) = call(
            functools.partial(stack_rest_kernel, rows),
            [shape(members, quarter, width)],
            [mixed_all],
            "stack_out",
        )
        wo_parts, _ = lax.optimization_barrier((wo_parts, kv_all))
        wo_own = gather(wo_parts, GROUP, members)
    else:
        kv_all = lax.all_gather(kv, PLANE, axis=0)
    got = attention(ids, kv_all, pq, bias)
    att, den = got[:2]
    att_parts = scatter(got[2:], "zl")
    if few:
        wo_own, _ = lax.optimization_barrier((wo_own, att_parts[2]))
        wo_all = wo_own + [exchange(v, "core", 2, 1) for v in wo_own]
        (w_full,) = call(
            functools.partial(weights_out_kernel, shard),
            [shape(width, width)],
            [ids, *wo_all],
            "weights_out",
            smem=1,
        )
    else:
        w_full = lax.all_gather(w_out, ("zh", "zl", "x"), axis=0, tiled=True)

    first, norm_rows, inverse, att_rows = call(
        norm_one_kernel,
        [row_shape, row_shape, shape(rows, 128), row_shape],
        [ids, *att_parts, mixed, w_full, vec],
        "norm_one",
        smem=1,
    )
    first, ff_slab = lax.optimization_barrier((first, ff_slab))
    firsts = gather(first, GROUP, members)
    full_rows = shape(queries, blocks * down)
    ff_matrices = call(
        functools.partial(prepare_kernel, shard),
        [shape(width, blocks * down, dtype=bf16)] * 2
        + [shape(blocks * down, width, dtype=bf16)] * 2,
        [ff_slab],
        "prepare",
    )
    got = call(
        forward_kernel,
        [full_rows, shape(queries, width)] + [row_shape] * members,
        [*firsts, *ff_matrices, vec],
        "forward",
    )
    pre, first_all = got[:2]
    parts = scatter(got[2:], GROUP)
    out_rows, dz2, grads_two = call(
        norm_two_kernel,
        [row_shape, row_shape, shape(8, width)],
        [*parts, first, cot_rows, vec],
        "norm_two",
    )
    dzs = gather(dz2, GROUP, members)
    got = call(
        backward_kernel,
        [shape(queries, width), full_rows] + [row_shape] * members,
        [*dzs, pre, *ff_matrices],
        "backward",
    )
    dz2_all, d_pre = got[:2]
    parts = scatter(got[2:], GROUP)

    head_rows = shape(rows, lanes)
    got = call(
        norm_one_back_kernel,
        [row_shape, shape(8, width)] + [head_rows] * members,
        [ids, *parts, dz2, norm_rows, inverse, w_full, vec],
        "norm_one_back",
        smem=1,
    )
    dz1, grads_one = got[:2]
    grads = scatter(got[2:], "zl")
    first_all, d_pre, pre, dz2_all, _ = lax.optimization_barrier(
        (first_all, d_pre, pre, dz2_all, dz1)
    )
    ff_grads, up_row = call(
        functools.partial(ff_weights_kernel, shard, down),
        [shape(blocks, shard + down, width), shape(8, blocks * down)],
        [first_all, d_pre, pre, dz2_all],
        "ff_weights",
    )


    part = shape(members, members, quarter, width)
    out_shares = call(
        functools.partial(out_weights_kernel, places, members),
        [part, part] if few else [shape(places, members, quarter, width)],
        [ids, att_rows, dz1],
        "out_weights",
        smem=1,
    )
    def sum_cores(own, other, name):
        came = exchange(other, "core", 2, 1)
        if name == "sum_keys":
            (own,) = call(copy_kernel, [shape(*own.shape)], [own], "load_keys")
        return call(sum_cores_kernel, [shape(*own.shape[1:])] * members, [own, came], name)

    if few:
        out_shares = sum_cores(*out_shares, "sum_out")
        grads, out_shares, ff_grads = lax.optimization_barrier((grads, out_shares, ff_grads))
        out_shares = scatter(out_shares, GROUP)
    else:
        grads, ff_grads = lax.optimization_barrier((grads, ff_grads))
    ff_grads = lax.psum_scatter(ff_grads, LINES, scatter_dimension=0, tiled=False)
    out_came, out_core = exchange(out_rows, "y", 2, 1), exchange(out_rows, "core", 2, 1)
    back = attention_back(ids, kv_all, pq, bias, att, den, grads)
    back, out_came, out_core = lax.optimization_barrier((back, out_came, out_core))
    if few:
        back, out_shares = lax.optimization_barrier((back, out_shares))
        arrived = scatter(sum_cores(back[0], back[1], "sum_keys"), GROUP)
    else:
        arrived = lax.psum_scatter(back[0], PLANE, scatter_dimension=0, tiled=False)
        arrived = [arrived] + [jnp.zeros_like(arrived)] * 3
    dpq, dbias = back[-2:]
    out_parts = [out_rows, out_core, out_came, exchange(out_came, "core", 2, 1)]
    output = place(ids, out_parts, "place_output")
    arrived, output = lax.optimization_barrier((arrived, output))

    part = shape(members, members, quarter + 8, full)
    got = call(
        functools.partial(qkv_back_kernel, shard, span, places),
        [shape(queries, width)]
        + ([part, part] if few else [shape(places, members, quarter + 8, full)]),
        [ids, *arrived, pq, dpq, kv, keys, proj, w_cols, x, dbias, grads_one, grads_two, up_row],
        "qkv_back",
        scratch=[
            pltpu.VMEM((full, queries), f32),
            pltpu.VMEM((blocks, -(-members * down // 128) * 128), f32),
        ],
        smem=1,
    )
    shares_out = got[1:]
    piece = shape(rows + -(-quarter // 8) * 8, width)
    if few:
        mixed_grads = call(
            sum_mixed_kernel, [piece] * members, [ids, *out_shares, got[0]], "sum_mixed", smem=1
        )
    else:
        part = lax.psum_scatter(out_shares[0], PLANE, scatter_dimension=0, tiled=False)
        part = jnp.concatenate(
            [got[0].reshape(members, rows, width), part], axis=1
        )
        part = jnp.pad(part, ((0, 0), (0, piece.shape[0] - part.shape[1]), (0, 0)))
        mixed_grads = [
            lax.dynamic_index_in_dim(part, zl_at ^ k, 0, keepdims=False) for k in range(members)
        ]

    def split_plane(parts, piece, name):
        if few:
            return call(sum_split_kernel, [piece] * members, parts, name)
        part = lax.psum_scatter(parts[0], PLANE, scatter_dimension=0, tiled=False)
        return [
            lax.dynamic_index_in_dim(part, zl_at ^ k, 0, keepdims=False) for k in range(members)
        ]

    if few:
        shares_out = sum_cores(*shares_out, "sum_qkv")
    shares_out, mixed_grads, ff_grads = lax.optimization_barrier(
        (shares_out, mixed_grads, ff_grads)
    )
    ff_grads = swap(ff_grads)
    mine = scatter(shares_out, GROUP) if few else shares_out
    mixed_grads = scatter(mixed_grads, "zl")
    mine, mixed_grads = lax.optimization_barrier((mine, mixed_grads))
    mine = split_plane(mine, shape(quarter + 8, full), "sum_qkv_plane")
    mine, ff_grads = lax.optimization_barrier((mine, ff_grads))
    (d_input_rows,) = call(sum_four_kernel, [row_shape], [*mixed_grads, dz1], "sum_rows")
    ff_came = exchange(ff_grads, "y", 2, 1)
    input_came = exchange(d_input_rows, "y", 2, 1)
    mine = scatter(mine, "zl")
    got = call(
        functools.partial(merge_kernel, shard, rows),
        [
            shape(quarter, 4 * width),
            shape(*b_qkv.shape),
            shape(*position_bias.shape),
        ]
        + [shape(shard)] * 6
        + [shape(*b_up.shape)],
        [ids, *mine, *mixed_grads],
        "merge",
        scratch=[pltpu.VMEM((1, 3 * width), f32)],
        smem=1,
    )
    merged, d_b_qkv, d_position_bias, d_ln1_gain, d_ln1_bias, d_b_out = got[:6]
    d_ln2_gain, d_ln2_bias, d_b_down, d_b_up = got[6:]
    merged_came = exchange(merged, "y", 2, 1)

    def relayed(value, came):
        return [value, exchange(value, "core", 2, 1), came, exchange(came, "core", 2, 1)]

    ff_came, input_came, _ = lax.optimization_barrier((ff_came, input_came, merged))
    d_inputs = place(ids, relayed(d_input_rows, input_came), "place_inputs")
    ff_parts = relayed(ff_grads, ff_came)
    d_w_up, d_w_down = call(
        functools.partial(place_ff_kernel, shard, down),
        [shape(shard, w_up.shape[1]), shape(*w_down.shape)],
        [ids, *ff_parts],
        "place_ff",
        smem=1,
    )
    merged_came, d_inputs, d_w_up, d_w_down = lax.optimization_barrier(
        (merged_came, d_inputs, d_w_up, d_w_down)
    )
    d_w_qkv, d_w_out = call(
        place_weights_kernel,
        [shape(*w_qkv.shape), shape(shard, width)],
        [ids, *relayed(merged, merged_came)],
        "place_weights",
        smem=1,
    )

    return (
        output,
        d_inputs,
        d_position_bias,
        d_w_qkv,
        d_b_qkv,
        d_w_out,
        d_b_out,
        d_ln1_gain,
        d_ln1_bias,
        d_w_up,
        d_b_up,
        d_w_down,
        d_b_down,
        d_ln2_gain,
        d_ln2_bias,
    )


def solution(mesh):
    feats, wides = mesh.shape["feat"], mesh.shape["wide"]
    ys, zhs = feats // 2, wides // (2 * feats)
    fine = Mesh(mesh.devices.reshape(ys, 2, zhs, feats, 2), ("y", "core", "zh", "zl", "x"))
    wide = ("zh", "zl", "x")
    mat, vector, lane = P(wide, None), P(wide), P(None, wide)
    return jax.shard_map(
        functools.partial(body, ys, zhs),
        mesh=fine,
        in_specs=(mat, mat, P(None, FEAT), lane, mat, vector, mat, vector)
        + (vector, vector, mat, vector, mat, vector, vector, vector),
        out_specs=(mat, mat, lane, mat, vector, mat, vector, vector)
        + (vector, mat, vector, mat, vector, vector, vector),
        check_vma=False,
    )
```

```python
import functools
import math

import jax
import jax.numpy as jnp
from jax import lax
from jax.experimental import pallas as pl
from jax.experimental.pallas import tpu as pltpu
from jax.sharding import Mesh
from jax.sharding import PartitionSpec as P

HEADS = 12
HEAD_DIM = 64
FEATURES = 64
EPS = 1e-06
f32 = jnp.float32
bf16 = jnp.bfloat16

GROUP = ("y", "x")
FEAT = ("y", "core")
PLANE = ("zh", "x", "y", "core")
LINES = ("zh", "zl", "core")
CORE, MEMBER, OWN, HEAD, WIDE, PLACE = range(6)


def split(value):
    high = value.astype(bf16)
    return high, (value - high.astype(f32)).astype(bf16)


def dot(a, b, ca, cb):
    return lax.dot_general(a, b, (((ca,), (cb,)), ((), ())), preferred_element_type=f32)


def dot3s(a, b, ca, cb):
    return dot(a[0], b[0], ca, cb) + (dot(a[0], b[1], ca, cb) + dot(a[1], b[0], ca, cb))


def dot3(a, b, ca, cb):
    return dot3s(split(a), split(b), ca, cb)


def cost():
    return pl.CostEstimate(flops=1 << 20, bytes_accessed=1 << 10, transcendentals=0)


def tiled(dims):
    if len(dims) < 2:
        return 0
    return math.prod(dims[:-2]) * -(-dims[-2] // 8) * -(-dims[-1] // 128) * 4096


def call(kernel, outs, args, name, scratch=(), smem=0, room=8, limit=0, fetch=(), push=(), far=False, deep=False, late=None, stream=()):
    held = sum(tiled(ref.shape) for ref in scratch)
    held += sum(size for size in map(lambda a: tiled(a.shape), [*args, *outs]) if size > 4 << 20)
    if deep and not far:
        fetch = [i for i in range(smem, len(args)) if i not in stream]
        push, limit = range(len(outs)), 60 << 20
    fetch, push = tuple(fetch), tuple(push)
    near = [pltpu.VMEM(args[i].shape, args[i].dtype) for i in fetch]
    near += [pltpu.VMEM(outs[i].shape, outs[i].dtype) for i in push]
    held += sum(args[i].size * args[i].dtype.itemsize for i in fetch)
    held += sum(outs[i].size * outs[i].dtype.itemsize for i in push)
    count = len(args) + len(outs)
    flow = []
    if stream:
        first = args[stream[0]]
        flow = [
            pltpu.VMEM((len(stream),) + first.shape, first.dtype),
            pltpu.SemaphoreType.DMA((len(stream),)),
        ]

    def moved(*refs):
        whole, own = list(refs[:count]), refs[count : count + len(scratch)]
        spare, sems = refs[count + len(scratch) : -1 - len(flow)], refs[-1 - len(flow)]
        copies, after = [], []
        for at, (i, ref) in enumerate(zip(fetch, spare)):
            copies.append(pltpu.make_async_copy(whole[i], ref, sems.at[at]))
            whole[i] = ref
        for at, (i, ref) in enumerate(zip(push, spare[len(fetch) :])):
            i += len(args)
            after.append(pltpu.make_async_copy(ref, whole[i], sems.at[len(fetch) + at]))
            whole[i] = ref
        for copy in copies:
            copy.start()
        if flow:
            held, flow_sems = refs[-2:]
            for i, at in enumerate(stream):
                pltpu.make_async_copy(whole[at], held.at[i], flow_sems.at[i]).start()
        for i, copy in zip(fetch, copies):
            if late is None or i not in late:
                copy.wait()
        started = []

        def arrive(i):
            copies[fetch.index(i)].wait()

        def start(i):
            started.append(push.index(i))
            after[started[-1]].start()

        def wait(i):
            pltpu.make_async_copy(held.at[i], held.at[i], flow_sems.at[i]).wait()

        if flow:
            whole = [ref for i, ref in enumerate(whole) if i not in stream]
            kernel(*whole, *own, held=held, wait=wait, start=start)
        elif late is not None:
            kernel(*whole, *own, arrive=arrive, start=start)
        else:
            kernel(*whole, *own)
        for i, copy in enumerate(after):
            if i not in started:
                copy.start()
        for copy in after:
            copy.wait()

    def spec(i, which):
        return pl.BlockSpec(memory_space=pltpu.HBM if i in which else pltpu.VMEM)

    return pl.pallas_call(
        moved if near else kernel,
        out_shape=outs,
        in_specs=[pl.BlockSpec(memory_space=pltpu.SMEM)] * smem
        + [
            spec(i, range(len(args)) if far else (*fetch, *stream))
            for i in range(smem, len(args))
        ],
        out_specs=[spec(i, push) for i in range(len(outs))],
        scratch_shapes=list(scratch)
        + near
        + ([pltpu.SemaphoreType.DMA((len(near),))] if near else [])
        + flow,
        compiler_params=pltpu.CompilerParams(vmem_limit_bytes=limit or held + (room << 20)),
        cost_estimate=cost(),
        name=name,
    )(*args)


def when(condition):
    if isinstance(condition, bool):
        return lambda run: run() if condition else None
    return pl.when(condition)


def shape(*dims, dtype=f32):
    return jax.ShapeDtypeStruct(dims, dtype)


def by_case(value, count, run):
    for i in range(count):
        pl.when(value == i)(functools.partial(run, i))


def pack_qkv_kernel(rows, members, ids, *refs):
    count = (len(refs) - members - 3) // 2 + 1
    sources, pieces = refs[:count], refs[count : count + members]
    mixed, cot_out = refs[count + members : count + members + 2]
    held, sems = refs[count + members + 2 : -1], refs[-1]
    part = cot_out.shape[0]
    at = pl.multiple_of(ids[OWN] * part, 8)
    copies = [
        pltpu.make_async_copy(source.at[pl.ds(at, part)], target, sems.at[i])
        for i, (source, target) in enumerate(
            zip(sources[:2], (mixed.at[pl.ds(0, part)], cot_out))
        )
    ]
    quarter = rows // members
    for i, (source, target) in enumerate(zip(sources[2:], held)):
        if source.shape != target.shape:
            source = source.at[pl.ds(pl.multiple_of(ids[OWN] * quarter, 8), quarter)]
        copies.append(pltpu.make_async_copy(source, target, sems.at[2 + i]))
    for copy in copies:
        copy.start()
    for copy in copies:
        copy.wait()
    w_ref, out_ref, bias_ref, b_ref, proj_ref, up_ref = held[:6]
    width = w_ref.shape[1] // 3
    lanes = width // members
    heads = bias_ref.shape[0] // members
    for piece in pieces:
        piece[quarter:, :] = jnp.zeros((8, 3 * lanes), f32)
        piece[quarter : quarter + 1, : b_ref.shape[0]] = b_ref[...].reshape(1, -1)
        for i, ref in enumerate(held[6:]):
            row, lane = (4, i) if i < 5 else (5, 0)
            piece[quarter + row : quarter + row + 1, lane * rows : (lane + 1) * rows] = ref[
                ...
            ].reshape(1, -1)
        piece[quarter + 5 : quarter + 6, rows : rows + up_ref.shape[0]] = up_ref[...].reshape(1, -1)
        per = 3 * lanes // HEAD_DIM
        for i in range(proj_ref.shape[0]):
            row, lane = quarter + 6 + i // per, HEAD_DIM * (i % per)
            piece[row : row + 1, lane : lane + HEAD_DIM] = proj_ref[i : i + 1]

    def own(f):
        first = 0 if w_ref.shape[0] == quarter else quarter * f
        mixed[part : part + quarter] = out_ref[first : first + quarter]

        def head(t):
            for k, piece in enumerate(pieces):
                to = t ^ k
                for p in range(3):
                    at = width * p + lanes * to
                    piece[:quarter, lanes * p : lanes * (p + 1)] = w_ref[
                        first : first + quarter, at : at + lanes
                    ]
                piece[quarter + 1 : quarter + 1 + heads, : bias_ref.shape[1]] = bias_ref[
                    heads * to : heads * (to + 1)
                ]

        by_case(ids[HEAD], members, head)

    by_case(ids[OWN], members, own)


def pack_ff_kernel(members, down, ids, up_ref, down_ref, out):
    rows = up_ref.shape[0]
    blocks = up_ref.shape[1] // (members * down)

    def case(i):
        for w in range(blocks):
            at = (w * members + i) * down
            out[:rows, down * w : down * (w + 1)] = up_ref[:, at : at + down]
        out[rows : rows + down, :] = down_ref[down * i : down * (i + 1)]

    by_case(ids[OWN], members, case)


def plane_place(ids, members, few, i):
    if not few:
        zh, rest = divmod(i, 2 * members)
        return zh, rest // members, rest % members
    other, j = divmod(i, members)
    member = lax.bitwise_xor(ids[MEMBER], j)
    return 0, lax.rem(member, 2), 2 * lax.div(member, 2) + lax.bitwise_xor(ids[CORE], other)


def qkv_kernel(rows, members, spans, few, ids, *refs, arrive=None, start=None):
    mixed, refs = refs[0], refs[1:]
    w_out, x_out, pq_out, kv_out, key_out, proj_out, bias_out, vec_out, extra, held, directions = refs[-11:]
    slabs = refs[:-11]
    slabs = list(slabs) if few else [slabs[0].at[i] for i in range(slabs[0].shape[0])]
    width = x_out.shape[1]
    blocks = extra.shape[0]
    full = w_out.shape[1]
    lanes = full // 3
    heads = lanes // HEAD_DIM
    quarter = rows // members
    part = x_out.shape[0] // members
    for z in range(members):
        x_out[part * z : part * (z + 1), :] = mixed[z, :part]
    for i, slab in enumerate(slabs):
        if arrive is not None and few:
            arrive(2 + i)
        zh, x, f = plane_place(ids, members, few, i)
        for k in range(members):
            w = 2 * (members * zh + lax.bitwise_xor(ids[HEAD], k)) + x
            if i < 2 if few else f == 0:
                extra[w] = slab[k, quarter:]
            if quarter % 8 == 0:
                at = pl.multiple_of(w * rows + f * quarter, 8)
                w_out[pl.ds(at, quarter), :] = slab[k, :quarter]
            else:
                held[w * members + f] = slab[k, :quarter]
    if quarter % 8:
        for i in range(held.shape[0]):
            w_out[quarter * i : quarter * (i + 1)] = held[i]

    share = FEATURES // members
    per = full // HEAD_DIM
    for i, slab in enumerate(slabs):
        zh, x, f = plane_place(ids, members, few, i)
        if few or (zh, x) == (0, 0):
            for r in range(share):
                at, lane = quarter + 6 + r // per, HEAD_DIM * (r % per)
                directions[share * f + r] = slab[0, at : at + 1, lane : lane + HEAD_DIM]
    for r in range(FEATURES):
        proj_out[r : r + 1, :] = directions[r]
    bias_out[...] = jnp.zeros_like(bias_out)
    b_row = []
    for w in range(blocks):
        b_row.append(extra[w, 0:1, : spans[0]])
        count = spans[1]
        bias_out[:heads, count * w : count * (w + 1)] = extra[w, 1 : 1 + heads, :count]
        for i in range(6):
            row, lane = (4, i) if i < 5 else (5, 0)
            vec_out[1 + i : 2 + i, rows * w : rows * (w + 1)] = extra[
                w, row : row + 1, lane * rows : (lane + 1) * rows
            ]
    vec_out[7:8] = jnp.zeros((1, width), f32)
    b_row = jnp.concatenate(b_row, axis=1)

    def unit(g):
        count = spans[2]
        for w in range(blocks):
            vec_out[0:1, count * w : count * (w + 1)] = extra[
                w, 5:6, rows + count * g : rows + count * (g + 1)
            ]

    by_case(ids[MEMBER], members, unit)
    if start is not None:
        for i in (0, 1, 5, 6, 7):
            start(i)
    qkv = dot3(x_out[...], w_out[...], 1, 0)
    scale = HEAD_DIM**-0.25
    proj = split(proj_out[...])

    def head(t):
        bias = [b_row[:, width * p + lanes * t : width * p + lanes * (t + 1)] for p in range(3)]
        turned = (qkv + jnp.concatenate(bias, axis=1)).T
        for h in range(heads):
            lo, hi = HEAD_DIM * h, HEAD_DIM * (h + 1)
            q = turned[lo:hi] * scale
            k = turned[lanes + lo : lanes + hi] * scale
            pq_out[lo:hi] = jnp.exp(dot3s(proj, split(q), 1, 0))
            pk = dot3s(proj, split(k), 1, 0) - 0.5 * jnp.sum(k * k, axis=0, keepdims=True)
            kv_out[128 * h : 128 * h + 64] = jnp.exp(pk)
            kv_out[128 * h + 64 : 128 * h + 128] = turned[2 * lanes + lo : 2 * lanes + hi]
            key_out[lo:hi] = k

    by_case(ids[HEAD], members, head)


def rolled_rows(table, row):
    wide = jnp.broadcast_to(row, (8, row.shape[1]))
    return pltpu.roll(wide, 0, 1, stride=1, stride_axis=0)


def make_tables(tables, bias_ref, heads):
    length = bias_ref.shape[1]
    for h in range(heads):
        rows = rolled_rows(None, jnp.exp(bias_ref[h : h + 1]))
        tables[0, 8 * h : 8 * h + 8] = rows
        tables[1, 8 * h : 8 * h + 8] = pltpu.roll(rows, length - 64, 1)


def factor_tile(windows):
    first = lax.broadcasted_iota(jnp.int32, (8, 128), 1) < 64
    pairs = {}
    for g in range(8):
        for d in range(-3, 3):
            low = pltpu.roll(windows[d + 3], (8 * g + 64) % 128, 1)
            high = windows[d + 4] if g == 0 else pltpu.roll(windows[d + 4], 8 * g, 1)
            pairs[d, g] = jnp.where(first, low, high)
    rows = []
    for z in range(4):
        for g in range(8):
            rows.append(jnp.concatenate([pairs[-z, g], pairs[2 - z, g]], axis=1))
    return jnp.concatenate(rows, axis=0)


def window_sums(pairs):
    first = lax.broadcasted_iota(jnp.int32, (8, 128), 1) < 64
    sums = [jnp.zeros((8, 128), f32) for _ in range(7)]
    for g in range(8):
        for d in range(-3, 3):
            total = None
            for z in range(4):
                for p in range(2):
                    if 2 * p - z == d:
                        term = pairs[64 * z + 8 * g : 64 * z + 8 * g + 8, 128 * p : 128 * p + 128]
                        total = term if total is None else total + term
            low = pltpu.roll(jnp.where(first, total, 0.0), 64 - 8 * g, 1)
            high = jnp.where(first, 0.0, total)
            sums[d + 3] = sums[d + 3] + low
            sums[d + 4] = sums[d + 4] + (high if g == 0 else pltpu.roll(high, 128 - 8 * g, 1))
    return sums


def window_start(ids, members, groups, seg, length, n):
    if groups == 1:
        other, j = n // members, n % members
        member = lax.bitwise_xor(ids[MEMBER], j)
        zh, x = ids[PLACE] * 0, lax.rem(member, 2)
        f = 2 * lax.div(member, 2) + lax.bitwise_xor(ids[CORE], other)
    else:
        zh, x, f = n // (2 * members), lax.rem(lax.div(n, members), 2), lax.rem(n, members)
    own = ids[PLACE]
    away = 8 * members * (lax.div(own, 2 * members) - zh)
    away += members * (lax.rem(lax.div(own, members), 2) - x) + ids[OWN] - f
    start = away + length // (2 * seg) - 1
    odd = lax.rem(start, 2)
    return start - odd, odd


def window_at(start, d):
    return pl.multiple_of(start * 64 + 512 * d, 128)


def split_block(block, h, kcat, vcat):
    for part, cat in ((0, kcat), (64, vcat)):
        high, low = split(block[128 * h + part : 128 * h + part + 64])
        cat[h, 0:64] = high
        cat[h, 64:128] = low
        cat[h, 128:192] = high


def attention_kernel(groups, blocks, ids, *refs, held=None, wait=None, start=None):
    if groups > 1:
        held, refs = refs[0], refs[1:]
    pq_ref, bias_ref, att_out, den_out = refs[:4]
    parts = refs[4:8]
    tables, qcat, out_rows, kcat, vcat = refs[8:]
    heads = pq_ref.shape[0] // 64
    queries = pq_ref.shape[1]
    step = pl.program_id(0) if groups > 1 else 0

    @when(step == 0)
    def _():
        make_tables(tables, bias_ref, heads)
        for h in range(heads):
            high, low = split(pq_ref[64 * h : 64 * h + 64])
            qcat[h, 0:64] = high
            qcat[h, 64:128] = high
            qcat[h, 128:192] = low
        att_out[...] = jnp.zeros_like(att_out)
        den_out[...] = jnp.zeros_like(den_out)

    def advance(n, carry):
        first, odd = window_start(ids, 4, groups, 64, bias_ref.shape[1], step * blocks + n)
        if wait is not None:
            wait(n)
        for h in range(heads):
            split_block(held.at[n], h, kcat.at[n], vcat.at[n])
            scores = dot(kcat[n, h], qcat[h], 0, 0)
            rows = slice(8 * h, 8 * h + 8)
            windows = [
                tables[odd, rows, pl.ds(window_at(first, d), 128)] for d in range(-3, 4)
            ]
            weight = scores * factor_tile(windows)
            high, low = split(weight)
            both = dot(vcat[n, h, 0:128], high, 1, 0)
            more = dot(vcat[n, h, 0:64], low, 1, 0)
            att_out[64 * h : 64 * h + 64] += both[0:64] + both[64:128] + more
            den_out[h : h + 1] += jnp.sum(weight, axis=0, keepdims=True)
        return carry

    lax.fori_loop(0, blocks, advance, 0, unroll=2)

    @when(step == groups - 1)
    def _():
        for h in range(heads):
            att_out[64 * h : 64 * h + 64] = att_out[64 * h : 64 * h + 64] / den_out[h : h + 1]
        out_rows[...] = att_out[...].T
        rows = queries // 4
        for k in range(4):
            first = pl.multiple_of(lax.bitwise_xor(ids[HEAD], k) * rows, 8)
            parts[k][...] = out_rows[pl.ds(first, rows), :]


def attention(ids, kv, pq, window):
    stacked = not isinstance(kv, list)
    count = kv.shape[0] if stacked else len(kv)
    blocks = 8 if stacked else count
    groups = count // blocks
    queries = pq.shape[1]
    heads = pq.shape[0] // 64
    rows = shape(queries // 4, heads * 64)
    outs = [shape(heads * 64, queries), shape(8, queries)] + [rows] * 4
    scratch = [
        pltpu.VMEM((2, 8 * heads, window.shape[1]), f32),
        pltpu.VMEM((heads, 192, queries), bf16),
        pltpu.VMEM((queries, heads * 64), f32),
        pltpu.VMEM((blocks, heads, 192, queries), bf16),
        pltpu.VMEM((blocks, heads, 192, queries), bf16),
    ]
    kernel = functools.partial(attention_kernel, groups, blocks)
    if not stacked:
        args = [ids, *kv, pq, window]
        stream = range(1, 1 + count)
        return call(kernel, outs, args, "attention", scratch, 1, deep=True, stream=stream)
    whole = lambda a: pl.BlockSpec(a.shape, lambda g, nd=len(a.shape): (0,) * nd)
    smem = pl.BlockSpec(memory_space=pltpu.SMEM)
    kv_spec = pl.BlockSpec((blocks,) + kv.shape[1:], lambda g: (g, 0, 0))
    return pl.pallas_call(
        kernel,
        grid=(groups,),
        out_shape=outs,
        in_specs=[smem, kv_spec, whole(pq), whole(window)],
        out_specs=[whole(a) for a in outs],
        scratch_shapes=scratch,
        compiler_params=pltpu.CompilerParams(vmem_limit_bytes=52 << 20),
        name="attention",
    )(ids, kv, pq, window)


def attention_back_kernel(groups, blocks, ids, *refs, held=None, wait=None, start=None):
    if groups > 1:
        held, refs = refs[0], refs[1:]
    pq_ref, bias_ref, att_ref, den_ref = refs[:4]
    grads = refs[4:8]
    if groups == 1:
        own, other, dpq_out, dbias_out = refs[8:12]
    else:
        dkv, dpq_out, dbias_out = refs[8:11]
    tables, qcat, gcat, gden, diag, grad_rows, kcat, vcat = refs[-8:]
    heads = pq_ref.shape[0] // 64
    queries = pq_ref.shape[1]
    step = pl.program_id(0) if groups > 1 else 0

    @when(step == 0)
    def _():
        rows = queries // 4
        for k in range(4):
            first = pl.multiple_of(lax.bitwise_xor(ids[HEAD], k) * rows, 8)
            grad_rows[pl.ds(first, rows), :] = grads[k][...]
        make_tables(tables, bias_ref, heads)
        d_att = grad_rows[...].T
        gden[...] = jnp.zeros_like(gden)
        for h in range(heads):
            lo, hi = 64 * h, 64 * h + 64
            for value, cat in ((pq_ref[lo:hi], qcat), (d_att[lo:hi] / den_ref[h : h + 1], gcat)):
                high, low = split(value)
                cat[h, 0:64] = high
                cat[h, 64:128] = high
                cat[h, 128:192] = low
            gden[h : h + 1] = -(
                jnp.sum(d_att[lo:hi] * att_ref[lo:hi], axis=0, keepdims=True) / den_ref[h : h + 1]
            )
        dpq_out[...] = jnp.zeros_like(dpq_out)
        diag[...] = jnp.zeros_like(diag)

    def advance(dkv, first, n, carry):
        begin, odd = window_start(ids, 4, groups, 64, bias_ref.shape[1], step * blocks + n)
        if wait is not None:
            wait(n)
        for h in range(heads):
            split_block(held.at[n], h, kcat.at[n], vcat.at[n])
            scores = dot(kcat[n, h], qcat[h], 0, 0)
            rows = slice(8 * h, 8 * h + 8)
            factor = factor_tile(
                [tables[odd, rows, pl.ds(window_at(begin, d), 128)] for d in range(-3, 4)]
            )
            d_weight = dot(vcat[n, h], gcat[h], 0, 0) + gden[h : h + 1]
            w_high, w_low = split(scores * factor)
            e_high, e_low = split(d_weight * factor)
            pairs = d_weight * scores
            both = dot(gcat[h, 64:192], w_high, 1, 1)
            dv = both[0:64] + both[64:128] + dot(gcat[h, 0:64], w_low, 1, 1)
            both = dot(qcat[h, 64:192], e_high, 1, 1)
            dk = both[0:64] + both[64:128] + dot(qcat[h, 0:64], e_low, 1, 1)
            both = dot(kcat[n, h, 0:128], e_high, 1, 0)
            dq = both[0:64] + both[64:128] + dot(kcat[n, h, 0:64], e_low, 1, 0)
            dpq_out[64 * h : 64 * h + 64] += dq
            dkv[n - first, 128 * h : 128 * h + 64] = dk
            dkv[n - first, 128 * h + 64 : 128 * h + 128] = dv
            for i, total in enumerate(window_sums(pairs)):
                diag[odd, rows, pl.ds(window_at(begin, i - 3), 128)] += total
        return carry

    if groups == 1:
        half = blocks // 2
        lax.fori_loop(half, blocks, functools.partial(advance, other, half), 0, unroll=2)
        if start is not None:
            start(1)
        lax.fori_loop(0, half, functools.partial(advance, own, 0), 0, unroll=2)
        if start is not None:
            start(0)
    else:
        lax.fori_loop(0, blocks, functools.partial(advance, dkv, 0), 0)

    @when(step == groups - 1)
    def _():
        length = diag.shape[2]
        dbias_out[...] = jnp.zeros_like(dbias_out)
        for h in range(heads):
            both = diag[0, 8 * h : 8 * h + 8] + pltpu.roll(diag[1, 8 * h : 8 * h + 8], 64, 1)
            total = both[0:1]
            for s in range(1, 8):
                total = total + pltpu.roll(both[s : s + 1], length - s, 1)
            dbias_out[h : h + 1] = total * jnp.exp(bias_ref[h : h + 1])


def attention_back(ids, kv, pq, window, att, den, grads):
    stacked = not isinstance(kv, list)
    count = kv.shape[0] if stacked else len(kv)
    blocks = 8 if stacked else count
    groups = count // blocks
    queries = pq.shape[1]
    heads = pq.shape[0] // 64
    outs = [shape(heads * 64, queries), shape(8, window.shape[1])]
    scratch = [
        pltpu.VMEM((2, 8 * heads, window.shape[1]), f32),
        pltpu.VMEM((heads, 192, queries), bf16),
        pltpu.VMEM((heads, 192, queries), bf16),
        pltpu.VMEM((8, queries), f32),
        pltpu.VMEM((2, 8 * heads, window.shape[1]), f32),
        pltpu.VMEM((queries, heads * 64), f32),
        pltpu.VMEM((blocks, heads, 192, queries), bf16),
        pltpu.VMEM((blocks, heads, 192, queries), bf16),
    ]
    kernel = functools.partial(attention_back_kernel, groups, blocks)
    small = [pq, window, att, den] + list(grads)
    if not stacked:
        half = shape(count // 2, heads * 128, queries)
        return call(
            kernel,
            [half, half] + outs,
            [ids, *kv] + small,
            "attention_back",
            scratch,
            1,
            deep=True,
            stream=range(1, 1 + count),
        )
    whole = lambda a: pl.BlockSpec(a.shape, lambda g, nd=len(a.shape): (0,) * nd)
    smem = pl.BlockSpec(memory_space=pltpu.SMEM)
    kv_spec = pl.BlockSpec((blocks, heads * 128, queries), lambda g: (g, 0, 0))
    return pl.pallas_call(
        kernel,
        grid=(groups,),
        out_shape=[shape(count, heads * 128, queries)] + outs,
        in_specs=[smem, kv_spec] + [whole(a) for a in small],
        out_specs=[kv_spec] + [whole(a) for a in outs],
        scratch_shapes=scratch,
        compiler_params=pltpu.CompilerParams(vmem_limit_bytes=52 << 20),
        name="attention_back",
    )(ids, kv, *small)


def normed(value):
    mean = jnp.mean(value, axis=1, keepdims=True)
    centered = value - mean
    var = jnp.mean(centered * centered, axis=1, keepdims=True)
    inverse = lax.rsqrt(var + EPS)
    return centered * inverse, inverse


def norm_back(upstream, n, inverse, gain):
    scaled = gain * upstream
    mean = jnp.mean(scaled, axis=1, keepdims=True)
    slope = jnp.mean(scaled * n, axis=1, keepdims=True)
    return (scaled - mean - n * slope) * inverse


def colsum(value):
    return jnp.sum(value, axis=0, keepdims=True)


def weights_out_kernel(rows, ids, *refs):
    out = refs[-1]
    members, quarter, _ = refs[0].shape
    for i, ref in enumerate(refs[:-1]):
        other, j = divmod(i, members)
        place = lax.bitwise_xor(ids[MEMBER], j)
        f = 2 * lax.div(place, 2) + lax.bitwise_xor(ids[CORE], other)
        for k in range(members):
            w = 2 * k + lax.rem(place, 2)
            out[pl.ds(pl.multiple_of(rows * w + quarter * f, 8), quarter), :] = ref[k]


def norm_one_kernel(ids, a0, a1, a2, a3, x_ref, w_ref, vec_ref, *refs):
    first_out, n_out, inverse_out, att_out = refs
    lanes = a0.shape[1]

    def head(t):
        for k, ref in enumerate((a0, a1, a2, a3)):
            at = lanes * (t ^ k)
            att_out[:, at : at + lanes] = ref[...]

    by_case(ids[HEAD], 4, head)
    projected = dot3(att_out[...], w_ref[...], 1, 0)
    n, inverse = normed(x_ref[: a0.shape[0]] + (projected + vec_ref[1:2]))
    first_out[...] = n * vec_ref[2:3] + vec_ref[3:4]
    n_out[...] = n
    inverse_out[...] = jnp.broadcast_to(inverse, inverse_out.shape)


def norm_two_kernel(p0, p1, p2, p3, first_ref, cot_ref, vec_ref, rows_out, dz_out, grads_out):
    value = first_ref[...] + ((p0[...] + p1[...]) + (p2[...] + p3[...]) + vec_ref[4:5])
    n, inverse = normed(value)
    rows_out[...] = n * vec_ref[5:6] + vec_ref[6:7]
    up = cot_ref[...]
    dz = norm_back(up, n, inverse, vec_ref[5:6])
    dz_out[...] = dz
    grads_out[...] = jnp.zeros_like(grads_out)
    grads_out[0:1] = colsum(up * n)
    grads_out[1:2] = colsum(up)
    grads_out[2:3] = colsum(dz)


def norm_one_back_kernel(ids, p0, p1, p2, p3, dz_ref, n_ref, inverse_ref, w_ref, vec_ref, *refs):
    dz_out, grads_out = refs[:2]
    parts = refs[2:6]
    up = dz_ref[...] + ((p0[...] + p1[...]) + (p2[...] + p3[...]))
    n = n_ref[...]
    dz = norm_back(up, n, inverse_ref[:, 0:1], vec_ref[2:3])
    dz_out[...] = dz
    grads_out[...] = jnp.zeros_like(grads_out)
    grads_out[0:1] = colsum(up * n)
    grads_out[1:2] = colsum(up)
    grads_out[2:3] = colsum(dz)
    d_att = dot3(dz, w_ref[...], 1, 1)
    lanes = parts[0].shape[1]

    def case(i):
        for k in range(4):
            at = lanes * (i ^ k)
            parts[k][...] = d_att[:, at : at + lanes]

    by_case(ids[HEAD], 4, case)


def stack_rest_kernel(first, source, out):
    out[...] = source[:, first : first + out.shape[1]]


def copy_kernel(source, out):
    out[...] = source[...]


def stack_kernel(*refs):
    for i, ref in enumerate(refs[:-1]):
        refs[-1][i] = ref[...]


def stack_rows(target, refs):
    rows = refs[0].shape[0]
    for k, ref in enumerate(refs):
        target[rows * k : rows * (k + 1), :] = ref[...]


def prepare_kernel(rows_up, slab, up_high, up_low, down_high, down_low):
    for first, count, high, low in (
        (0, rows_up, up_high, up_low),
        (rows_up, slab.shape[1] - rows_up, down_high, down_low),
    ):
        pieces = [slab[w, first : first + count] for w in range(slab.shape[0])]
        high[...], low[...] = split(jnp.concatenate(pieces, axis=0))


def forward_kernel(f0, f1, f2, f3, up_high, up_low, down_high, down_low, vec_ref, *refs):
    pre_out, first_out = refs[:2]
    parts = refs[2:6]
    stack_rows(first_out, (f0, f1, f2, f3))
    pre = dot3s(split(first_out[...]), (up_high[...], up_low[...]), 1, 0) + vec_ref[0:1]
    pre_out[...] = pre
    hidden = 0.5 * pre * (1.0 + lax.erf(pre * (0.5**0.5)))
    branch = dot3s(split(hidden), (down_high[...], down_low[...]), 1, 0)
    rows = f0.shape[0]
    for k in range(4):
        parts[k][...] = branch[rows * k : rows * (k + 1)]


def backward_kernel(z0, z1, z2, z3, pre_ref, up_high, up_low, down_high, down_low, *refs):
    dz_out, d_pre_out = refs[:2]
    parts = refs[2:6]
    stack_rows(dz_out, (z0, z1, z2, z3))
    d_hidden = dot3s(split(dz_out[...]), (down_high[...], down_low[...]), 1, 1)
    pre = pre_ref[...]
    density = jnp.exp(-0.5 * pre * pre) * ((2.0 * jnp.pi) ** -0.5)
    d_pre = d_hidden * (0.5 * (1.0 + lax.erf(pre * (0.5**0.5))) + pre * density)
    d_pre_out[...] = d_pre
    d_first = dot3s(split(d_pre), (up_high[...], up_low[...]), 1, 1)
    rows = z0.shape[0]
    for k in range(4):
        parts[k][...] = d_first[rows * k : rows * (k + 1)]


def ff_weights_kernel(rows_up, rows_down, first_ref, d_pre_ref, pre_ref, dz_ref, out, b_out):
    pre = pre_ref[...]
    hidden = 0.5 * pre * (1.0 + lax.erf(pre * (0.5**0.5)))
    d_pre = d_pre_ref[...]
    b_out[...] = jnp.broadcast_to(colsum(d_pre), b_out.shape)
    up = dot3(first_ref[...], d_pre, 0, 0)
    down = dot3(hidden, dz_ref[...], 0, 0)
    for w in range(out.shape[0]):
        out[w, :rows_up, :] = up[rows_up * w : rows_up * (w + 1)]
        out[w, rows_up:, :] = down[rows_down * w : rows_down * (w + 1)]


def share(ids, outs, places, members, write):
    if len(outs) == 1:
        for place in range(places):
            for z in range(members):
                write(outs[0].at[place, z], place, z)
        return

    def case(core):
        for place in range(places):
            x, f = divmod(place, members)
            j = lax.bitwise_xor(ids[MEMBER], 2 * (f // 2) + x)
            for z in range(members):
                target = outs[core ^ (f % 2)].at[j, lax.bitwise_xor(ids[HEAD], z)]
                write(target, place, z)

    by_case(ids[CORE], 2, case)


def shard_of(place, z, members):
    zh, rest = divmod(place, 2 * members)
    return 2 * (members * zh + z) + rest // members, rest % members


def out_weights_kernel(places, members, ids, att_ref, dz_ref, *outs):
    quarter = outs[0].shape[2]
    a_high, a_low = split(att_ref[...])
    d_high, d_low = split(dz_ref[...])
    value = dot(
        jnp.concatenate([a_high, a_low, a_high], axis=0),
        jnp.concatenate([d_high, d_high, d_low], axis=0),
        0,
        0,
    )

    def write(target, place, z):
        w, f = shard_of(place, z, members)
        at = (w * members + f) * quarter
        target[...] = value[at : at + quarter]

    share(ids, outs, places, members, write)


def sum_cores_kernel(own, came, *outs):
    for j, out in enumerate(outs):
        out[...] = own[j] + came[j]


def qkv_back_kernel(
    rows, span, places, ids, d0, d1, d2, d3, pq_ref, dpq_ref, kv_ref, key_ref, proj_ref, w_ref, *refs
):
    x_ref, dbias_ref, grads_ref, late_ref, up_ref, rows_out = refs[:6]
    outs, turned, up_rows = refs[6:-2], refs[-2], refs[-1]
    heads = pq_ref.shape[0] // 64
    width = heads * 64
    scale = HEAD_DIM**-0.25
    proj = split(proj_ref[...])
    dkv = (d0[...] + d1[...]) + (d2[...] + d3[...])
    for h in range(heads):
        lo, hi = 64 * h, 64 * h + 64
        turned[lo:hi] = scale * dot3s(proj, split(dpq_ref[lo:hi] * pq_ref[lo:hi]), 0, 0)
        pk = dkv[128 * h : 128 * h + 64] * kv_ref[128 * h : 128 * h + 64]
        turned[width + lo : width + hi] = scale * (
            dot3s(proj, split(pk), 0, 0) - key_ref[lo:hi] * colsum(pk)
        )
        turned[2 * width + lo : 2 * width + hi] = dkv[128 * h + 64 : 128 * h + 128]
    d_qkv = turned[...].T
    d_split = split(d_qkv)
    rows_out[...] = dot3s(d_split, split(w_ref[...]), 1, 1)

    members = outs[0].shape[1]
    quarter = rows // members
    d_b = colsum(d_qkv)
    weights = dot3s(split(x_ref[...]), d_split, 0, 0)

    up_rows[...] = jnp.zeros_like(up_rows)
    down = up_ref.shape[1] // up_rows.shape[0]

    def unit(g):
        for w in range(up_rows.shape[0]):
            up_rows[w : w + 1, down * g : down * (g + 1)] = up_ref[0:1, down * w : down * (w + 1)]

    by_case(ids[MEMBER], members, unit)

    def write(target, place, z):
        w, f = shard_of(place, z, members)
        at = (w * members + f) * quarter
        target[:quarter] = weights[at : at + quarter]
        target[quarter:] = jnp.zeros((8, d_b.shape[1]), f32)
        target[quarter : quarter + 1] = d_b
        for i in range(3):
            target[quarter + 1 : quarter + 2, rows * i : rows * (i + 1)] = grads_ref[
                i : i + 1, rows * w : rows * (w + 1)
            ]
            target[quarter + 6 : quarter + 7, rows * i : rows * (i + 1)] = late_ref[
                i : i + 1, rows * w : rows * (w + 1)
            ]
        target[quarter + 2 : quarter + 5, :span] = dbias_ref[0:3, span * w : span * (w + 1)]
        target[quarter + 5 : quarter + 6, : members * down] = up_rows[w : w + 1, : members * down]

    share(ids, outs, places, members, write)


def merge_kernel(rows, skip, ids, r0, r1, r2, r3, w0, w1, w2, w3, out, b_own, bias_out, *rest):
    refs, b_out = (r0, r1, r2, r3), rest[7]
    members = len(refs)
    lanes = r0.shape[1] // 3
    width = lanes * members
    span = bias_out.shape[1]
    quarter = rows // members
    total = (r0[quarter:] + r1[quarter:]) + (r2[quarter:] + r3[quarter:])
    for i in range(3):
        rest[i][...] = total[1:2, rows * i : rows * (i + 1)].reshape(rows)
        rest[3 + i][...] = total[6:7, rows * i : rows * (i + 1)].reshape(rows)
    rest[6][...] = total[5:6, : rest[6].shape[0]].reshape(rest[6].shape)
    last = slice(skip, skip + quarter)
    out[:, 3 * width :] = (w0[last] + w1[last]) + (w2[last] + w3[last])

    def head(t):
        for k, ref in enumerate(refs):
            f = t ^ k
            for p in range(3):
                at = width * p + lanes * f
                out[:, at : at + lanes] = ref[:quarter, lanes * p : lanes * (p + 1)]
                b_out[:, at : at + lanes] = ref[
                    quarter : quarter + 1, lanes * p : lanes * (p + 1)
                ]
            bias_out[3 * f : 3 * f + 3] = ref[quarter + 2 : quarter + 5, :span]

    by_case(ids[HEAD], members, head)
    count = b_own.shape[0]

    def place(w):
        b_own[...] = b_out[:, count * w : count * (w + 1)].reshape(count)

    by_case(ids[WIDE], b_out.shape[1] // count, place)


def place_weights_kernel(ids, r0, r1, r2, r3, w_out, wo_out):
    quarter = r0.shape[0]
    full = w_out.shape[1]

    def own(f):
        for k, ref in enumerate((r0, r1, r2, r3)):
            at = quarter * (f ^ k)
            w_out[at : at + quarter] = ref[:, :full]
            wo_out[at : at + quarter] = ref[:, full:]

    by_case(ids[OWN], 4, own)


def sum_split_kernel(a, b, c, d, *outs):
    for k, out in enumerate(outs):
        out[...] = (a[k] + b[k]) + (c[k] + d[k])


def sum_mixed_kernel(ids, a, b, c, d, rows_ref, *outs):
    rows = rows_ref.shape[0] // len(outs)
    quarter = a.shape[1]
    for k, out in enumerate(outs):
        at = pl.multiple_of(lax.bitwise_xor(ids[HEAD], k) * rows, 8)
        out[:rows] = rows_ref[pl.ds(at, rows), :]
        out[rows : rows + quarter] = (a[k] + b[k]) + (c[k] + d[k])


def sum_kernel(*refs):
    total = refs[0][...]
    for ref in refs[1:-1]:
        total = total + ref[...]
    refs[-1][...] = total


def sum_four_kernel(p0, p1, p2, p3, dz_ref, out):
    rows = out.shape[0]
    out[...] = dz_ref[...] + ((p0[:rows] + p1[:rows]) + (p2[:rows] + p3[:rows]))


def place_kernel(ids, r0, r1, r2, r3, out):
    rows = r0.shape[0]
    for k, ref in enumerate((r0, r1, r2, r3)):
        out[pl.ds(pl.multiple_of(lax.bitwise_xor(ids[OWN], k) * rows, 8), rows), :] = ref[...]


def place_ff_kernel(rows, down, ids, r0, r1, r2, r3, up_out, down_out):
    refs = (r0, r1, r2, r3)
    members = len(refs)

    def own(i):
        for k, ref in enumerate(refs):
            f = i ^ k
            for w in range(up_out.shape[1] // (members * down)):
                at = (w * members + f) * down
                up_out[:, at : at + down] = ref[:rows, down * w : down * (w + 1)]
            down_out[down * f : down * (f + 1)] = ref[rows:]

    by_case(ids[OWN], members, own)


def exchange(value, axes, count, k):
    return lax.ppermute(value, axes, [(i, i ^ k) for i in range(count)])


def swap(value):
    return lax.ppermute(value, ("core", "x"), [(0, 0), (1, 2), (2, 1), (3, 3)])


def place(ids, values, name):
    return call(
        place_kernel,
        [shape(len(values) * values[0].shape[0], values[0].shape[1])],
        [ids, *values],
        name,
        smem=1,
    )[0]


def gather(value, axes, count):
    return [value] + [exchange(value, axes, count, k) for k in range(1, count)]


def relay(value):
    came = exchange(value, "y", 2, 1)
    return [value, exchange(value, "core", 2, 1), came, exchange(came, "core", 2, 1)]


def scatter(parts, axes):
    return [parts[0]] + [exchange(parts[k], axes, len(parts), k) for k in range(1, len(parts))]


def body(
    ys,
    zhs,
    inputs,
    cotangent,
    random_proj,
    position_bias,
    w_qkv,
    b_qkv,
    w_out,
    b_out,
    ln1_gain,
    ln1_bias,
    w_up,
    b_up,
    w_down,
    b_down,
    ln2_gain,
    ln2_bias,
):
    members = 2 * ys
    blocks = 2 * zhs * members
    places = 2 * zhs * members
    few = zhs == 1
    core = lax.axis_index("core")
    x_at, y_at = lax.axis_index("x"), lax.axis_index("y")
    zh_at, zl_at = lax.axis_index("zh"), lax.axis_index("zl")
    feat = 2 * y_at + core
    group = 2 * y_at + x_at
    wide = 2 * (members * zh_at + zl_at) + x_at
    place_at = (2 * zh_at + x_at) * members + feat
    ids = jnp.stack([core, group, feat, zl_at, wide, place_at]).astype(jnp.int32)
    queries, width = inputs.shape
    rows = queries // members
    shard = w_qkv.shape[0]
    quarter = shard // members
    down = w_down.shape[0] // members
    heads = HEADS // members
    lanes = heads * HEAD_DIM
    span = position_bias.shape[1]
    full = 3 * lanes
    length = queries * blocks
    row_shape = shape(rows, width)

    packed = [w_qkv, w_out, position_bias, b_qkv, random_proj.T]
    packed += [b_up, b_out, ln1_gain, ln1_bias, b_down, ln2_gain, ln2_bias]
    got = call(
        functools.partial(pack_qkv_kernel, shard, members),
        [shape(quarter + 8, full)] * members + [shape(rows + -(-quarter // 8) * 8, width), row_shape],
        [ids, inputs, cotangent] + packed,
        "pack_qkv",
        scratch=[
            pltpu.VMEM((quarter, a.shape[1]) if i < 2 and quarter % 8 == 0 else a.shape, f32)
            for i, a in enumerate(packed)
        ]
        + [pltpu.SemaphoreType.DMA((len(packed) + 2,))],
        smem=1,
        limit=60 << 20,
        far=True,
    )
    mixed, cot_rows = got[members:]
    pieces = scatter(got[:members], "zl")
    pack_ids, _ = lax.optimization_barrier((ids, mixed))
    (ff_slab,) = call(
        functools.partial(pack_ff_kernel, members, down),
        [shape(shard + down, width)],
        [pack_ids, w_up, w_down],
        "pack_ff",
        smem=1,
    )
    ff_slab = swap(ff_slab)
    mixed_all = lax.all_gather(mixed, "zl", axis=0)
    pieces, ff_slab = lax.optimization_barrier((pieces, ff_slab))
    (slab,) = call(
        stack_kernel, [shape(members, quarter + 8, full)], pieces, "stack_pieces"
    )
    if few:
        slabs = gather(slab, GROUP, members)
    else:
        slabs = [lax.all_gather(slab, PLANE, axis=0)]
    slabs, mixed_all = lax.optimization_barrier((slabs, mixed_all))
    if few:
        slabs = slabs + [exchange(v, "core", 2, 1) for v in slabs]
    slabs, ff_slab = lax.optimization_barrier((slabs, ff_slab))
    ff_slab = lax.all_gather(ff_slab, LINES, axis=0)
    spare = 1 if quarter % 8 == 0 else blocks * members
    got = call(
        functools.partial(qkv_kernel, shard, members, (b_qkv.shape[0], span, down), few),
        [
            shape(width, full),
            shape(queries, width),
            shape(lanes, queries),
            shape(2 * lanes, queries),
            shape(lanes, queries),
            shape(FEATURES, HEAD_DIM),
            shape(8, 2 * length),
            shape(8, width),
        ],
        [ids, mixed_all, *slabs],
        "qkv",
        scratch=[
            pltpu.VMEM((blocks, 8, full), f32),
            pltpu.VMEM((spare, quarter, full), f32),
            pltpu.VMEM((FEATURES, 1, HEAD_DIM), f32),
        ],
        smem=1,
        deep=True,
        late=range(2, 2 + len(slabs)) if few else (),
    )
    w_cols, x, pq, kv, keys, proj, bias, vec = got

    if few:
        kv_own = gather(kv, GROUP, members)
        kv_all = kv_own + [exchange(v, "core", 2, 1) for v in kv_own]
        (wo_parts,) = call(
            functools.partial(stack_rest_kernel, rows),
            [shape(members, quarter, width)],
            [mixed_all],
            "stack_out",
        )
        wo_parts, _ = lax.optimization_barrier((wo_parts, kv_all))
        wo_x, wo_y = exchange(wo_parts, "x", 2, 1), exchange(wo_parts, "y", 2, 1)
    else:
        kv_all = lax.all_gather(kv, PLANE, axis=0)
    got = attention(ids, kv_all, pq, bias)
    att, den = got[:2]
    att_parts = scatter(got[2:], "zl")
    if few:
        wo_y, _ = lax.optimization_barrier((wo_y, got))
        wo_own = [wo_parts, wo_x, wo_y, exchange(wo_y, "x", 2, 1)]
        wo_own, _ = lax.optimization_barrier((wo_own, att_parts[2]))
        wo_all = wo_own + [exchange(v, "core", 2, 1) for v in wo_own]
        (w_full,) = call(
            functools.partial(weights_out_kernel, shard),
            [shape(width, width)],
            [ids, *wo_all],
            "weights_out",
            smem=1,
        )
    else:
        w_full = lax.all_gather(w_out, ("zh", "zl", "x"), axis=0, tiled=True)

    first, norm_rows, inverse, att_rows = call(
        norm_one_kernel,
        [row_shape, row_shape, shape(rows, 128), row_shape],
        [ids, *att_parts, mixed, w_full, vec],
        "norm_one",
        smem=1,
    )
    first, ff_slab = lax.optimization_barrier((first, ff_slab))
    firsts = gather(first, GROUP, members)
    full_rows = shape(queries, blocks * down)
    ff_matrices = call(
        functools.partial(prepare_kernel, shard),
        [shape(width, blocks * down, dtype=bf16)] * 2
        + [shape(blocks * down, width, dtype=bf16)] * 2,
        [ff_slab],
        "prepare",
    )
    got = call(
        forward_kernel,
        [full_rows, shape(queries, width)] + [row_shape] * members,
        [*firsts, *ff_matrices, vec],
        "forward",
    )
    pre, first_all = got[:2]
    parts = scatter(got[2:], GROUP)
    out_rows, dz2, grads_two = call(
        norm_two_kernel,
        [row_shape, row_shape, shape(8, width)],
        [*parts, first, cot_rows, vec],
        "norm_two",
    )
    dzs = gather(dz2, GROUP, members)
    got = call(
        backward_kernel,
        [shape(queries, width), full_rows] + [row_shape] * members,
        [*dzs, pre, *ff_matrices],
        "backward",
    )
    dz2_all, d_pre = got[:2]
    parts = scatter(got[2:], GROUP)

    head_rows = shape(rows, lanes)
    got = call(
        norm_one_back_kernel,
        [row_shape, shape(8, width)] + [head_rows] * members,
        [ids, *parts, dz2, norm_rows, inverse, w_full, vec],
        "norm_one_back",
        smem=1,
    )
    dz1, grads_one = got[:2]
    grads = scatter(got[2:], "zl")
    first_all, d_pre, pre, dz2_all, _ = lax.optimization_barrier(
        (first_all, d_pre, pre, dz2_all, dz1)
    )
    ff_grads, up_row = call(
        functools.partial(ff_weights_kernel, shard, down),
        [shape(blocks, shard + down, width), shape(8, blocks * down)],
        [first_all, d_pre, pre, dz2_all],
        "ff_weights",
    )


    part = shape(members, members, quarter, width)
    out_shares = call(
        functools.partial(out_weights_kernel, places, members),
        [part, part] if few else [shape(places, members, quarter, width)],
        [ids, att_rows, dz1],
        "out_weights",
        smem=1,
    )
    def sum_cores(own, other, name):
        came = exchange(other, "core", 2, 1)
        if name == "sum_keys":
            (own,) = call(copy_kernel, [shape(*own.shape)], [own], "load_keys")
        return call(sum_cores_kernel, [shape(*own.shape[1:])] * members, [own, came], name)

    if few:
        out_shares = sum_cores(*out_shares, "sum_out")
        grads, out_shares, ff_grads = lax.optimization_barrier((grads, out_shares, ff_grads))
        out_shares = scatter(out_shares, GROUP)
    else:
        grads, ff_grads = lax.optimization_barrier((grads, ff_grads))
    ff_grads = lax.psum_scatter(ff_grads, LINES, scatter_dimension=0, tiled=False)
    out_came, out_core = exchange(out_rows, "y", 2, 1), exchange(out_rows, "core", 2, 1)
    back = attention_back(ids, kv_all, pq, bias, att, den, grads)
    back, out_came, out_core = lax.optimization_barrier((back, out_came, out_core))
    if few:
        back, out_shares = lax.optimization_barrier((back, out_shares))
        arrived = scatter(sum_cores(back[0], back[1], "sum_keys"), GROUP)
    else:
        arrived = lax.psum_scatter(back[0], PLANE, scatter_dimension=0, tiled=False)
        arrived = [arrived] + [jnp.zeros_like(arrived)] * 3
    dpq, dbias = back[-2:]
    out_parts = [out_rows, out_core, out_came, exchange(out_came, "core", 2, 1)]
    output = place(ids, out_parts, "place_output")
    arrived, output = lax.optimization_barrier((arrived, output))

    part = shape(members, members, quarter + 8, full)
    got = call(
        functools.partial(qkv_back_kernel, shard, span, places),
        [shape(queries, width)]
        + ([part, part] if few else [shape(places, members, quarter + 8, full)]),
        [ids, *arrived, pq, dpq, kv, keys, proj, w_cols, x, dbias, grads_one, grads_two, up_row],
        "qkv_back",
        scratch=[
            pltpu.VMEM((full, queries), f32),
            pltpu.VMEM((blocks, -(-members * down // 128) * 128), f32),
        ],
        smem=1,
    )
    shares_out = got[1:]
    piece = shape(rows + -(-quarter // 8) * 8, width)
    if few:
        mixed_grads = call(
            sum_mixed_kernel, [piece] * members, [ids, *out_shares, got[0]], "sum_mixed", smem=1
        )
    else:
        part = lax.psum_scatter(out_shares[0], PLANE, scatter_dimension=0, tiled=False)
        part = jnp.concatenate(
            [got[0].reshape(members, rows, width), part], axis=1
        )
        part = jnp.pad(part, ((0, 0), (0, piece.shape[0] - part.shape[1]), (0, 0)))
        mixed_grads = [
            lax.dynamic_index_in_dim(part, zl_at ^ k, 0, keepdims=False) for k in range(members)
        ]

    def split_plane(parts, piece, name):
        if few:
            return call(sum_split_kernel, [piece] * members, parts, name)
        part = lax.psum_scatter(parts[0], PLANE, scatter_dimension=0, tiled=False)
        return [
            lax.dynamic_index_in_dim(part, zl_at ^ k, 0, keepdims=False) for k in range(members)
        ]

    if few:
        shares_out = sum_cores(*shares_out, "sum_qkv")
    shares_out, mixed_grads, ff_grads = lax.optimization_barrier(
        (shares_out, mixed_grads, ff_grads)
    )
    ff_grads = swap(ff_grads)
    mine = scatter(shares_out, GROUP) if few else shares_out
    mixed_grads = scatter(mixed_grads, "zl")
    ff_came = exchange(ff_grads, "y", 2, 1)
    mine, mixed_grads, ff_came = lax.optimization_barrier((mine, mixed_grads, ff_came))
    mine = split_plane(mine, shape(quarter + 8, full), "sum_qkv_plane")
    (d_input_rows,) = call(sum_four_kernel, [row_shape], [*mixed_grads, dz1], "sum_rows")
    input_came = exchange(d_input_rows, "y", 2, 1)
    mine = scatter(mine, "zl")
    got = call(
        functools.partial(merge_kernel, shard, rows),
        [
            shape(quarter, 4 * width),
            shape(*b_qkv.shape),
            shape(*position_bias.shape),
        ]
        + [shape(shard)] * 6
        + [shape(*b_up.shape)],
        [ids, *mine, *mixed_grads],
        "merge",
        scratch=[pltpu.VMEM((1, 3 * width), f32)],
        smem=1,
    )
    merged, d_b_qkv, d_position_bias, d_ln1_gain, d_ln1_bias, d_b_out = got[:6]
    d_ln2_gain, d_ln2_bias, d_b_down, d_b_up = got[6:]
    merged_came = exchange(merged, "y", 2, 1)

    def relayed(value, came):
        return [value, exchange(value, "core", 2, 1), came, exchange(came, "core", 2, 1)]

    ff_came, input_came, _ = lax.optimization_barrier((ff_came, input_came, merged))
    d_inputs = place(ids, relayed(d_input_rows, input_came), "place_inputs")
    ff_parts = relayed(ff_grads, ff_came)
    d_w_up, d_w_down = call(
        functools.partial(place_ff_kernel, shard, down),
        [shape(shard, w_up.shape[1]), shape(*w_down.shape)],
        [ids, *ff_parts],
        "place_ff",
        smem=1,
    )
    merged_came, d_inputs, d_w_up, d_w_down = lax.optimization_barrier(
        (merged_came, d_inputs, d_w_up, d_w_down)
    )
    d_w_qkv, d_w_out = call(
        place_weights_kernel,
        [shape(*w_qkv.shape), shape(shard, width)],
        [ids, *relayed(merged, merged_came)],
        "place_weights",
        smem=1,
    )

    return (
        output,
        d_inputs,
        d_position_bias,
        d_w_qkv,
        d_b_qkv,
        d_w_out,
        d_b_out,
        d_ln1_gain,
        d_ln1_bias,
        d_w_up,
        d_b_up,
        d_w_down,
        d_b_down,
        d_ln2_gain,
        d_ln2_bias,
    )


def solution(mesh):
    feats, wides = mesh.shape["feat"], mesh.shape["wide"]
    ys, zhs = feats // 2, wides // (2 * feats)
    fine = Mesh(mesh.devices.reshape(ys, 2, zhs, feats, 2), ("y", "core", "zh", "zl", "x"))
    wide = ("zh", "zl", "x")
    mat, vector, lane = P(wide, None), P(wide), P(None, wide)
    return jax.shard_map(
        functools.partial(body, ys, zhs),
        mesh=fine,
        in_specs=(mat, mat, P(None, FEAT), lane, mat, vector, mat, vector)
        + (vector, vector, mat, vector, mat, vector, vector, vector),
        out_specs=(mat, mat, lane, mat, vector, mat, vector, vector)
        + (vector, mat, vector, mat, vector, vector, vector),
        check_vma=False,
    )
```

```python
import functools
import math

import jax
import jax.numpy as jnp
from jax import lax
from jax.experimental import pallas as pl
from jax.experimental.pallas import tpu as pltpu
from jax.sharding import Mesh
from jax.sharding import PartitionSpec as P

HEADS = 12
HEAD_DIM = 64
FEATURES = 64
EPS = 1e-06
f32 = jnp.float32
bf16 = jnp.bfloat16

GROUP = ("y", "x")
FEAT = ("y", "core")
PLANE = ("zh", "x", "y", "core")
LINES = ("zh", "zl", "core")
CORE, MEMBER, OWN, HEAD, WIDE, PLACE = range(6)


def split(value):
    high = value.astype(bf16)
    return high, (value - high.astype(f32)).astype(bf16)


def dot(a, b, ca, cb):
    return lax.dot_general(a, b, (((ca,), (cb,)), ((), ())), preferred_element_type=f32)


def dot3s(a, b, ca, cb):
    return dot(a[0], b[0], ca, cb) + (dot(a[0], b[1], ca, cb) + dot(a[1], b[0], ca, cb))


def dot3(a, b, ca, cb):
    return dot3s(split(a), split(b), ca, cb)


def cost():
    return pl.CostEstimate(flops=1 << 20, bytes_accessed=1 << 10, transcendentals=0)


def tiled(dims):
    if len(dims) < 2:
        return 0
    return math.prod(dims[:-2]) * -(-dims[-2] // 8) * -(-dims[-1] // 128) * 4096


def call(kernel, outs, args, name, scratch=(), smem=0, room=8, limit=0, fetch=(), push=(), far=False, deep=False, late=None, stream=()):
    held = sum(tiled(ref.shape) for ref in scratch)
    held += sum(size for size in map(lambda a: tiled(a.shape), [*args, *outs]) if size > 4 << 20)
    if deep and not far:
        fetch = [i for i in range(smem, len(args)) if i not in stream]
        push, limit = range(len(outs)), 60 << 20
    fetch, push = tuple(fetch), tuple(push)
    near = [pltpu.VMEM(args[i].shape, args[i].dtype) for i in fetch]
    near += [pltpu.VMEM(outs[i].shape, outs[i].dtype) for i in push]
    held += sum(args[i].size * args[i].dtype.itemsize for i in fetch)
    held += sum(outs[i].size * outs[i].dtype.itemsize for i in push)
    count = len(args) + len(outs)
    flow = []
    if stream:
        first = args[stream[0]]
        flow = [
            pltpu.VMEM((len(stream),) + first.shape, first.dtype),
            pltpu.SemaphoreType.DMA((len(stream),)),
        ]

    def moved(*refs):
        whole, own = list(refs[:count]), refs[count : count + len(scratch)]
        spare, sems = refs[count + len(scratch) : -1 - len(flow)], refs[-1 - len(flow)]
        copies, after = [], []
        for at, (i, ref) in enumerate(zip(fetch, spare)):
            copies.append(pltpu.make_async_copy(whole[i], ref, sems.at[at]))
            whole[i] = ref
        for at, (i, ref) in enumerate(zip(push, spare[len(fetch) :])):
            i += len(args)
            after.append(pltpu.make_async_copy(ref, whole[i], sems.at[len(fetch) + at]))
            whole[i] = ref
        for copy in copies:
            copy.start()
        if flow:
            held, flow_sems = refs[-2:]
            for i, at in enumerate(stream):
                pltpu.make_async_copy(whole[at], held.at[i], flow_sems.at[i]).start()
        for i, copy in zip(fetch, copies):
            if late is None or i not in late:
                copy.wait()
        started = []

        def arrive(i):
            copies[fetch.index(i)].wait()

        def start(i):
            started.append(push.index(i))
            after[started[-1]].start()

        def wait(i):
            pltpu.make_async_copy(held.at[i], held.at[i], flow_sems.at[i]).wait()

        if flow:
            whole = [ref for i, ref in enumerate(whole) if i not in stream]
            kernel(*whole, *own, held=held, wait=wait, start=start)
        elif late is not None:
            kernel(*whole, *own, arrive=arrive, start=start)
        else:
            kernel(*whole, *own)
        for i, copy in enumerate(after):
            if i not in started:
                copy.start()
        for copy in after:
            copy.wait()

    def spec(i, which):
        return pl.BlockSpec(memory_space=pltpu.HBM if i in which else pltpu.VMEM)

    return pl.pallas_call(
        moved if near else kernel,
        out_shape=outs,
        in_specs=[pl.BlockSpec(memory_space=pltpu.SMEM)] * smem
        + [
            spec(i, range(len(args)) if far else (*fetch, *stream))
            for i in range(smem, len(args))
        ],
        out_specs=[spec(i, push) for i in range(len(outs))],
        scratch_shapes=list(scratch)
        + near
        + ([pltpu.SemaphoreType.DMA((len(near),))] if near else [])
        + flow,
        compiler_params=pltpu.CompilerParams(vmem_limit_bytes=limit or held + (room << 20)),
        cost_estimate=cost(),
        name=name,
    )(*args)


def when(condition):
    if isinstance(condition, bool):
        return lambda run: run() if condition else None
    return pl.when(condition)


def shape(*dims, dtype=f32):
    return jax.ShapeDtypeStruct(dims, dtype)


def by_case(value, count, run):
    for i in range(count):
        pl.when(value == i)(functools.partial(run, i))


def pack_qkv_kernel(rows, members, ids, *refs):
    count = (len(refs) - members - 3) // 2 + 1
    sources, pieces = refs[:count], refs[count : count + members]
    mixed, cot_out = refs[count + members : count + members + 2]
    held, sems = refs[count + members + 2 : -1], refs[-1]
    part = cot_out.shape[0]
    at = pl.multiple_of(ids[OWN] * part, 8)
    copies = [
        pltpu.make_async_copy(source.at[pl.ds(at, part)], target, sems.at[i])
        for i, (source, target) in enumerate(
            zip(sources[:2], (mixed.at[pl.ds(0, part)], cot_out))
        )
    ]
    quarter = rows // members
    for i, (source, target) in enumerate(zip(sources[2:], held)):
        if source.shape != target.shape:
            source = source.at[pl.ds(pl.multiple_of(ids[OWN] * quarter, 8), quarter)]
        copies.append(pltpu.make_async_copy(source, target, sems.at[2 + i]))
    for copy in copies:
        copy.start()
    for copy in copies:
        copy.wait()
    w_ref, out_ref, bias_ref, b_ref, proj_ref, up_ref = held[:6]
    width = w_ref.shape[1] // 3
    lanes = width // members
    heads = bias_ref.shape[0] // members
    for piece in pieces:
        piece[quarter:, :] = jnp.zeros((8, 3 * lanes), f32)
        piece[quarter : quarter + 1, : b_ref.shape[0]] = b_ref[...].reshape(1, -1)
        for i, ref in enumerate(held[6:]):
            row, lane = (4, i) if i < 5 else (5, 0)
            piece[quarter + row : quarter + row + 1, lane * rows : (lane + 1) * rows] = ref[
                ...
            ].reshape(1, -1)
        piece[quarter + 5 : quarter + 6, rows : rows + up_ref.shape[0]] = up_ref[...].reshape(1, -1)
        per = 3 * lanes // HEAD_DIM
        for i in range(proj_ref.shape[0]):
            row, lane = quarter + 6 + i // per, HEAD_DIM * (i % per)
            piece[row : row + 1, lane : lane + HEAD_DIM] = proj_ref[i : i + 1]

    def own(f):
        first = 0 if w_ref.shape[0] == quarter else quarter * f
        mixed[part : part + quarter] = out_ref[first : first + quarter]

        def head(t):
            for k, piece in enumerate(pieces):
                to = t ^ k
                for p in range(3):
                    at = width * p + lanes * to
                    piece[:quarter, lanes * p : lanes * (p + 1)] = w_ref[
                        first : first + quarter, at : at + lanes
                    ]
                piece[quarter + 1 : quarter + 1 + heads, : bias_ref.shape[1]] = bias_ref[
                    heads * to : heads * (to + 1)
                ]

        by_case(ids[HEAD], members, head)

    by_case(ids[OWN], members, own)


def pack_ff_kernel(members, down, ids, up_ref, down_ref, out):
    rows = up_ref.shape[0]
    blocks = up_ref.shape[1] // (members * down)

    def case(i):
        for w in range(blocks):
            at = (w * members + i) * down
            out[:rows, down * w : down * (w + 1)] = up_ref[:, at : at + down]
        out[rows : rows + down, :] = down_ref[down * i : down * (i + 1)]

    by_case(ids[OWN], members, case)


def plane_place(ids, members, few, i):
    if not few:
        zh, rest = divmod(i, 2 * members)
        return zh, rest // members, rest % members
    other, j = divmod(i, members)
    member = lax.bitwise_xor(ids[MEMBER], j)
    return 0, lax.rem(member, 2), 2 * lax.div(member, 2) + lax.bitwise_xor(ids[CORE], other)


def qkv_kernel(rows, members, spans, few, ids, *refs, arrive=None, start=None):
    mixed, refs = refs[0], refs[1:]
    w_out, x_out, pq_out, kv_out, key_out, proj_out, bias_out, vec_out, extra, held, directions = refs[-11:]
    slabs = refs[:-11]
    slabs = list(slabs) if few else [slabs[0].at[i] for i in range(slabs[0].shape[0])]
    width = x_out.shape[1]
    blocks = extra.shape[0]
    full = w_out.shape[1]
    lanes = full // 3
    heads = lanes // HEAD_DIM
    quarter = rows // members
    part = x_out.shape[0] // members
    for z in range(members):
        x_out[part * z : part * (z + 1), :] = mixed[z, :part]
    for i, slab in enumerate(slabs):
        if arrive is not None and few:
            arrive(2 + i)
        zh, x, f = plane_place(ids, members, few, i)
        for k in range(members):
            w = 2 * (members * zh + lax.bitwise_xor(ids[HEAD], k)) + x
            if i < 2 if few else f == 0:
                extra[w] = slab[k, quarter:]
            if quarter % 8 == 0:
                at = pl.multiple_of(w * rows + f * quarter, 8)
                w_out[pl.ds(at, quarter), :] = slab[k, :quarter]
            else:
                held[w * members + f] = slab[k, :quarter]
    if quarter % 8:
        for i in range(held.shape[0]):
            w_out[quarter * i : quarter * (i + 1)] = held[i]

    share = FEATURES // members
    per = full // HEAD_DIM
    for i, slab in enumerate(slabs):
        zh, x, f = plane_place(ids, members, few, i)
        if few or (zh, x) == (0, 0):
            for r in range(share):
                at, lane = quarter + 6 + r // per, HEAD_DIM * (r % per)
                directions[share * f + r] = slab[0, at : at + 1, lane : lane + HEAD_DIM]
    for r in range(FEATURES):
        proj_out[r : r + 1, :] = directions[r]
    bias_out[...] = jnp.zeros_like(bias_out)
    b_row = []
    for w in range(blocks):
        b_row.append(extra[w, 0:1, : spans[0]])
        count = spans[1]
        bias_out[:heads, count * w : count * (w + 1)] = extra[w, 1 : 1 + heads, :count]
        for i in range(6):
            row, lane = (4, i) if i < 5 else (5, 0)
            vec_out[1 + i : 2 + i, rows * w : rows * (w + 1)] = extra[
                w, row : row + 1, lane * rows : (lane + 1) * rows
            ]
    vec_out[7:8] = jnp.zeros((1, width), f32)
    b_row = jnp.concatenate(b_row, axis=1)

    def unit(g):
        count = spans[2]
        for w in range(blocks):
            vec_out[0:1, count * w : count * (w + 1)] = extra[
                w, 5:6, rows + count * g : rows + count * (g + 1)
            ]

    by_case(ids[MEMBER], members, unit)
    if start is not None:
        for i in (0, 1, 5, 6, 7):
            start(i)
    qkv = dot3(x_out[...], w_out[...], 1, 0)
    scale = HEAD_DIM**-0.25
    proj = split(proj_out[...])

    def head(t):
        bias = [b_row[:, width * p + lanes * t : width * p + lanes * (t + 1)] for p in range(3)]
        turned = (qkv + jnp.concatenate(bias, axis=1)).T
        for h in range(heads):
            lo, hi = HEAD_DIM * h, HEAD_DIM * (h + 1)
            q = turned[lo:hi] * scale
            k = turned[lanes + lo : lanes + hi] * scale
            pq_out[lo:hi] = jnp.exp(dot3s(proj, split(q), 1, 0))
            pk = dot3s(proj, split(k), 1, 0) - 0.5 * jnp.sum(k * k, axis=0, keepdims=True)
            kv_out[128 * h : 128 * h + 64] = jnp.exp(pk)
            kv_out[128 * h + 64 : 128 * h + 128] = turned[2 * lanes + lo : 2 * lanes + hi]
            key_out[lo:hi] = k

    by_case(ids[HEAD], members, head)


def rolled_rows(table, row):
    wide = jnp.broadcast_to(row, (8, row.shape[1]))
    return pltpu.roll(wide, 0, 1, stride=1, stride_axis=0)


def make_tables(tables, bias_ref, heads):
    length = bias_ref.shape[1]
    for h in range(heads):
        rows = rolled_rows(None, jnp.exp(bias_ref[h : h + 1]))
        tables[0, 8 * h : 8 * h + 8] = rows
        tables[1, 8 * h : 8 * h + 8] = pltpu.roll(rows, length - 64, 1)


def factor_tile(windows):
    first = lax.broadcasted_iota(jnp.int32, (8, 128), 1) < 64
    pairs = {}
    for g in range(8):
        for d in range(-3, 3):
            low = pltpu.roll(windows[d + 3], (8 * g + 64) % 128, 1)
            high = windows[d + 4] if g == 0 else pltpu.roll(windows[d + 4], 8 * g, 1)
            pairs[d, g] = jnp.where(first, low, high)
    rows = []
    for z in range(4):
        for g in range(8):
            rows.append(jnp.concatenate([pairs[-z, g], pairs[2 - z, g]], axis=1))
    return jnp.concatenate(rows, axis=0)


def window_sums(pairs):
    first = lax.broadcasted_iota(jnp.int32, (8, 128), 1) < 64
    sums = [jnp.zeros((8, 128), f32) for _ in range(7)]
    for g in range(8):
        for d in range(-3, 3):
            total = None
            for z in range(4):
                for p in range(2):
                    if 2 * p - z == d:
                        term = pairs[64 * z + 8 * g : 64 * z + 8 * g + 8, 128 * p : 128 * p + 128]
                        total = term if total is None else total + term
            low = pltpu.roll(jnp.where(first, total, 0.0), 64 - 8 * g, 1)
            high = jnp.where(first, 0.0, total)
            sums[d + 3] = sums[d + 3] + low
            sums[d + 4] = sums[d + 4] + (high if g == 0 else pltpu.roll(high, 128 - 8 * g, 1))
    return sums


def window_start(ids, members, groups, seg, length, n):
    if groups == 1:
        other, j = n // members, n % members
        member = lax.bitwise_xor(ids[MEMBER], j)
        zh, x = ids[PLACE] * 0, lax.rem(member, 2)
        f = 2 * lax.div(member, 2) + lax.bitwise_xor(ids[CORE], other)
    else:
        zh, x, f = n // (2 * members), lax.rem(lax.div(n, members), 2), lax.rem(n, members)
    own = ids[PLACE]
    away = 8 * members * (lax.div(own, 2 * members) - zh)
    away += members * (lax.rem(lax.div(own, members), 2) - x) + ids[OWN] - f
    start = away + length // (2 * seg) - 1
    odd = lax.rem(start, 2)
    return start - odd, odd


def window_at(start, d):
    return pl.multiple_of(start * 64 + 512 * d, 128)


def split_block(block, h, kcat, vcat):
    for part, cat in ((0, kcat), (64, vcat)):
        high, low = split(block[128 * h + part : 128 * h + part + 64])
        cat[h, 0:64] = high
        cat[h, 64:128] = low
        cat[h, 128:192] = high


def attention_kernel(groups, blocks, ids, *refs, held=None, wait=None, start=None):
    if groups > 1:
        held, refs = refs[0], refs[1:]
    pq_ref, bias_ref, att_out, den_out = refs[:4]
    parts = refs[4:8]
    tables, qcat, out_rows, kcat, vcat = refs[8:]
    heads = pq_ref.shape[0] // 64
    queries = pq_ref.shape[1]
    step = pl.program_id(0) if groups > 1 else 0

    @when(step == 0)
    def _():
        make_tables(tables, bias_ref, heads)
        for h in range(heads):
            high, low = split(pq_ref[64 * h : 64 * h + 64])
            qcat[h, 0:64] = high
            qcat[h, 64:128] = high
            qcat[h, 128:192] = low
        att_out[...] = jnp.zeros_like(att_out)
        den_out[...] = jnp.zeros_like(den_out)

    def advance(n, carry):
        first, odd = window_start(ids, 4, groups, 64, bias_ref.shape[1], step * blocks + n)
        if wait is not None:
            wait(n)
        for h in range(heads):
            split_block(held.at[n], h, kcat.at[n], vcat.at[n])
            scores = dot(kcat[n, h], qcat[h], 0, 0)
            rows = slice(8 * h, 8 * h + 8)
            windows = [
                tables[odd, rows, pl.ds(window_at(first, d), 128)] for d in range(-3, 4)
            ]
            weight = scores * factor_tile(windows)
            high, low = split(weight)
            both = dot(vcat[n, h, 0:128], high, 1, 0)
            more = dot(vcat[n, h, 0:64], low, 1, 0)
            att_out[64 * h : 64 * h + 64] += both[0:64] + both[64:128] + more
            den_out[h : h + 1] += jnp.sum(weight, axis=0, keepdims=True)
        return carry

    lax.fori_loop(0, blocks, advance, 0, unroll=2)

    @when(step == groups - 1)
    def _():
        for h in range(heads):
            att_out[64 * h : 64 * h + 64] = att_out[64 * h : 64 * h + 64] / den_out[h : h + 1]
        out_rows[...] = att_out[...].T
        rows = queries // 4
        for k in range(4):
            first = pl.multiple_of(lax.bitwise_xor(ids[HEAD], k) * rows, 8)
            parts[k][...] = out_rows[pl.ds(first, rows), :]


def attention(ids, kv, pq, window):
    stacked = not isinstance(kv, list)
    count = kv.shape[0] if stacked else len(kv)
    blocks = 8 if stacked else count
    groups = count // blocks
    queries = pq.shape[1]
    heads = pq.shape[0] // 64
    rows = shape(queries // 4, heads * 64)
    outs = [shape(heads * 64, queries), shape(8, queries)] + [rows] * 4
    scratch = [
        pltpu.VMEM((2, 8 * heads, window.shape[1]), f32),
        pltpu.VMEM((heads, 192, queries), bf16),
        pltpu.VMEM((queries, heads * 64), f32),
        pltpu.VMEM((blocks, heads, 192, queries), bf16),
        pltpu.VMEM((blocks, heads, 192, queries), bf16),
    ]
    kernel = functools.partial(attention_kernel, groups, blocks)
    if not stacked:
        args = [ids, *kv, pq, window]
        stream = range(1, 1 + count)
        return call(kernel, outs, args, "attention", scratch, 1, deep=True, stream=stream)
    whole = lambda a: pl.BlockSpec(a.shape, lambda g, nd=len(a.shape): (0,) * nd)
    smem = pl.BlockSpec(memory_space=pltpu.SMEM)
    kv_spec = pl.BlockSpec((blocks,) + kv.shape[1:], lambda g: (g, 0, 0))
    return pl.pallas_call(
        kernel,
        grid=(groups,),
        out_shape=outs,
        in_specs=[smem, kv_spec, whole(pq), whole(window)],
        out_specs=[whole(a) for a in outs],
        scratch_shapes=scratch,
        compiler_params=pltpu.CompilerParams(vmem_limit_bytes=52 << 20),
        name="attention",
    )(ids, kv, pq, window)


def attention_back_kernel(groups, blocks, ids, *refs, held=None, wait=None, start=None):
    if groups > 1:
        held, refs = refs[0], refs[1:]
    pq_ref, bias_ref, att_ref, den_ref = refs[:4]
    grads = refs[4:8]
    if groups == 1:
        own, other, dpq_out, dbias_out = refs[8:12]
    else:
        dkv, dpq_out, dbias_out = refs[8:11]
    tables, qcat, gcat, gden, diag, grad_rows, kcat, vcat = refs[-8:]
    heads = pq_ref.shape[0] // 64
    queries = pq_ref.shape[1]
    step = pl.program_id(0) if groups > 1 else 0

    @when(step == 0)
    def _():
        rows = queries // 4
        for k in range(4):
            first = pl.multiple_of(lax.bitwise_xor(ids[HEAD], k) * rows, 8)
            grad_rows[pl.ds(first, rows), :] = grads[k][...]
        make_tables(tables, bias_ref, heads)
        d_att = grad_rows[...].T
        gden[...] = jnp.zeros_like(gden)
        for h in range(heads):
            lo, hi = 64 * h, 64 * h + 64
            for value, cat in ((pq_ref[lo:hi], qcat), (d_att[lo:hi] / den_ref[h : h + 1], gcat)):
                high, low = split(value)
                cat[h, 0:64] = high
                cat[h, 64:128] = high
                cat[h, 128:192] = low
            gden[h : h + 1] = -(
                jnp.sum(d_att[lo:hi] * att_ref[lo:hi], axis=0, keepdims=True) / den_ref[h : h + 1]
            )
        dpq_out[...] = jnp.zeros_like(dpq_out)
        diag[...] = jnp.zeros_like(diag)

    def advance(dkv, first, n, carry):
        begin, odd = window_start(ids, 4, groups, 64, bias_ref.shape[1], step * blocks + n)
        if wait is not None:
            wait(n)
        for h in range(heads):
            split_block(held.at[n], h, kcat.at[n], vcat.at[n])
            scores = dot(kcat[n, h], qcat[h], 0, 0)
            rows = slice(8 * h, 8 * h + 8)
            factor = factor_tile(
                [tables[odd, rows, pl.ds(window_at(begin, d), 128)] for d in range(-3, 4)]
            )
            d_weight = dot(vcat[n, h], gcat[h], 0, 0) + gden[h : h + 1]
            w_high, w_low = split(scores * factor)
            e_high, e_low = split(d_weight * factor)
            pairs = d_weight * scores
            both = dot(gcat[h, 64:192], w_high, 1, 1)
            dv = both[0:64] + both[64:128] + dot(gcat[h, 0:64], w_low, 1, 1)
            both = dot(qcat[h, 64:192], e_high, 1, 1)
            dk = both[0:64] + both[64:128] + dot(qcat[h, 0:64], e_low, 1, 1)
            both = dot(kcat[n, h, 0:128], e_high, 1, 0)
            dq = both[0:64] + both[64:128] + dot(kcat[n, h, 0:64], e_low, 1, 0)
            dpq_out[64 * h : 64 * h + 64] += dq
            dkv[n - first, 128 * h : 128 * h + 64] = dk
            dkv[n - first, 128 * h + 64 : 128 * h + 128] = dv
            for i, total in enumerate(window_sums(pairs)):
                diag[odd, rows, pl.ds(window_at(begin, i - 3), 128)] += total
        return carry

    if groups == 1:
        half = blocks // 2
        lax.fori_loop(half, blocks, functools.partial(advance, other, half), 0, unroll=2)
        if start is not None:
            start(1)
        lax.fori_loop(0, half, functools.partial(advance, own, 0), 0, unroll=2)
        if start is not None:
            start(0)
    else:
        lax.fori_loop(0, blocks, functools.partial(advance, dkv, 0), 0)

    @when(step == groups - 1)
    def _():
        length = diag.shape[2]
        dbias_out[...] = jnp.zeros_like(dbias_out)
        for h in range(heads):
            both = diag[0, 8 * h : 8 * h + 8] + pltpu.roll(diag[1, 8 * h : 8 * h + 8], 64, 1)
            total = both[0:1]
            for s in range(1, 8):
                total = total + pltpu.roll(both[s : s + 1], length - s, 1)
            dbias_out[h : h + 1] = total * jnp.exp(bias_ref[h : h + 1])


def attention_back(ids, kv, pq, window, att, den, grads):
    stacked = not isinstance(kv, list)
    count = kv.shape[0] if stacked else len(kv)
    blocks = 8 if stacked else count
    groups = count // blocks
    queries = pq.shape[1]
    heads = pq.shape[0] // 64
    outs = [shape(heads * 64, queries), shape(8, window.shape[1])]
    scratch = [
        pltpu.VMEM((2, 8 * heads, window.shape[1]), f32),
        pltpu.VMEM((heads, 192, queries), bf16),
        pltpu.VMEM((heads, 192, queries), bf16),
        pltpu.VMEM((8, queries), f32),
        pltpu.VMEM((2, 8 * heads, window.shape[1]), f32),
        pltpu.VMEM((queries, heads * 64), f32),
        pltpu.VMEM((blocks, heads, 192, queries), bf16),
        pltpu.VMEM((blocks, heads, 192, queries), bf16),
    ]
    kernel = functools.partial(attention_back_kernel, groups, blocks)
    small = [pq, window, att, den] + list(grads)
    if not stacked:
        half = shape(count // 2, heads * 128, queries)
        return call(
            kernel,
            [half, half] + outs,
            [ids, *kv] + small,
            "attention_back",
            scratch,
            1,
            deep=True,
            stream=range(1, 1 + count),
        )
    whole = lambda a: pl.BlockSpec(a.shape, lambda g, nd=len(a.shape): (0,) * nd)
    smem = pl.BlockSpec(memory_space=pltpu.SMEM)
    kv_spec = pl.BlockSpec((blocks, heads * 128, queries), lambda g: (g, 0, 0))
    return pl.pallas_call(
        kernel,
        grid=(groups,),
        out_shape=[shape(count, heads * 128, queries)] + outs,
        in_specs=[smem, kv_spec] + [whole(a) for a in small],
        out_specs=[kv_spec] + [whole(a) for a in outs],
        scratch_shapes=scratch,
        compiler_params=pltpu.CompilerParams(vmem_limit_bytes=52 << 20),
        name="attention_back",
    )(ids, kv, *small)


def normed(value):
    mean = jnp.mean(value, axis=1, keepdims=True)
    centered = value - mean
    var = jnp.mean(centered * centered, axis=1, keepdims=True)
    inverse = lax.rsqrt(var + EPS)
    return centered * inverse, inverse


def norm_back(upstream, n, inverse, gain):
    scaled = gain * upstream
    mean = jnp.mean(scaled, axis=1, keepdims=True)
    slope = jnp.mean(scaled * n, axis=1, keepdims=True)
    return (scaled - mean - n * slope) * inverse


def colsum(value):
    return jnp.sum(value, axis=0, keepdims=True)


def weights_out_kernel(rows, ids, *refs):
    out = refs[-1]
    members, quarter, _ = refs[0].shape
    for i, ref in enumerate(refs[:-1]):
        other, j = divmod(i, members)
        place = lax.bitwise_xor(ids[MEMBER], j)
        f = 2 * lax.div(place, 2) + lax.bitwise_xor(ids[CORE], other)
        for k in range(members):
            w = 2 * k + lax.rem(place, 2)
            out[pl.ds(pl.multiple_of(rows * w + quarter * f, 8), quarter), :] = ref[k]


def norm_one_kernel(ids, a0, a1, a2, a3, x_ref, w_ref, vec_ref, *refs):
    first_out, n_out, inverse_out, att_out = refs
    lanes = a0.shape[1]

    def head(t):
        for k, ref in enumerate((a0, a1, a2, a3)):
            at = lanes * (t ^ k)
            att_out[:, at : at + lanes] = ref[...]

    by_case(ids[HEAD], 4, head)
    projected = dot3(att_out[...], w_ref[...], 1, 0)
    n, inverse = normed(x_ref[: a0.shape[0]] + (projected + vec_ref[1:2]))
    first_out[...] = n * vec_ref[2:3] + vec_ref[3:4]
    n_out[...] = n
    inverse_out[...] = jnp.broadcast_to(inverse, inverse_out.shape)


def norm_two_kernel(p0, p1, p2, p3, first_ref, cot_ref, vec_ref, rows_out, dz_out, grads_out):
    value = first_ref[...] + ((p0[...] + p1[...]) + (p2[...] + p3[...]) + vec_ref[4:5])
    n, inverse = normed(value)
    rows_out[...] = n * vec_ref[5:6] + vec_ref[6:7]
    up = cot_ref[...]
    dz = norm_back(up, n, inverse, vec_ref[5:6])
    dz_out[...] = dz
    grads_out[...] = jnp.zeros_like(grads_out)
    grads_out[0:1] = colsum(up * n)
    grads_out[1:2] = colsum(up)
    grads_out[2:3] = colsum(dz)


def norm_one_back_kernel(ids, p0, p1, p2, p3, dz_ref, n_ref, inverse_ref, w_ref, vec_ref, *refs):
    dz_out, grads_out = refs[:2]
    parts = refs[2:6]
    up = dz_ref[...] + ((p0[...] + p1[...]) + (p2[...] + p3[...]))
    n = n_ref[...]
    dz = norm_back(up, n, inverse_ref[:, 0:1], vec_ref[2:3])
    dz_out[...] = dz
    grads_out[...] = jnp.zeros_like(grads_out)
    grads_out[0:1] = colsum(up * n)
    grads_out[1:2] = colsum(up)
    grads_out[2:3] = colsum(dz)
    d_att = dot3(dz, w_ref[...], 1, 1)
    lanes = parts[0].shape[1]

    def case(i):
        for k in range(4):
            at = lanes * (i ^ k)
            parts[k][...] = d_att[:, at : at + lanes]

    by_case(ids[HEAD], 4, case)


def stack_rest_kernel(first, source, out):
    out[...] = source[:, first : first + out.shape[1]]


def copy_kernel(source, out):
    out[...] = source[...]


def stack_kernel(*refs):
    for i, ref in enumerate(refs[:-1]):
        refs[-1][i] = ref[...]


def stack_rows(target, refs):
    rows = refs[0].shape[0]
    for k, ref in enumerate(refs):
        target[rows * k : rows * (k + 1), :] = ref[...]


def prepare_kernel(rows_up, slab, up_high, up_low, down_high, down_low):
    for first, count, high, low in (
        (0, rows_up, up_high, up_low),
        (rows_up, slab.shape[1] - rows_up, down_high, down_low),
    ):
        pieces = [slab[w, first : first + count] for w in range(slab.shape[0])]
        high[...], low[...] = split(jnp.concatenate(pieces, axis=0))


def forward_kernel(f0, f1, f2, f3, up_high, up_low, down_high, down_low, vec_ref, *refs):
    pre_out, first_out = refs[:2]
    parts = refs[2:6]
    stack_rows(first_out, (f0, f1, f2, f3))
    pre = dot3s(split(first_out[...]), (up_high[...], up_low[...]), 1, 0) + vec_ref[0:1]
    pre_out[...] = pre
    hidden = 0.5 * pre * (1.0 + lax.erf(pre * (0.5**0.5)))
    branch = dot3s(split(hidden), (down_high[...], down_low[...]), 1, 0)
    rows = f0.shape[0]
    for k in range(4):
        parts[k][...] = branch[rows * k : rows * (k + 1)]


def backward_kernel(z0, z1, z2, z3, pre_ref, up_high, up_low, down_high, down_low, *refs):
    dz_out, d_pre_out = refs[:2]
    parts = refs[2:6]
    stack_rows(dz_out, (z0, z1, z2, z3))
    d_hidden = dot3s(split(dz_out[...]), (down_high[...], down_low[...]), 1, 1)
    pre = pre_ref[...]
    density = jnp.exp(-0.5 * pre * pre) * ((2.0 * jnp.pi) ** -0.5)
    d_pre = d_hidden * (0.5 * (1.0 + lax.erf(pre * (0.5**0.5))) + pre * density)
    d_pre_out[...] = d_pre
    d_first = dot3s(split(d_pre), (up_high[...], up_low[...]), 1, 1)
    rows = z0.shape[0]
    for k in range(4):
        parts[k][...] = d_first[rows * k : rows * (k + 1)]


def ff_weights_kernel(rows_up, rows_down, first_ref, d_pre_ref, pre_ref, dz_ref, out, b_out):
    pre = pre_ref[...]
    hidden = 0.5 * pre * (1.0 + lax.erf(pre * (0.5**0.5)))
    d_pre = d_pre_ref[...]
    b_out[...] = jnp.broadcast_to(colsum(d_pre), b_out.shape)
    up = dot3(first_ref[...], d_pre, 0, 0)
    down = dot3(hidden, dz_ref[...], 0, 0)
    for w in range(out.shape[0]):
        out[w, :rows_up, :] = up[rows_up * w : rows_up * (w + 1)]
        out[w, rows_up:, :] = down[rows_down * w : rows_down * (w + 1)]


def share(ids, outs, places, members, write):
    if len(outs) == 1:
        for place in range(places):
            for z in range(members):
                write(outs[0].at[place, z], place, z)
        return

    def case(core):
        for place in range(places):
            x, f = divmod(place, members)
            j = lax.bitwise_xor(ids[MEMBER], 2 * (f // 2) + x)
            for z in range(members):
                target = outs[core ^ (f % 2)].at[j, lax.bitwise_xor(ids[HEAD], z)]
                write(target, place, z)

    by_case(ids[CORE], 2, case)


def shard_of(place, z, members):
    zh, rest = divmod(place, 2 * members)
    return 2 * (members * zh + z) + rest // members, rest % members


def out_weights_kernel(places, members, ids, att_ref, dz_ref, *outs):
    quarter = outs[0].shape[2]
    a_high, a_low = split(att_ref[...])
    d_high, d_low = split(dz_ref[...])
    value = dot(
        jnp.concatenate([a_high, a_low, a_high], axis=0),
        jnp.concatenate([d_high, d_high, d_low], axis=0),
        0,
        0,
    )

    def write(target, place, z):
        w, f = shard_of(place, z, members)
        at = (w * members + f) * quarter
        target[...] = value[at : at + quarter]

    share(ids, outs, places, members, write)


def sum_cores_kernel(own, came, *outs):
    for j, out in enumerate(outs):
        out[...] = own[j] + came[j]


def qkv_back_kernel(
    rows, span, places, ids, d0, d1, d2, d3, pq_ref, dpq_ref, kv_ref, key_ref, proj_ref, w_ref, *refs
):
    x_ref, dbias_ref, grads_ref, late_ref, up_ref, rows_out = refs[:6]
    outs, turned, up_rows = refs[6:-2], refs[-2], refs[-1]
    heads = pq_ref.shape[0] // 64
    width = heads * 64
    scale = HEAD_DIM**-0.25
    proj = split(proj_ref[...])
    dkv = (d0[...] + d1[...]) + (d2[...] + d3[...])
    for h in range(heads):
        lo, hi = 64 * h, 64 * h + 64
        turned[lo:hi] = scale * dot3s(proj, split(dpq_ref[lo:hi] * pq_ref[lo:hi]), 0, 0)
        pk = dkv[128 * h : 128 * h + 64] * kv_ref[128 * h : 128 * h + 64]
        turned[width + lo : width + hi] = scale * (
            dot3s(proj, split(pk), 0, 0) - key_ref[lo:hi] * colsum(pk)
        )
        turned[2 * width + lo : 2 * width + hi] = dkv[128 * h + 64 : 128 * h + 128]
    d_qkv = turned[...].T
    d_split = split(d_qkv)
    rows_out[...] = dot3s(d_split, split(w_ref[...]), 1, 1)

    members = outs[0].shape[1]
    quarter = rows // members
    d_b = colsum(d_qkv)
    weights = dot3s(split(x_ref[...]), d_split, 0, 0)

    up_rows[...] = jnp.zeros_like(up_rows)
    down = up_ref.shape[1] // up_rows.shape[0]

    def unit(g):
        for w in range(up_rows.shape[0]):
            up_rows[w : w + 1, down * g : down * (g + 1)] = up_ref[0:1, down * w : down * (w + 1)]

    by_case(ids[MEMBER], members, unit)

    def write(target, place, z):
        w, f = shard_of(place, z, members)
        at = (w * members + f) * quarter
        target[:quarter] = weights[at : at + quarter]
        target[quarter:] = jnp.zeros((8, d_b.shape[1]), f32)
        target[quarter : quarter + 1] = d_b
        for i in range(3):
            target[quarter + 1 : quarter + 2, rows * i : rows * (i + 1)] = grads_ref[
                i : i + 1, rows * w : rows * (w + 1)
            ]
            target[quarter + 6 : quarter + 7, rows * i : rows * (i + 1)] = late_ref[
                i : i + 1, rows * w : rows * (w + 1)
            ]
        target[quarter + 2 : quarter + 5, :span] = dbias_ref[0:3, span * w : span * (w + 1)]
        target[quarter + 5 : quarter + 6, : members * down] = up_rows[w : w + 1, : members * down]

    share(ids, outs, places, members, write)


def merge_kernel(rows, skip, ids, r0, r1, r2, r3, w0, w1, w2, w3, out, b_own, bias_out, *rest):
    refs, b_out = (r0, r1, r2, r3), rest[7]
    members = len(refs)
    lanes = r0.shape[1] // 3
    width = lanes * members
    span = bias_out.shape[1]
    quarter = rows // members
    total = (r0[quarter:] + r1[quarter:]) + (r2[quarter:] + r3[quarter:])
    for i in range(3):
        rest[i][...] = total[1:2, rows * i : rows * (i + 1)].reshape(rows)
        rest[3 + i][...] = total[6:7, rows * i : rows * (i + 1)].reshape(rows)
    rest[6][...] = total[5:6, : rest[6].shape[0]].reshape(rest[6].shape)
    last = slice(skip, skip + quarter)
    out[:, 3 * width :] = (w0[last] + w1[last]) + (w2[last] + w3[last])

    def head(t):
        for k, ref in enumerate(refs):
            f = t ^ k
            for p in range(3):
                at = width * p + lanes * f
                out[:, at : at + lanes] = ref[:quarter, lanes * p : lanes * (p + 1)]
                b_out[:, at : at + lanes] = ref[
                    quarter : quarter + 1, lanes * p : lanes * (p + 1)
                ]
            bias_out[3 * f : 3 * f + 3] = ref[quarter + 2 : quarter + 5, :span]

    by_case(ids[HEAD], members, head)
    count = b_own.shape[0]

    def place(w):
        b_own[...] = b_out[:, count * w : count * (w + 1)].reshape(count)

    by_case(ids[WIDE], b_out.shape[1] // count, place)


def place_weights_kernel(ids, r0, r1, r2, r3, w_out, wo_out):
    quarter = r0.shape[0]
    full = w_out.shape[1]

    def own(f):
        for k, ref in enumerate((r0, r1, r2, r3)):
            at = quarter * (f ^ k)
            w_out[at : at + quarter] = ref[:, :full]
            wo_out[at : at + quarter] = ref[:, full:]

    by_case(ids[OWN], 4, own)


def sum_split_kernel(a, b, c, d, *outs):
    for k, out in enumerate(outs):
        out[...] = (a[k] + b[k]) + (c[k] + d[k])


def sum_mixed_kernel(ids, a, b, c, d, rows_ref, *outs):
    rows = rows_ref.shape[0] // len(outs)
    quarter = a.shape[1]
    for k, out in enumerate(outs):
        at = pl.multiple_of(lax.bitwise_xor(ids[HEAD], k) * rows, 8)
        out[:rows] = rows_ref[pl.ds(at, rows), :]
        out[rows : rows + quarter] = (a[k] + b[k]) + (c[k] + d[k])


def sum_kernel(*refs):
    total = refs[0][...]
    for ref in refs[1:-1]:
        total = total + ref[...]
    refs[-1][...] = total


def sum_four_kernel(p0, p1, p2, p3, dz_ref, out):
    rows = out.shape[0]
    out[...] = dz_ref[...] + ((p0[:rows] + p1[:rows]) + (p2[:rows] + p3[:rows]))


def place_kernel(ids, r0, r1, r2, r3, out):
    rows = r0.shape[0]
    for k, ref in enumerate((r0, r1, r2, r3)):
        out[pl.ds(pl.multiple_of(lax.bitwise_xor(ids[OWN], k) * rows, 8), rows), :] = ref[...]


def place_ff_kernel(rows, down, ids, r0, r1, r2, r3, up_out, down_out):
    refs = (r0, r1, r2, r3)
    members = len(refs)

    def own(i):
        for k, ref in enumerate(refs):
            f = i ^ k
            for w in range(up_out.shape[1] // (members * down)):
                at = (w * members + f) * down
                up_out[:, at : at + down] = ref[:rows, down * w : down * (w + 1)]
            down_out[down * f : down * (f + 1)] = ref[rows:]

    by_case(ids[OWN], members, own)


def exchange(value, axes, count, k):
    return lax.ppermute(value, axes, [(i, i ^ k) for i in range(count)])


def swap(value):
    return lax.ppermute(value, ("core", "x"), [(0, 0), (1, 2), (2, 1), (3, 3)])


def place(ids, values, name):
    return call(
        place_kernel,
        [shape(len(values) * values[0].shape[0], values[0].shape[1])],
        [ids, *values],
        name,
        smem=1,
    )[0]


def gather(value, axes, count):
    return [value] + [exchange(value, axes, count, k) for k in range(1, count)]


def relay(value):
    came = exchange(value, "y", 2, 1)
    return [value, exchange(value, "core", 2, 1), came, exchange(came, "core", 2, 1)]


def scatter(parts, axes):
    return [parts[0]] + [exchange(parts[k], axes, len(parts), k) for k in range(1, len(parts))]


def body(
    ys,
    zhs,
    inputs,
    cotangent,
    random_proj,
    position_bias,
    w_qkv,
    b_qkv,
    w_out,
    b_out,
    ln1_gain,
    ln1_bias,
    w_up,
    b_up,
    w_down,
    b_down,
    ln2_gain,
    ln2_bias,
):
    members = 2 * ys
    blocks = 2 * zhs * members
    places = 2 * zhs * members
    few = zhs == 1
    core = lax.axis_index("core")
    x_at, y_at = lax.axis_index("x"), lax.axis_index("y")
    zh_at, zl_at = lax.axis_index("zh"), lax.axis_index("zl")
    feat = 2 * y_at + core
    group = 2 * y_at + x_at
    wide = 2 * (members * zh_at + zl_at) + x_at
    place_at = (2 * zh_at + x_at) * members + feat
    ids = jnp.stack([core, group, feat, zl_at, wide, place_at]).astype(jnp.int32)
    queries, width = inputs.shape
    rows = queries // members
    shard = w_qkv.shape[0]
    quarter = shard // members
    down = w_down.shape[0] // members
    heads = HEADS // members
    lanes = heads * HEAD_DIM
    span = position_bias.shape[1]
    full = 3 * lanes
    length = queries * blocks
    row_shape = shape(rows, width)

    packed = [w_qkv, w_out, position_bias, b_qkv, random_proj.T]
    packed += [b_up, b_out, ln1_gain, ln1_bias, b_down, ln2_gain, ln2_bias]
    got = call(
        functools.partial(pack_qkv_kernel, shard, members),
        [shape(quarter + 8, full)] * members + [shape(rows + -(-quarter // 8) * 8, width), row_shape],
        [ids, inputs, cotangent] + packed,
        "pack_qkv",
        scratch=[
            pltpu.VMEM((quarter, a.shape[1]) if i < 2 and quarter % 8 == 0 else a.shape, f32)
            for i, a in enumerate(packed)
        ]
        + [pltpu.SemaphoreType.DMA((len(packed) + 2,))],
        smem=1,
        limit=60 << 20,
        far=True,
    )
    mixed, cot_rows = got[members:]
    pieces = scatter(got[:members], "zl")
    pack_ids, _ = lax.optimization_barrier((ids, mixed))
    (ff_slab,) = call(
        functools.partial(pack_ff_kernel, members, down),
        [shape(shard + down, width)],
        [pack_ids, w_up, w_down],
        "pack_ff",
        smem=1,
    )
    ff_slab = swap(ff_slab)
    mixed_all = lax.all_gather(mixed, "zl", axis=0)
    pieces, ff_slab = lax.optimization_barrier((pieces, ff_slab))
    (slab,) = call(
        stack_kernel, [shape(members, quarter + 8, full)], pieces, "stack_pieces"
    )
    if few:
        slabs = gather(slab, GROUP, members)
    else:
        slabs = [lax.all_gather(slab, PLANE, axis=0)]
    slabs, mixed_all = lax.optimization_barrier((slabs, mixed_all))
    if few:
        slabs = slabs + [exchange(v, "core", 2, 1) for v in slabs]
    mixed_all, ff_slab = lax.optimization_barrier((mixed_all, ff_slab))
    ff_slab = lax.all_gather(ff_slab, LINES, axis=0)
    spare = 1 if quarter % 8 == 0 else blocks * members
    got = call(
        functools.partial(qkv_kernel, shard, members, (b_qkv.shape[0], span, down), few),
        [
            shape(width, full),
            shape(queries, width),
            shape(lanes, queries),
            shape(2 * lanes, queries),
            shape(lanes, queries),
            shape(FEATURES, HEAD_DIM),
            shape(8, 2 * length),
            shape(8, width),
        ],
        [ids, mixed_all, *slabs],
        "qkv",
        scratch=[
            pltpu.VMEM((blocks, 8, full), f32),
            pltpu.VMEM((spare, quarter, full), f32),
            pltpu.VMEM((FEATURES, 1, HEAD_DIM), f32),
        ],
        smem=1,
        deep=True,
        late=range(2, 2 + len(slabs)) if few else (),
    )
    w_cols, x, pq, kv, keys, proj, bias, vec = got

    if few:
        kv_own = gather(kv, GROUP, members)
        kv_all = kv_own + [exchange(v, "core", 2, 1) for v in kv_own]
        (wo_parts,) = call(
            functools.partial(stack_rest_kernel, rows),
            [shape(members, quarter, width)],
            [mixed_all],
            "stack_out",
        )
        wo_parts, _ = lax.optimization_barrier((wo_parts, kv_all))
        wo_x, wo_y = exchange(wo_parts, "x", 2, 1), exchange(wo_parts, "y", 2, 1)
    else:
        kv_all = lax.all_gather(kv, PLANE, axis=0)
    got = attention(ids, kv_all, pq, bias)
    att, den = got[:2]
    att_parts = scatter(got[2:], "zl")
    if few:
        wo_y, _ = lax.optimization_barrier((wo_y, got))
        wo_own = [wo_parts, wo_x, wo_y, exchange(wo_y, "x", 2, 1)]
        wo_own, _ = lax.optimization_barrier((wo_own, att_parts[2]))
        wo_all = wo_own + [exchange(v, "core", 2, 1) for v in wo_own]
        (w_full,) = call(
            functools.partial(weights_out_kernel, shard),
            [shape(width, width)],
            [ids, *wo_all],
            "weights_out",
            smem=1,
        )
    else:
        w_full = lax.all_gather(w_out, ("zh", "zl", "x"), axis=0, tiled=True)

    first, norm_rows, inverse, att_rows = call(
        norm_one_kernel,
        [row_shape, row_shape, shape(rows, 128), row_shape],
        [ids, *att_parts, mixed, w_full, vec],
        "norm_one",
        smem=1,
    )
    first, ff_slab = lax.optimization_barrier((first, ff_slab))
    firsts = gather(first, GROUP, members)
    full_rows = shape(queries, blocks * down)
    ff_matrices = call(
        functools.partial(prepare_kernel, shard),
        [shape(width, blocks * down, dtype=bf16)] * 2
        + [shape(blocks * down, width, dtype=bf16)] * 2,
        [ff_slab],
        "prepare",
    )
    got = call(
        forward_kernel,
        [full_rows, shape(queries, width)] + [row_shape] * members,
        [*firsts, *ff_matrices, vec],
        "forward",
    )
    pre, first_all = got[:2]
    parts = scatter(got[2:], GROUP)
    out_rows, dz2, grads_two = call(
        norm_two_kernel,
        [row_shape, row_shape, shape(8, width)],
        [*parts, first, cot_rows, vec],
        "norm_two",
    )
    dzs = gather(dz2, GROUP, members)
    got = call(
        backward_kernel,
        [shape(queries, width), full_rows] + [row_shape] * members,
        [*dzs, pre, *ff_matrices],
        "backward",
    )
    dz2_all, d_pre = got[:2]
    parts = scatter(got[2:], GROUP)

    head_rows = shape(rows, lanes)
    got = call(
        norm_one_back_kernel,
        [row_shape, shape(8, width)] + [head_rows] * members,
        [ids, *parts, dz2, norm_rows, inverse, w_full, vec],
        "norm_one_back",
        smem=1,
    )
    dz1, grads_one = got[:2]
    grads = scatter(got[2:], "zl")
    first_all, d_pre, pre, dz2_all, _ = lax.optimization_barrier(
        (first_all, d_pre, pre, dz2_all, dz1)
    )
    ff_grads, up_row = call(
        functools.partial(ff_weights_kernel, shard, down),
        [shape(blocks, shard + down, width), shape(8, blocks * down)],
        [first_all, d_pre, pre, dz2_all],
        "ff_weights",
    )


    part = shape(members, members, quarter, width)
    out_shares = call(
        functools.partial(out_weights_kernel, places, members),
        [part, part] if few else [shape(places, members, quarter, width)],
        [ids, att_rows, dz1],
        "out_weights",
        smem=1,
    )
    def sum_cores(own, other, name):
        came = exchange(other, "core", 2, 1)
        if name == "sum_keys":
            (own,) = call(copy_kernel, [shape(*own.shape)], [own], "load_keys")
        return call(sum_cores_kernel, [shape(*own.shape[1:])] * members, [own, came], name)

    if few:
        out_shares = sum_cores(*out_shares, "sum_out")
        grads, out_shares, ff_grads = lax.optimization_barrier((grads, out_shares, ff_grads))
        out_shares = scatter(out_shares, GROUP)
    else:
        grads, ff_grads = lax.optimization_barrier((grads, ff_grads))
    ff_grads = lax.psum_scatter(ff_grads, LINES, scatter_dimension=0, tiled=False)
    out_came, out_core = exchange(out_rows, "y", 2, 1), exchange(out_rows, "core", 2, 1)
    back = attention_back(ids, kv_all, pq, bias, att, den, grads)
    back, out_came, out_core = lax.optimization_barrier((back, out_came, out_core))
    if few:
        back, out_shares = lax.optimization_barrier((back, out_shares))
        arrived = scatter(sum_cores(back[0], back[1], "sum_keys"), GROUP)
    else:
        arrived = lax.psum_scatter(back[0], PLANE, scatter_dimension=0, tiled=False)
        arrived = [arrived] + [jnp.zeros_like(arrived)] * 3
    dpq, dbias = back[-2:]
    out_parts = [out_rows, out_core, out_came, exchange(out_came, "core", 2, 1)]
    output = place(ids, out_parts, "place_output")
    arrived, output = lax.optimization_barrier((arrived, output))

    part = shape(members, members, quarter + 8, full)
    got = call(
        functools.partial(qkv_back_kernel, shard, span, places),
        [shape(queries, width)]
        + ([part, part] if few else [shape(places, members, quarter + 8, full)]),
        [ids, *arrived, pq, dpq, kv, keys, proj, w_cols, x, dbias, grads_one, grads_two, up_row],
        "qkv_back",
        scratch=[
            pltpu.VMEM((full, queries), f32),
            pltpu.VMEM((blocks, -(-members * down // 128) * 128), f32),
        ],
        smem=1,
    )
    shares_out = got[1:]
    piece = shape(rows + -(-quarter // 8) * 8, width)
    if few:
        mixed_grads = call(
            sum_mixed_kernel, [piece] * members, [ids, *out_shares, got[0]], "sum_mixed", smem=1
        )
    else:
        part = lax.psum_scatter(out_shares[0], PLANE, scatter_dimension=0, tiled=False)
        part = jnp.concatenate(
            [got[0].reshape(members, rows, width), part], axis=1
        )
        part = jnp.pad(part, ((0, 0), (0, piece.shape[0] - part.shape[1]), (0, 0)))
        mixed_grads = [
            lax.dynamic_index_in_dim(part, zl_at ^ k, 0, keepdims=False) for k in range(members)
        ]

    def split_plane(parts, piece, name):
        if few:
            return call(sum_split_kernel, [piece] * members, parts, name)
        part = lax.psum_scatter(parts[0], PLANE, scatter_dimension=0, tiled=False)
        return [
            lax.dynamic_index_in_dim(part, zl_at ^ k, 0, keepdims=False) for k in range(members)
        ]

    if few:
        shares_out = sum_cores(*shares_out, "sum_qkv")
    shares_out, mixed_grads, ff_grads = lax.optimization_barrier(
        (shares_out, mixed_grads, ff_grads)
    )
    ff_grads = swap(ff_grads)
    mine = scatter(shares_out, GROUP) if few else shares_out
    mixed_grads = scatter(mixed_grads, "zl")
    ff_came = exchange(ff_grads, "y", 2, 1)
    mine, mixed_grads, ff_came = lax.optimization_barrier((mine, mixed_grads, ff_came))
    mine = split_plane(mine, shape(quarter + 8, full), "sum_qkv_plane")
    (d_input_rows,) = call(sum_four_kernel, [row_shape], [*mixed_grads, dz1], "sum_rows")
    input_came = exchange(d_input_rows, "y", 2, 1)
    mine = scatter(mine, "zl")
    got = call(
        functools.partial(merge_kernel, shard, rows),
        [
            shape(quarter, 4 * width),
            shape(*b_qkv.shape),
            shape(*position_bias.shape),
        ]
        + [shape(shard)] * 6
        + [shape(*b_up.shape)],
        [ids, *mine, *mixed_grads],
        "merge",
        scratch=[pltpu.VMEM((1, 3 * width), f32)],
        smem=1,
    )
    merged, d_b_qkv, d_position_bias, d_ln1_gain, d_ln1_bias, d_b_out = got[:6]
    d_ln2_gain, d_ln2_bias, d_b_down, d_b_up = got[6:]
    merged_came = exchange(merged, "y", 2, 1)

    def relayed(value, came):
        return [value, exchange(value, "core", 2, 1), came, exchange(came, "core", 2, 1)]

    ff_came, input_came, _ = lax.optimization_barrier((ff_came, input_came, merged))
    d_inputs = place(ids, relayed(d_input_rows, input_came), "place_inputs")
    ff_parts = relayed(ff_grads, ff_came)
    d_w_up, d_w_down = call(
        functools.partial(place_ff_kernel, shard, down),
        [shape(shard, w_up.shape[1]), shape(*w_down.shape)],
        [ids, *ff_parts],
        "place_ff",
        smem=1,
    )
    merged_came, d_inputs, d_w_up, d_w_down = lax.optimization_barrier(
        (merged_came, d_inputs, d_w_up, d_w_down)
    )
    d_w_qkv, d_w_out = call(
        place_weights_kernel,
        [shape(*w_qkv.shape), shape(shard, width)],
        [ids, *relayed(merged, merged_came)],
        "place_weights",
        smem=1,
    )

    return (
        output,
        d_inputs,
        d_position_bias,
        d_w_qkv,
        d_b_qkv,
        d_w_out,
        d_b_out,
        d_ln1_gain,
        d_ln1_bias,
        d_w_up,
        d_b_up,
        d_w_down,
        d_b_down,
        d_ln2_gain,
        d_ln2_bias,
    )


def solution(mesh):
    feats, wides = mesh.shape["feat"], mesh.shape["wide"]
    ys, zhs = feats // 2, wides // (2 * feats)
    fine = Mesh(mesh.devices.reshape(ys, 2, zhs, feats, 2), ("y", "core", "zh", "zl", "x"))
    wide = ("zh", "zl", "x")
    mat, vector, lane = P(wide, None), P(wide), P(None, wide)
    return jax.shard_map(
        functools.partial(body, ys, zhs),
        mesh=fine,
        in_specs=(mat, mat, P(None, FEAT), lane, mat, vector, mat, vector)
        + (vector, vector, mat, vector, mat, vector, vector, vector),
        out_specs=(mat, mat, lane, mat, vector, mat, vector, vector)
        + (vector, mat, vector, mat, vector, vector, vector),
        check_vma=False,
    )
```
